32 devices in a mesh: dp: 4 (over y, x), seq: 4 (over z), heads: 2 (over core).
Axes of the slice: x: 2, y: 2, z: 4, core: 2. Of those that a mesh axis runs over, the one named last changes fastest.
Arguments:
- tokens: bfloat16 [4, 4096, 1024], P('dp', ('seq', 'heads')), may hold values from -6 to 6
- cotangent: bfloat16 [4, 4096, 1024], P('dp', ('seq', 'heads')), may hold values from -6 to 6
- qkvu_weight: bfloat16 [1024, 4, 1024], P(None, None, 'heads'), may hold values from -0.1875 to 0.1875
- out_weight: bfloat16 [1024, 1024], P('heads'), may hold values from -0.1875 to 0.1875
- up_weight: bfloat16 [1024, 2816], replicated, may hold values from -0.1875 to 0.1875
- gate_weight: bfloat16 [1024, 2816], replicated, may hold values from -0.1875 to 0.1875
- down_weight: bfloat16 [2816, 1024], replicated, may hold values from -0.109375 to 0.109375
- decay_rate: float32 [8], P('heads'), may hold values from 4.8828126e-05 to 0.02
- item_length: int32 [4], replicated, may hold values from 1024 to 4096, as said below
- item_slot: int32 [4], replicated, may hold values from 0 to 3, each once
Outputs:
- block_output: bfloat16 [4, 4096, 1024], P('dp', ('seq', 'heads'))
- input_grad: float32 [4, 4096, 1024], P('dp', ('seq', 'heads'))
- qkvu_grad: float32 [1024, 4, 1024], P(None, None, 'heads')
- out_grad: float32 [1024, 1024], P('heads')
- up_grad: float32 [1024, 2816], P(None, 'heads')
- gate_grad: float32 [1024, 2816], P(None, 'heads')
- down_grad: float32 [2816, 1024], P('heads')
The draws below stay inside these ranges and needn't reach their ends.
Inputs may be any that keep to these rules, and one draw needn't show every extreme that they name: `item_length`: an item's valid positions are its first ones; at least one item fills all 4096 positions. `item_slot`: each item stands at exactly one index of dp.
All inputs are finite; a program needn't handle non-finite values.
Results may differ from the reference program's by a relative error of at most 0.012.
Values may be sent and summed in bfloat16 or wider, within the bound.
No kernel may reach another device: no remote copies, remote signals or barrier semaphores. Data moves between devices by JAX's collectives and lax.ppermute only.
A program may use at most 256 MiB of HBM per device.

```python
import math
import jax
import jax.numpy as jnp
from jax import lax

D = 1024
HEADS = 8
FF = 2816
ATT_BLOCK = 512
SEQ_DEV = 1024
LEN = 4096
ITEMS = 4


def draw_item_length(key, part):
    key = jax.random.fold_in(key, 11)
    first_key, second_key = jax.random.split(key)
    drawn = jax.random.randint(first_key, (ITEMS,), SEQ_DEV, LEN + 1)
    longest = jax.random.randint(second_key, (), 0, ITEMS)
    return jnp.where(jnp.arange(ITEMS) == longest, LEN, drawn).astype(jnp.int32)


def levels(stream_key, shape, pieces, smallest, top_value):
    def one(dim, blocks):
        steps = jax.random.uniform(jax.random.fold_in(jax.random.fold_in(stream_key, 6), dim), (blocks,), jnp.float32, smallest / len(pieces), top_value / len(pieces))
        return jnp.repeat(jnp.exp(steps), shape[dim] // blocks).reshape((-1,) + (1,) * (len(shape) - dim - 1))

    factor_of = one(*pieces[0])
    for cut in pieces[1:]:
        factor_of = factor_of * one(*cut)
    return factor_of


def bell_draw(rng, dims, scale, bound, cuts=(), kind=jnp.bfloat16):
    gain = levels(rng, dims, cuts, -0.22, 0.18) if cuts else 1.0
    entries = jax.random.normal(rng, dims, jnp.float32) * scale * gain
    return jnp.minimum(jnp.maximum(entries, -bound), bound).astype(kind)


def setup_inputs(seed: int = 0) -> dict:
    key_list = jax.random.split(jax.random.key(seed), 11)
    tokens = bell_draw(key_list[0], (ITEMS, LEN, D), 1.0, 6.0, ((0, 4), (1, 8)))
    cotangent = bell_draw(key_list[1], (ITEMS, LEN, D), 1.0, 6.0, ((0, 4), (1, 8)))
    qkvu_weight = bell_draw(key_list[2], (D, 4, D), D ** -0.5, 0.1875, ((2, 2),))
    out_weight = bell_draw(key_list[3], (D, D), D ** -0.5, 0.1875, ((0, 2),))
    up_weight = bell_draw(key_list[4], (D, FF), D ** -0.5, 0.1875)
    gate_weight = bell_draw(key_list[5], (D, FF), D ** -0.5, 0.1875)
    down_weight = bell_draw(key_list[6], (FF, D), FF ** -0.5, 0.109375)
    decay_rate = jnp.clip(jnp.exp(math.log(0.02) - 6.015181 * jax.random.uniform(key_list[7], (HEADS,), jnp.float32) ** levels(key_list[7], (HEADS,), ((0, 2),), -0.2, 0.2)), 4.882812572759576e-05, 0.02)
    item_length = draw_item_length(jax.random.fold_in(key_list[10], 71), 0)
    item_slot = jax.random.permutation(key_list[9], ITEMS).astype(jnp.int32)
    return {"tokens": tokens, "cotangent": cotangent, "qkvu_weight": qkvu_weight, "out_weight": out_weight, "up_weight": up_weight, "gate_weight": gate_weight, "down_weight": down_weight, "decay_rate": decay_rate, "item_length": item_length, "item_slot": item_slot}


epsilon = 1e-06
highest = lax.Precision.HIGHEST

@jax.custom_vjp
def low(v):
    return lax.optimization_barrier(v.astype(jnp.bfloat16)).astype(jnp.float32)

@jax.custom_vjp
def low_back(v):
    return v

def low_keep(v):
    return (low(v), None)

def low_pass(kept, grad):
    return (grad,)

def back_keep(v):
    return (v, None)

def back_low(kept, grad):
    return (low(grad),)
low.defvjp(low_keep, low_pass)
low_back.defvjp(back_keep, back_low)

def product(left_side, right_side):
    return jnp.dot(left_side, right_side, precision=highest)

def simple_norm(value):
    return value * lax.rsqrt(lax.optimization_barrier(jnp.mean(value * value, axis=-1, keepdims=True)) + epsilon)

def swish(value):
    return value * jax.nn.sigmoid(value)

def rotation(positions, half_dim):
    frequency = 10000.0 ** (-jnp.arange(half_dim, dtype=jnp.float32) / half_dim)
    angles = positions[:, None] * frequency[None, :]
    return (jnp.cos(angles)[:, None, :], jnp.sin(angles)[:, None, :])

def rotate(value, cosine, sine_part):
    half_dim = value.shape[-1] // 2
    first_half = value[..., :half_dim]
    second_half = value[..., half_dim:]
    return jnp.concatenate([first_half * cosine - second_half * sine_part, first_half * sine_part + second_half * cosine], axis=-1)

def attention_tables(rates, block):
    offsets = jnp.arange(block, dtype=jnp.float32)
    spread = offsets[:, None] - offsets[None, :]
    decay_matrix = jnp.where(spread[None] >= 0.0, jnp.exp(-rates[:, None, None] * jnp.maximum(spread, 0.0)[None]), 0.0)
    entering = jnp.exp(-rates[None, :] * (offsets[:, None] + 1.0))
    leaving = jnp.exp(-rates[None, :] * (block - 1.0 - offsets[:, None]))
    carried = jnp.exp(-rates * block)
    return (decay_matrix, entering, leaving, carried)

def decay_attention(queries, keys, values, rates):
    length, heads, head_dim = queries.shape
    block = ATT_BLOCK
    blocks = length // block
    decay_matrix, entering, leaving, carried = attention_tables(rates, block)

    def step(state, inputs):
        query_part, key_part, value_part = inputs
        scores = jnp.einsum('thd,shd->hts', query_part, key_part, precision=highest)
        weights = low(low_back(scores) * decay_matrix)
        inner = jnp.einsum('hts,shd->thd', weights, value_part, precision=highest)
        outer = entering[:, :, None] * jnp.einsum('thd,hde->the', query_part, low(state), precision=highest)
        scaled_keys = low(key_part * leaving[:, :, None])
        new_state = carried[:, None, None] * state + jnp.einsum('shd,she->hde', scaled_keys, value_part, precision=highest)
        return (new_state, inner + outer)
    start = jnp.zeros((heads, head_dim, head_dim), jnp.float32)
    shaped = (queries.reshape(blocks, block, heads, head_dim), keys.reshape(blocks, block, heads, head_dim), values.reshape(blocks, block, heads, head_dim))
    final_state, outputs = lax.scan(jax.checkpoint(step), start, shaped)
    return outputs.reshape(length, heads, head_dim)

def layer(inputs, qkvu, out_matrix, up_matrix, gate_matrix, down_matrix, rates, valid, positions):
    length, width = inputs.shape
    heads = rates.shape[0]
    head_dim = width // heads
    normed = low(simple_norm(inputs))
    proj = low_back(product(normed, qkvu.reshape(width, 4 * width))).reshape(length, 4, heads, head_dim)
    cosine, sine_part = rotation(positions, head_dim // 2)
    queries = low(low_back(rotate(swish(proj[:, 0]), cosine, sine_part)))
    keys = low(low_back(rotate(swish(proj[:, 1]), cosine, sine_part)))
    values = low(low_back(swish(proj[:, 2])))
    gates = low(proj[:, 3].reshape(length, width))
    attended = decay_attention(queries, keys, values, rates)
    attended = low(low_back(attended)).reshape(length, width)
    mixed = low(simple_norm(attended) * gates)
    hidden = inputs + low_back(product(mixed, out_matrix))
    normed_two = low(simple_norm(hidden))
    left = low_back(product(normed_two, up_matrix))
    right = low_back(product(normed_two, gate_matrix))
    inner = low(left * right)
    result = hidden + low_back(product(inner, down_matrix))
    return result * valid[:, None]

def reference(tokens, cotangent, qkvu_weight, out_weight, up_weight, gate_weight, down_weight, decay_rate, item_length, item_slot):
    length = tokens.shape[1]
    positions = jnp.arange(length, dtype=jnp.float32)
    lengths_here = item_length[item_slot]
    weights = (qkvu_weight.astype(jnp.float32), out_weight.astype(jnp.float32), up_weight.astype(jnp.float32), gate_weight.astype(jnp.float32), down_weight.astype(jnp.float32))

    def per_item(totals, inputs):
        token_block, cotangent_block, item_size = inputs
        valid = (jnp.arange(length, dtype=jnp.int32) < item_size).astype(jnp.float32)

        def forward(inputs_here, qkvu, out_matrix, up_matrix, gate_matrix, down_matrix):
            return layer(inputs_here, qkvu, out_matrix, up_matrix, gate_matrix, down_matrix, decay_rate, valid, positions)
        result, pullback = jax.vjp(forward, token_block.astype(jnp.float32), weights[0], weights[1], weights[2], weights[3], weights[4])
        grads = pullback(cotangent_block.astype(jnp.float32))
        new_totals = (totals[0] + grads[1], totals[1] + grads[2], totals[2] + grads[3], totals[3] + grads[4], totals[4] + grads[5])
        return (new_totals, (result.astype(jnp.bfloat16), grads[0]))
    start = (jnp.zeros_like(weights[0]), jnp.zeros_like(weights[1]), jnp.zeros_like(weights[2]), jnp.zeros_like(weights[3]), jnp.zeros_like(weights[4]))
    totals, (outputs, input_grads) = lax.scan(per_item, start, (tokens, cotangent, lengths_here))
    return (outputs, input_grads, totals[0], totals[1], totals[2], totals[3], totals[4])
```

```python
import functools

import jax
import jax.numpy as jnp
from jax import lax
from jax.experimental import pallas as pl
from jax.experimental.pallas import tpu as pltpu
from jax.sharding import PartitionSpec as P

epsilon = 1e-06
f32 = jnp.float32
bf16 = jnp.bfloat16
CHUNK = 128


def dot(a, b):
    return jnp.dot(a, b, preferred_element_type=f32)


def dot_t(a, b):
    return lax.dot_general(a, b, (((1,), (1,)), ((), ())), preferred_element_type=f32)


def t_dot(a, b):
    return lax.dot_general(a, b, (((0,), (0,)), ((), ())), preferred_element_type=f32)


def whole(value):
    rank = value.ndim
    return pl.BlockSpec(value.shape, lambda i, s: (0,) * rank)


def tiles(value, rows):
    return pl.BlockSpec((rows, value.shape[1]), lambda i, s: (i, 0))


SMEM = pl.BlockSpec(memory_space=pltpu.SMEM)


def call(body, steps, info, ins, outs, scratch=(), after=(), name=None):
    used = len(ins)

    def kernel(info_ref, *refs):
        body(info_ref, *refs[:used], *refs[used + len(after) :])

    return pl.pallas_call(
        kernel,
        grid_spec=pltpu.PrefetchScalarGridSpec(
            num_scalar_prefetch=1,
            grid=(steps,),
            in_specs=[spec for _, spec in ins] + [pl.BlockSpec(memory_space=pl.ANY)] * len(after),
            out_specs=[spec for _, _, spec in outs],
            scratch_shapes=list(scratch),
        ),
        out_shape=[jax.ShapeDtypeStruct(shape, kind) for shape, kind, _ in outs],
        compiler_params=pltpu.CompilerParams(vmem_limit_bytes=52 * 2**20),
        cost_estimate=pl.CostEstimate(flops=0, bytes_accessed=0, transcendentals=0),
        name=name,
    )(info, *[value for value, _ in ins], *after)


def loop(count, step, body):
    def turn(i, _):
        body(pl.ds(pl.multiple_of(i * step, step), step), i * step)
        return 0

    lax.fori_loop(0, count // step, turn, 0)


def head(h, dim):
    return pl.ds(h * dim, dim)


def rotate(value, cosine, sine):
    return value * cosine + pltpu.roll(value, value.shape[1] // 2, 1) * sine


def swish_and_slope(value):
    s = jax.nn.sigmoid(value)
    return value * s, s * (1.0 + value * (1.0 - s))


def row_numbers(start, rows, columns):
    return (lax.broadcasted_iota(jnp.int32, (rows, columns), 0) + start).astype(f32)


def decay_of(rate, start, rows, columns):
    gap = row_numbers(start, rows, columns) - lax.broadcasted_iota(
        jnp.int32, (rows, columns), 1
    ).astype(f32)
    return jnp.where(gap >= 0.0, jnp.exp(-rate * jnp.maximum(gap, 0.0)), 0.0)


def scale_of(total, width):
    return lax.rsqrt(total / width + epsilon)


def row_sum(value):
    return jnp.sum(value, axis=-1, keepdims=True)


def wide(scalar, dim):
    return jnp.full((1, dim), scalar, f32)


def project_kv(block, heads, dim, info, own, other, wk, wv, cs, sn, rate, normed, k, v, sk, sv, contrib, local, pk, pv, kd):
    b = pl.program_id(0)
    mine = b == info[0]
    width = own.shape[1]

    def norm(r, _):
        x = jnp.where(mine, own[r, :].astype(f32), other[r, :].astype(f32))
        normed[r, :] = (x * scale_of(row_sum(x * x), width)).astype(bf16)

    loop(block, 32, norm)
    pk[...] = dot(normed[...], wk[0])
    pv[...] = dot(normed[...], wv[0])

    def act(r, start):
        cosine, sine = cs[r, :], sn[r, :]
        steps = block - 1.0 - row_numbers(start, 64, dim)
        for h in range(heads):
            c = head(h, dim)
            y, slope = swish_and_slope(pk[r, c])
            key = rotate(y, cosine, sine).astype(bf16)
            k[r, c] = key
            sk[r, c] = slope.astype(bf16)
            kd[r, c] = (key.astype(f32) * jnp.exp(-rate[h] * steps)).astype(bf16)
            y, slope = swish_and_slope(pv[r, c])
            v[r, c] = y.astype(bf16)
            sv[r, c] = slope.astype(bf16)

    loop(block, 64, act)
    for h in range(heads):
        c = head(h, dim)
        contrib[b, h] = t_dot(kd[:, c], v[:, c])

    @pl.when(b == 1)
    def _():
        for h in range(heads):
            carried = jnp.exp(wide(-rate[h] * block, dim))
            local[h] = (carried * contrib[0, h] + contrib[1, h]).astype(bf16)


def project_qu(block, heads, dim, info, normed, wq, wu, cs, sn, rate, k, v, q, sq, u, intra, pq):
    pq[...] = dot(normed[...], wq[0])
    u[...] = dot(normed[...], wu[0]).astype(bf16)

    def act(r, start):
        cosine, sine = cs[r, :], sn[r, :]
        for h in range(heads):
            c = head(h, dim)
            y, slope = swish_and_slope(pq[r, c])
            q[r, c] = rotate(y, cosine, sine).astype(bf16)
            sq[r, c] = slope.astype(bf16)

    loop(block, 64, act)
    for h in range(heads):
        c = head(h, dim)
        for start in range(0, block, CHUNK):
            r, upto = pl.ds(start, CHUNK), start + CHUNK
            scores = dot_t(q[r, c], k[:upto, c]) * decay_of(rate[h], start, CHUNK, upto)
            intra[r, c] = dot(scores.astype(bf16), v[:upto, c])


def state_sum(arrived, powers, h, rate, rows, dim):
    total = None
    for part_, power in zip(arrived, powers):
        term = part_[h].astype(f32)
        if power:
            term = term * jnp.exp(wide(-rate[h] * (rows * power), dim))
        total = term if total is None else total + term
    return total


def attend(block, heads, dim, powers, info, q, intra, contrib, rate, *refs):
    arrived, (att, states) = refs[: len(powers)], refs[len(powers) :]
    for h in range(heads):
        c = head(h, dim)
        first = state_sum(arrived, powers, h, rate, 2 * block, dim)
        second = jnp.exp(wide(-rate[h] * block, dim)) * first + contrib[0, h]
        for b, state in enumerate((first, second)):
            states[b, h] = state.astype(bf16)
        for b in range(2):
            state = states[b, h]
            for start in range(0, block, CHUNK):
                r = pl.ds(b * block + start, CHUNK)
                entering = jnp.exp(-rate[h] * (row_numbers(start, CHUNK, dim) + 1.0))
                att[r, c] = (intra[r, c] + entering * dot(q[r, c], state)).astype(bf16)


def begin_back(rows, info, own, other, down, g, grad_inner):
    i = pl.program_id(0)
    mine = (i // 2) == info[0]

    def read(r, start):
        value = jnp.where(mine, own[r, :].astype(f32), other[r, :].astype(f32))
        place = lax.broadcasted_iota(jnp.int32, value.shape, 0) + (start + i * rows)
        g[r, :] = jnp.where(place < info[3], value, 0.0).astype(bf16)

    loop(rows, 32, read)
    grad_inner[...] = dot_t(g[...], down[...]).astype(bf16)


def mix_out(rows, info, att_own, att_other, u_own, u_other, wo_own, wo_other, own, other, hidden, n2, mixed, both):
    mine = (pl.program_id(0) // 2) == info[0]
    half = att_own.shape[1]
    width = 2 * half

    def mix(r, _):
        a, b = att_own[r, :].astype(f32), att_other[r, :].astype(f32)
        scale = scale_of(row_sum(a * a) + row_sum(b * b), width)
        m = (a * scale * u_own[r, :].astype(f32)).astype(bf16)
        mixed[r, :] = m
        both[r, :half] = m
        both[r, half:] = (b * scale * u_other[r, :].astype(f32)).astype(bf16)

    loop(rows, 32, mix)
    hidden[...] = dot(both[:, :half], wo_own[...]) + dot(both[:, half:], wo_other[...])

    def norm(r, _):
        x = jnp.where(mine, own[r, :].astype(f32), other[r, :].astype(f32))
        x = hidden[r, :] + x
        hidden[r, :] = x
        n2[r, :] = (x * scale_of(row_sum(x * x), width)).astype(bf16)

    loop(rows, 32, norm)


def feed(rows, info, n2, up, gate, grad_inner, inner, grad_left, grad_right, left, right):
    left[...] = dot(n2[...], up[...])
    right[...] = dot(n2[...], gate[...])

    def join(r, _):
        a, b, g = left[r, :], right[r, :], grad_inner[r, :].astype(f32)
        inner[r, :] = (a * b).astype(bf16)
        grad_left[r, :] = (g * b).astype(bf16)
        grad_right[r, :] = (g * a).astype(bf16)

    loop(rows, 16, join)


def weight_grad(info, lhs_a, rhs_a, lhs_b, rhs_b, send_a, keep_a, send_b, keep_b):
    step = pl.program_id(0)

    @pl.when(step == 0)
    def _():
        send_a[...] = t_dot(lhs_a[...], rhs_a[...]).astype(bf16)
        send_b[...] = t_dot(lhs_b[...], rhs_b[...]).astype(bf16)

    @pl.when(step == 1)
    def _():
        keep_a[...] = t_dot(lhs_a[...], rhs_a[...]).astype(bf16)
        keep_b[...] = t_dot(lhs_b[...], rhs_b[...]).astype(bf16)


def back_two(info, grad_left, grad_right, up, gate, out):
    out[...] = (dot_t(grad_left[...], up[...]) + dot_t(grad_right[...], gate[...])).astype(bf16)


def split_product(info, inner, down, send, keep):
    result = dot(inner[...], down[...])
    i = pl.program_id(0)

    @pl.when(i < 2)
    def _():
        send[...] = result.astype(bf16)

    @pl.when(i >= 2)
    def _():
        keep[...] = result.astype(bf16)


def back_in(info, du, ga, gb, w, send, keep):
    half = du.shape[1]
    i = pl.program_id(0)
    cut = ga.shape[1] - half
    result = dot_t(ga[:, :half], w[0]) + dot_t(ga[:, half:], w[1, :, :cut])
    result = result + dot_t(gb[:, : half - cut], w[1, :, cut:]) + dot_t(gb[:, half - cut :], w[2])
    result = result + dot_t(du[...], w[3])

    @pl.when(i < 2)
    def _():
        send[...] = result.astype(bf16)

    @pl.when(i >= 2)
    def _():
        keep[...] = result.astype(bf16)


def back_mix(rows, block, heads, dim, info, part_own, part_other, hidden, g, att_own, att_other, u_own, u_other, wo_own, wo_other, q, rate, dh, branch, dgates, datt, direct, local, dm_own, dm_other, es):
    i = pl.program_id(0)
    half = att_own.shape[1]
    width = 2 * half

    def hid(r, _):
        x = hidden[r, :]
        scale = scale_of(row_sum(x * x), width)
        dn = part_own[r, :].astype(f32) + part_other[r, :].astype(f32)
        mean = row_sum(x * dn) / width
        d = g[r, :].astype(f32) + scale * dn - x * (scale * scale * scale * mean)
        dh[r, :] = d
        branch[r, :] = d.astype(bf16)

    loop(rows, 16, hid)
    dm_own[...] = dot_t(branch[...], wo_own[...])
    dm_other[...] = dot_t(branch[...], wo_other[...])

    def att(r, start):
        a, b = att_own[r, :].astype(f32), att_other[r, :].astype(f32)
        scale = scale_of(row_sum(a * a) + row_sum(b * b), width)
        m = dm_own[r, :]
        dgates[r, :] = (m * (a * scale)).astype(bf16)
        da = m * u_own[r, :].astype(f32)
        db = dm_other[r, :] * u_other[r, :].astype(f32)
        mean = (row_sum(a * da) + row_sum(b * db)) / width
        d = (scale * da - a * (scale * scale * scale * mean)).astype(bf16)
        datt[r, :] = d
        place = row_numbers(start + 1, 16, dim) + (lax.rem(i, 2) * rows).astype(f32)
        for h in range(heads):
            c = head(h, dim)
            es[r, c] = (d[:, h * dim : (h + 1) * dim].astype(f32) * jnp.exp(-rate[h] * place)).astype(
                bf16
            )

    loop(rows, 16, att)
    for h in range(heads):
        c = head(h, dim)
        term = t_dot(q[:, c], es[:, c])
        b = i // 2

        @pl.when(lax.rem(i, 2) == 0)
        def _():
            direct[b, h] = term

        @pl.when(lax.rem(i, 2) == 1)
        def _():
            direct[b, h] = direct[b, h] + term

    @pl.when(i == 3)
    def _():
        for h in range(heads):
            carried = jnp.exp(wide(-rate[h] * block, dim))
            local[h] = (direct[0, h] + carried * direct[1, h]).astype(bf16)


def attend_back(block, heads, dim, info, q, k, v, datt, states, sq, cs, sn, rate, gq, dk, dv):
    for h in range(heads):
        c = head(h, dim)
        state = states[0, h]
        for start in reversed(range(0, block, CHUNK)):
            r, upto = pl.ds(start, CHUNK), start + CHUNK
            decay = decay_of(rate[h], start, CHUNK, upto)
            qc, da = q[r, c], datt[r, c]
            weights = (dot_t(qc, k[:upto, c]) * decay).astype(bf16)
            dscore = (dot_t(da, v[:upto, c]) * decay).astype(bf16)
            place = row_numbers(start + 1, CHUNK, dim)
            e = (da.astype(f32) * jnp.exp(-rate[h] * place)).astype(bf16)
            dq = dot(dscore, k[:upto, c]) + dot_t(e, state)
            gq[r, c] = (sq[r, c].astype(f32) * rotate(dq, cs[r, :], -sn[r, :])).astype(bf16)
            dk_term, dv_term = t_dot(dscore, qc), t_dot(weights, da)
            if upto == block:
                dk[:, c] = dk_term
                dv[:, c] = dv_term
            else:
                dk[:upto, c] = dk[:upto, c] + dk_term
                dv[:upto, c] = dv[:upto, c] + dv_term


def finish_back(block, heads, dim, powers, info, k, v, dk, dv, direct, sk, sv, cs, sn, rate, gq, *refs):
    arrived, (out_a, out_b, after) = refs[: len(powers)], refs[len(powers) :]
    b = pl.program_id(0)
    half = heads * dim
    cut = out_a.shape[1] - half

    def put(column, r, value):
        if column < out_a.shape[1]:
            out_a[r, pl.ds(column, dim)] = value
        else:
            out_b[r, pl.ds(column - out_a.shape[1], dim)] = value

    out_a[:, :half] = gq[...]
    for h in range(heads):
        c = head(h, dim)
        last = state_sum(arrived, powers, h, rate, 2 * block, dim)
        before = jnp.exp(wide(-rate[h] * block, dim)) * last + direct[1, h]
        after[...] = jnp.where(b == 1, last, before).astype(bf16)
        for start in range(0, block, CHUNK):
            r = pl.ds(start, CHUNK)
            leaving = jnp.exp(-rate[h] * (block - 1.0 - row_numbers(start, CHUNK, dim)))
            kd = (k[r, c].astype(f32) * leaving).astype(bf16)
            key_grad = dk[r, c] + leaving * dot_t(v[r, c], after[...])
            value_grad = dv[r, c] + dot(kd, after[...])
            gk = sk[r, c].astype(f32) * rotate(key_grad, cs[r, :], -sn[r, :])
            put(half + h * dim, r, gk.astype(bf16))
            put(2 * half + h * dim, r, (sv[r, c].astype(f32) * value_grad).astype(bf16))


def add_quarters(info, keep_a, first_a, second_a, keep_b, first_b, second_b, out):
    cut = keep_a.shape[1]

    def three(x, y, z):
        return (x[...].astype(f32) + y[...].astype(f32) + z[...].astype(f32)).astype(bf16)

    out[:, :cut] = three(keep_a, first_a, second_a)
    out[:, cut:] = three(keep_b, first_b, second_b)


def choose(info, step, pieces, bit_first, bit_second, use):
    first = (step // 2) != bit_first
    second = lax.rem(step, 2) != bit_second
    for index, piece in enumerate(pieces):
        at_first, at_second = index >= 2, index % 2 == 1

        @pl.when((first == at_first) & (second == at_second))
        def _(piece=piece):
            use(piece)


def place_columns(info, *refs):
    out = refs[8]
    step = pl.program_id(0)
    cut = refs[0].shape[1]

    def put_a(piece):
        out[:, :cut] = piece[...].astype(f32)

    def put_b(piece):
        out[:, cut:] = piece[...].astype(f32)

    choose(info, step, refs[:4], info[1], info[2], put_a)
    choose(info, step, refs[4:8], info[2], info[1], put_b)


def place_turned(info, *refs):
    out = refs[8]
    step = pl.program_id(0)
    cut = refs[0].shape[1]

    def put_a(piece):
        out[:cut, :] = piece[...].astype(f32).T

    def put_b(piece):
        out[cut:, :] = piece[...].astype(f32).T

    choose(info, step, refs[:4], info[1], info[2], put_a)
    choose(info, step, refs[4:8], info[2], info[1], put_b)


def place_heads(info, *refs):
    out = refs[12]
    step = pl.program_id(0)
    half = out.shape[2]
    cut = refs[0].shape[1] - half

    def put_a(piece):
        out[:, 0, :] = piece[:, :half].astype(f32)
        out[:, 1, :cut] = piece[:, half:].astype(f32)

    def put_b(piece):
        out[:, 1, cut:] = piece[:, : half - cut].astype(f32)
        out[:, 2, :] = piece[:, half - cut :].astype(f32)

    def put_u(piece):
        out[:, 3, :] = piece[...].astype(f32)

    choose(info, step, refs[:4], info[1], info[2], put_a)
    choose(info, step, refs[4:8], info[2], info[1], put_b)
    choose(info, step, refs[8:12], info[2], info[1], put_u)


def place_rows(info, *refs):
    out = refs[4]

    def put(piece):
        out[...] = piece[...].astype(f32)

    choose(info, pl.program_id(0), refs[:4], info[1], info[2], put)


def swap(value, axis, bit):
    return lax.ppermute(value, axis, [(i, i ^ bit) for i in range(lax.axis_size(axis))])


def shift(value, axis, distance):
    count = lax.axis_size(axis)
    return lax.ppermute(
        value, axis, [(i, i + distance) for i in range(count) if 0 <= i + distance < count]
    )


def part(value, index, rows, axis=0):
    return lax.dynamic_slice_in_dim(value, index * rows, rows, axis)


def add(*terms):
    total = terms[0].astype(f32)
    for term in terms[1:]:
        total = total + term.astype(f32)
    return total.astype(bf16)


def line_states(local, rate, rows, backward):
    count = lax.axis_size("seq")
    sign = -1 if backward else 1
    if count <= 4:
        distances = range(1, count)
        return [shift(local, "seq", sign * d) for d in distances], [d - 1 for d in distances]
    total = shift(local.astype(f32), "seq", sign)
    distance = 1
    while distance < count - 1:
        power = jnp.exp(-rate * rows * distance)[:, None, None]
        total = total + power * shift(total, "seq", sign * distance)
        distance *= 2
    return [total], [0]


class Sum:
    def __init__(self, info, send_a, keep_a, send_b, keep_b):
        self.info, self.keep = info, (keep_a, keep_b)
        self.first = swap(send_a, "dp", 1), swap(send_b, "dp", 2)

    def second(self):
        self.arrived = self.first
        places = 1 - self.info[2], 1 - self.info[1]
        rows = [k.shape[0] // 2 for k in self.keep]
        sent = [
            add(part(k, p, r), part(a, p, r))
            for k, a, p, r in zip(self.keep, self.arrived, places, rows)
        ]
        self.across = swap(sent[0], "dp", 2), swap(sent[1], "dp", 1)
        return sent

    def line(self):
        ins, widths = [], []
        for keep, arrived, across, place in zip(self.keep, self.arrived, self.across, (2, 1)):
            rows, width = across.shape
            spec = pl.BlockSpec((rows, width), lambda i, s, place=place: (s[place], 0))
            ins += [(keep, spec), (arrived, spec), (across, whole(across))]
            widths.append(width)
        self.cut = widths[0]
        shape = rows, sum(widths)
        self.value = call(
            add_quarters,
            1,
            self.info,
            ins,
            [(shape, bf16, pl.BlockSpec(shape, lambda i, s: (0, 0)))],
            name="add_quarters",
        )[0]
        self.four = lax.axis_size("seq") == 4
        if self.four:
            self.inward = lax.ppermute(self.value, "seq", [(0, 1), (3, 2)])
        return self.value

    def line_across(self):
        if self.four:
            self.value = add(self.value, self.inward)
            self.middle = lax.ppermute(self.value, "seq", [(1, 2), (2, 1)])
        return self.value

    def line_back(self):
        if self.four:
            self.total = add(self.value, self.middle)
            self.outer = lax.ppermute(self.total, "seq", [(1, 0), (2, 3)])
        return self.value

    def spread(self):
        if self.four:
            mine = lax.axis_index("seq")
            total = jnp.where((mine == 1) | (mine == 2), self.total, self.outer)
        else:
            total = lax.psum(self.value.astype(f32), "seq").astype(bf16)
        quarters = total[:, : self.cut], total[:, self.cut :]
        self.pieces = []
        for quarter, bit in zip(quarters, (1, 2)):
            second, first = swap(quarter, "dp", 3 ^ bit), swap(quarter, "dp", bit)
            self.pieces.append([quarter, second, first])
        return quarters

    def spread_on(self):
        for pieces, bit in zip(self.pieces, (1, 2)):
            pieces.append(swap(pieces[1], "dp", bit))

    def all_pieces(self):
        return self.pieces[0] + self.pieces[1]


def shards(
    tokens,
    cotangent,
    qkvu_weight,
    out_weight,
    up_weight,
    gate_weight,
    down_weight,
    decay_rate,
    item_length,
    item_slot,
):
    core = lax.axis_index("heads")
    seq_place = lax.axis_index("seq")
    data_place = lax.axis_index("dp")
    block, width = tokens.shape[1:]
    heads = decay_rate.shape[0]
    half = qkvu_weight.shape[2]
    dim = half // heads
    ff = up_weight.shape[1] // 2
    rows = 2 * block
    tile = block // 2
    rate = (decay_rate, SMEM)

    own, own_cot = tokens[0], cotangent[0]
    other = swap(own, "heads", 1)
    other_cot = swap(own_cot, "heads", 1)
    other_out = swap(out_weight, "heads", 1)
    slots = jnp.arange(item_slot.shape[0])
    slot_here = jnp.sum(jnp.where(slots == data_place, item_slot, 0))
    length_here = jnp.sum(jnp.where(slots == slot_here, item_length, 0))
    info = jnp.stack(
        [core, data_place % 2, data_place // 2, length_here - seq_place * rows]
    ).astype(jnp.int32)

    weights = jnp.transpose(qkvu_weight, (1, 0, 2))
    positions = (seq_place * rows + jnp.arange(rows, dtype=jnp.int32)).astype(f32)
    frequency = 10000.0 ** (-jnp.arange(dim // 2, dtype=f32) / (dim // 2))
    angles = positions[:, None] * frequency[None, :]
    cosine, sine = jnp.cos(angles), jnp.sin(angles)
    cs = jnp.concatenate([cosine, cosine], 1)
    sn = jnp.concatenate([-sine, sine], 1)

    def weight(j):
        return weights, pl.BlockSpec((1, width, half), lambda i, s: (j, 0, 0))

    def by(value, size):
        return value, tiles(value, size)

    def all_of(value):
        return value, whole(value)

    def out(columns, kind, size):
        return (rows, columns), kind, pl.BlockSpec((size, columns), lambda i, s: (i, 0))

    def fixed(shape, kind):
        return shape, kind, pl.BlockSpec(shape, lambda i, s: (0,) * len(shape))

    def fn(body, *sizes):
        return functools.partial(body, *sizes)

    square = (heads, dim, dim)
    big, low = pltpu.VMEM((block, half), f32), pltpu.VMEM((block, half), bf16)
    normed, k, v, sk, sv, contrib, local = call(
        fn(project_kv, block, heads, dim),
        2,
        info,
        [all_of(own), all_of(other), weight(1), weight(2), by(cs, block), by(sn, block), rate],
        [out(width, bf16, block)]
        + [out(half, bf16, block)] * 4
        + [fixed((2,) + square, f32), fixed(square, bf16)],
        [big, big, low],
        name="project_kv",
    )
    arrived, powers = line_states(local, decay_rate, rows, False)
    q, sq, u_own, intra = call(
        fn(project_qu, block, heads, dim),
        2,
        info,
        [by(normed, block), weight(0), weight(3), by(cs, block), by(sn, block), rate]
        + [by(k, block), by(v, block)],
        [out(half, bf16, block)] * 3 + [out(half, f32, block)],
        [big],
        after=[local],
        name="project_qu",
    )
    u_other = swap(u_own, "heads", 1)
    halves = pl.BlockSpec((tile, width), lambda i, s: (i % 2, 0))
    g, grad_inner = call(
        fn(begin_back, tile),
        4,
        info,
        [(own_cot, halves), (other_cot, halves)]
        + [(down_weight, pl.BlockSpec((ff, width), lambda i, s: (s[0], 0)))],
        [out(width, bf16, tile), out(ff, bf16, tile)],
        after=[q],
        name="begin_back",
    )
    att_own, states = call(
        fn(attend, block, heads, dim, powers),
        1,
        info,
        [all_of(q), all_of(intra), all_of(contrib), rate] + [all_of(a) for a in arrived],
        [fixed((rows, half), bf16), fixed((2,) + square, bf16)],
        after=[g],
        name="attend",
    )
    att_other = swap(att_own, "heads", 1)
    att_u = [by(att_own, tile), by(att_other, tile), by(u_own, tile), by(u_other, tile)]
    out_both = [all_of(out_weight), all_of(other_out)]
    hidden, n2, mixed = call(
        fn(mix_out, tile),
        4,
        info,
        att_u + out_both + [(own, halves), (other, halves)],
        [out(width, f32, tile), out(width, bf16, tile), out(half, bf16, tile)],
        [pltpu.VMEM((tile, width), bf16)],
        name="mix_out",
    )
    up_spec = pl.BlockSpec((width, ff), lambda i, s: (0, s[0]))
    inner, grad_left, grad_right = call(
        fn(feed, tile),
        4,
        info,
        [by(n2, tile), (up_weight, up_spec), (gate_weight, up_spec), by(grad_inner, tile)],
        [out(ff, bf16, tile)] * 3,
        [pltpu.VMEM((tile, ff), f32)] * 2,
        name="feed",
    )

    def grad(lhs_a, rhs_a, lhs_b, rhs_b, cuts=(None, None), after=(), name=None):
        ins, outs = [], []
        for lhs, rhs, place in ((lhs_a, rhs_a, 1), (lhs_b, rhs_b, 2)):
            size = lhs.shape[1] // 2
            ins += [
                (
                    lhs,
                    pl.BlockSpec(
                        (rows, size),
                        lambda i, s, place=place: (0, jnp.where(i == 0, 1 - s[place], s[place])),
                    ),
                ),
                all_of(rhs),
            ]
            outs += [fixed((size, rhs.shape[1]), bf16)] * 2
        return Sum(
            info, *call(weight_grad, 2, info, ins, outs, after=after, name=name)
        )

    cut = (ff // 128 + 1) // 2 * 128

    def two(value):
        return value[:, :cut], value[:, cut:]

    down_a, down_b = two(inner)
    left_a, left_b = two(grad_left)
    right_a, right_b = two(grad_right)
    down = grad(g, down_a, g, down_b, name="down_grad")
    up = grad(n2, left_a, n2, left_b, after=[down.keep[0]], name="up_grad")
    partial = call(
        back_two,
        4,
        info,
        [by(grad_left, tile), by(grad_right, tile), (up_weight, up_spec), (gate_weight, up_spec)],
        [out(width, bf16, tile)],
        after=[up.keep[0]],
        name="back_two",
    )[0]
    partial_other = swap(partial, "heads", 1)
    gate = grad(n2, right_a, n2, right_b, after=[partial], name="gate_grad")

    turn = pl.BlockSpec(
        (tile, ff), lambda i, s: (jnp.where(i < 2, 2 * (1 - s[0]) + i, 2 * s[0] + i - 2), 0)
    )

    def turned(value):
        return value, pl.BlockSpec(
            (tile, value.shape[1]),
            lambda i, s: (jnp.where(i < 2, 2 * (1 - s[0]) + i, 2 * s[0] + i - 2), 0),
        )

    send_spec = pl.BlockSpec((tile, width), lambda i, s: (jnp.minimum(i, 1), 0))
    keep_spec = pl.BlockSpec((tile, width), lambda i, s: (jnp.maximum(i - 2, 0), 0))
    sides = [((block, width), bf16, send_spec), ((block, width), bf16, keep_spec)]
    send_out, keep_out = call(
        split_product,
        4,
        info,
        [turned(inner), (down_weight, pl.BlockSpec((ff, width), lambda i, s: (s[0], 0)))],
        sides,
        after=[gate.keep[0]],
        name="split_product",
    )
    arrived_out = swap(send_out, "heads", 1)
    dh, branch, dgates, datt, direct, local = call(
        fn(back_mix, tile, block, heads, dim),
        4,
        info,
        [by(partial, tile), by(partial_other, tile), by(hidden, tile), by(g, tile)]
        + att_u
        + out_both
        + [by(q, tile), rate],
        [out(width, f32, tile), out(width, bf16, tile), out(half, bf16, tile), out(half, bf16, tile)]
        + [fixed((2,) + square, f32), fixed(square, bf16)],
        [pltpu.VMEM((tile, half), f32)] * 2 + [pltpu.VMEM((tile, half), bf16)],
        after=[keep_out],
        name="back_mix",
    )
    arrived, powers = line_states(local, decay_rate, rows, True)
    out_u = grad(mixed, branch, normed, dgates, after=[local], name="out_u_grad")
    down_sent = down.second()
    gq, dk, dv = call(
        fn(attend_back, block, heads, dim),
        2,
        info,
        [by(q, block), by(k, block), by(v, block), by(datt, block)]
        + [(states, pl.BlockSpec((1,) + square, lambda i, s: (i, 0, 0, 0))), by(sq, block)]
        + [by(cs, block), by(sn, block), rate],
        [out(half, bf16, block), out(half, f32, block), out(half, f32, block)],
        after=[out_u.keep[0]] + down_sent,
        name="attend_back",
    )
    third = 3 * half // 2
    ga, gb = call(
        fn(finish_back, block, heads, dim, powers),
        2,
        info,
        [by(k, block), by(v, block), by(dk, block), by(dv, block), all_of(direct)]
        + [by(sk, block), by(sv, block), by(cs, block), by(sn, block), rate, by(gq, block)]
        + [all_of(a) for a in arrived],
        [out(third, bf16, block), out(third, bf16, block)],
        [pltpu.VMEM((dim, dim), bf16)],
        name="finish_back",
    )
    qkv = grad(normed, ga, normed, gb, name="qkv_grad")
    up_sent = up.second()
    send_in, keep_in = call(
        back_in,
        4,
        info,
        [turned(dgates), turned(ga), turned(gb), all_of(weights)],
        sides,
        after=[qkv.keep[0]] + up_sent,
        name="back_in",
    )
    arrived_in = swap(send_in, "heads", 1)

    def own_rows(value):
        return part(value, core, block)

    mine = seq_place * rows + core * block + jnp.arange(block, dtype=jnp.int32)
    valid = (mine < length_here).astype(f32)[:, None]
    output = ((own_rows(hidden) + add_wide(keep_out, arrived_out)) * valid).astype(bf16)
    x = own.astype(f32)
    scale = lax.rsqrt(jnp.mean(x * x, axis=-1, keepdims=True) + epsilon)
    dn = add_wide(keep_in, arrived_in)
    grad_inputs = (
        own_rows(dh)
        + scale * dn
        - x * (scale * scale * scale) * jnp.mean(x * dn, axis=-1, keepdims=True)
    )

    gate.second()
    out_u.second()
    qkv.second()
    order = [down, up, gate, out_u, qkv]
    for stage in ("line", "line_across", "line_back", "spread", "spread_on"):
        for sums in order[:3] + order[4:]:
            getattr(sums, stage)()
    finish_apart(out_u)

    def place(body, sums, shape, spec, name):
        pieces = sums if isinstance(sums, list) else sums.all_pieces()
        return call(
            body, 4, info, [all_of(p) for p in pieces], [(shape, f32, spec)], name=name
        )[0]

    flat = pl.BlockSpec((width // 4, ff), lambda i, s: (i, 0))
    return (
        output[None],
        grad_inputs[None],
        place(
            place_heads,
            qkv.all_pieces() + out_u.pieces[1],
            (width, 4, half),
            pl.BlockSpec((width // 4, 4, half), lambda i, s: (i, 0, 0)),
            "place_qkvu",
        ),
        place(
            place_rows,
            out_u.pieces[0],
            (half, width),
            pl.BlockSpec((half // 4, width), lambda i, s: (i, 0)),
            "place_out",
        ),
        place(place_columns, up, (width, ff), flat, "place_up"),
        place(place_columns, gate, (width, ff), flat, "place_gate"),
        place(
            place_turned,
            down,
            (ff, width),
            pl.BlockSpec((ff, width // 4), lambda i, s: (0, i)),
            "place_down",
        ),
    )


def add_wide(a, b):
    return a.astype(f32) + b.astype(f32)


def finish_apart(sums):
    quarters = []
    for keep, arrived, across, place in zip(
        sums.keep, sums.arrived, sums.across, (sums.info[2], sums.info[1])
    ):
        rows = keep.shape[0] // 2
        quarters.append(add(part(keep, place, rows), part(arrived, place, rows), across))
    sums.pieces = []
    for quarter, bit in zip(quarters, (1, 2)):
        total = line_sum(quarter)
        second, first = swap(total, "dp", 3 ^ bit), swap(total, "dp", bit)
        sums.pieces.append([total, second, first, swap(second, "dp", bit)])


def line_sum(value):
    if lax.axis_size("seq") != 4:
        return lax.psum(value.astype(f32), "seq").astype(bf16)
    mine = lax.axis_index("seq")
    value = add(value, lax.ppermute(value, "seq", [(0, 1), (3, 2)]))
    total = add(value, lax.ppermute(value, "seq", [(1, 2), (2, 1)]))
    outer = lax.ppermute(total, "seq", [(1, 0), (2, 3)])
    return jnp.where((mine == 1) | (mine == 2), total, outer)


def solution(mesh):
    placed = (
        P("dp", ("seq", "heads"), None),
        P("dp", ("seq", "heads"), None),
        P(None, None, "heads"),
        P("heads", None),
        P(),
        P(),
        P(),
        P("heads"),
        P(),
        P(),
    )
    return jax.shard_map(
        shards,
        mesh=mesh,
        in_specs=placed,
        out_specs=(
            P("dp", ("seq", "heads"), None),
            P("dp", ("seq", "heads"), None),
            P(None, None, "heads"),
            P("heads", None),
            P(None, "heads"),
            P(None, "heads"),
            P("heads", None),
        ),
        check_vma=False,
    )
```

```python
import functools
import math

import jax
import jax.numpy as jnp
from jax import lax
from jax.experimental import pallas as pl
from jax.experimental.pallas import tpu as pltpu
from jax.sharding import PartitionSpec as P

epsilon = 1e-06
f32 = jnp.float32
bf16 = jnp.bfloat16
CHUNK = 512


def dot(a, b):
    return jnp.dot(a, b, preferred_element_type=f32)


def dot_t(a, b):
    return lax.dot_general(a, b, (((1,), (1,)), ((), ())), preferred_element_type=f32)


def t_dot(a, b):
    return lax.dot_general(a, b, (((0,), (0,)), ((), ())), preferred_element_type=f32)


def whole(value):
    rank = value.ndim
    return pl.BlockSpec(value.shape, lambda i: (0,) * rank, pipeline_mode=pl.Buffered(1))


class View:
    block_shape = None

    def __init__(self, at):
        self.at = at


class Places:
    def __getitem__(self, index):
        core, data = lax.axis_index("heads"), lax.axis_index("dp")
        low, high = lax.rem(data, 2), data // 2
        if index == 0:
            return core
        if index == 1:
            return jnp.where(core == 0, low, high)
        if index == 2:
            return jnp.where(core == 0, high, low)
        return data if index == 3 else lax.axis_index("seq")


def span(index, size):
    return pl.ds(pl.multiple_of(index * size, size), size)


def spec_of(spec):
    return pl.BlockSpec(memory_space=pltpu.VMEM) if isinstance(spec, View) else spec


def room(blocks, scratch, name):
    total = 0
    for spec, kind in blocks:
        if spec.block_shape is not None:
            buffers = 1 if spec.pipeline_mode is not None else 2
            total += buffers * math.prod(spec.block_shape) * jnp.dtype(kind).itemsize
    for buffer in scratch:
        if buffer.dtype in (f32, bf16):
            total += math.prod(buffer.shape) * jnp.dtype(buffer.dtype).itemsize
    return total + SLACK.get(name, 8) * 2**20


SLACK = {"back_two": 12, "back_mix": 14, "project_qu": 30}


def tiles(value, rows):
    return pl.BlockSpec((rows, value.shape[1]), lambda i: (i, 0))


SMEM = pl.BlockSpec(memory_space=pltpu.SMEM)


class Spine:
    def __init__(self):
        self.token = None
        self.done = []

    def call(self, body, steps, ins, outs, scratch=(), name=None):
        after = self.done + ([] if self.token is None else [self.token])
        used, given = len(ins), len(outs)
        specs = [spec for _, spec in ins] + [spec for _, _, spec in outs]
        blocks = [(spec, value.dtype) for value, spec in ins]
        blocks += [(spec, kind) for _, kind, spec in outs]

        def kernel(*refs):
            rest = refs[used + len(after) :]
            rest[given][...] = jnp.zeros((8, 128), f32)
            step, places = pl.program_id(0), Places()
            given_refs = [
                spec.at(ref, step, places) if isinstance(spec, View) else ref
                for spec, ref in zip(specs, list(refs[:used]) + list(rest[:given]))
            ]
            body(places, *given_refs, *rest[given + 1 :])

        results = pl.pallas_call(
            kernel,
            grid=(steps,),
            in_specs=[spec_of(spec) for _, spec in ins]
            + [pl.BlockSpec(memory_space=pl.ANY)] * len(after),
            out_specs=[spec_of(spec) for _, _, spec in outs]
            + [pl.BlockSpec(memory_space=pltpu.VMEM)],
            scratch_shapes=list(scratch),
            out_shape=[jax.ShapeDtypeStruct(shape, kind) for shape, kind, _ in outs]
            + [jax.ShapeDtypeStruct((8, 128), f32)],
            compiler_params=pltpu.CompilerParams(vmem_limit_bytes=room(blocks, scratch, name)),
            cost_estimate=pl.CostEstimate(flops=0, bytes_accessed=0, transcendentals=0),
            name=name,
        )(*[value for value, _ in ins], *after)
        self.token, self.done = results[-1], []
        return results[:-1]

    def after(self, *values):
        self.done += values

    def wait(self, *values):
        if self.done:
            token = self.token
            for value in self.done:
                token = token + value[:8, :128].astype(f32)
            self.token, self.done = token, []
        results = lax.optimization_barrier((self.token,) + values)
        self.token = results[0]
        return results[1:]


def loop(count, step, body, unroll=True):
    def turn(i, _):
        body(pl.ds(pl.multiple_of(i * step, step), step), i * step)
        return 0

    lax.fori_loop(0, count // step, turn, 0, unroll=unroll)


def head(h, dim):
    return pl.ds(h * dim, dim)


def rotate(value, cosine, sine):
    return value * cosine + pltpu.roll(value, value.shape[1] // 2, 1) * sine


def sigmoid(value):
    return 0.5 * jnp.tanh(0.5 * value) + 0.5


def swish(value):
    return value * sigmoid(value)


def swish_slope(value):
    s = sigmoid(value)
    y = value * s
    return y + s * (1.0 - y)


def row_numbers(start, rows, columns):
    return (lax.broadcasted_iota(jnp.int32, (rows, columns), 0) + start).astype(f32)


def fall_of(rate):
    return jnp.exp(-rate * row_numbers(0, CHUNK, CHUNK))


def decay_of(rate, start, fall):
    upto = start + CHUNK
    columns = lax.broadcasted_iota(jnp.int32, (1, upto), 1).astype(f32)
    rise = jnp.exp(rate * (columns - float(start)))
    tiles = [rise[:, j : j + CHUNK] * fall for j in range(0, upto, CHUNK)]
    rows = lax.broadcasted_iota(jnp.int32, (CHUNK, CHUNK), 0)
    inside = rows >= lax.broadcasted_iota(jnp.int32, (CHUNK, CHUNK), 1)
    tiles[-1] = jnp.where(inside, tiles[-1], 0.0)
    return jnp.concatenate(tiles, 1) if start else tiles[0]


def scale_of(total, width):
    return lax.rsqrt(total / width + epsilon)


def row_sum(value):
    return jnp.sum(value, axis=-1, keepdims=True)


def wide(scalar, dim):
    return jnp.full((1, dim), scalar, f32)


def copy_begin(copies):
    @pl.when(pl.program_id(0) == 0)
    def _():
        for source, target, sem in copies:
            pltpu.make_async_copy(source, target, sem).start()


def copy_end(copies):
    @pl.when(pl.program_id(0) == 1)
    def _():
        for source, target, sem in copies:
            pltpu.make_async_copy(source, target, sem).wait()


def project_kv(block, heads, dim, info, own, other, wk, wv, cs, sn, rate, down, normed, turned, k, v, pk, pv, contrib, local, down_half, sk, sv, kd, sem):
    b = pl.program_id(0)
    mine = b == info[0]
    width = own.shape[1]
    rows = down_half.shape[0]
    copies = [(down.at[span(info[0], rows), :], down_half, sem.at[0])]
    copy_begin(copies)

    def norm(r, _):
        x = jnp.where(mine, own[r, :].astype(f32), other[r, :].astype(f32))
        normed[r, :] = (x * scale_of(row_sum(x * x), width)).astype(bf16)

    loop(block, 16, norm)
    sk[...] = dot(normed[...], wk[0])
    sv[...] = dot(normed[...], wv[0])
    turned[...] = normed[...].T

    def act(r, start):
        cosine, sine = cs[r, :], sn[r, :]
        steps = block - 1.0 - row_numbers(start, 64, dim)
        for h in range(heads):
            c = head(h, dim)
            p = sk[r, c]
            pk[r, c] = p.astype(bf16)
            key = rotate(swish(p), cosine, sine).astype(bf16)
            k[r, c] = key
            kd[r, c] = (key.astype(f32) * jnp.exp(-rate[h] * steps)).astype(bf16)
            p = sv[r, c]
            pv[r, c] = p.astype(bf16)
            v[r, c] = swish(p).astype(bf16)

    loop(block, 64, act)
    for h in range(heads):
        c = head(h, dim)
        contrib[b, h] = t_dot(kd[:, c], v[:, c])

    @pl.when(b == 1)
    def _():
        for h in range(heads):
            carried = jnp.exp(wide(-rate[h] * block, dim))
            local[h] = (carried * contrib[0, h] + contrib[1, h]).astype(bf16)

    copy_end(copies)


def project_qu(block, heads, dim, info, normed, wq, wu, cs, sn, rate, k, v, up, gate, q, pq, u, intra, up_half, gate_half, sq, sem):
    columns = up_half.shape[1]
    copies = [
        (weight.at[:, span(info[0], columns)], half, sem.at[n])
        for n, (weight, half) in enumerate(((up, up_half), (gate, gate_half)))
    ]
    copy_begin(copies)
    sq[...] = dot(normed[...], wq[0])
    u[...] = dot(normed[...], wu[0]).astype(bf16)

    def act(r, start):
        cosine, sine = cs[r, :], sn[r, :]
        for h in range(heads):
            c = head(h, dim)
            p = sq[r, c]
            pq[r, c] = p.astype(bf16)
            q[r, c] = rotate(swish(p), cosine, sine).astype(bf16)

    loop(block, 64, act)
    for h in range(heads):
        c = head(h, dim)
        fall = fall_of(rate[h])
        for start in range(0, block, CHUNK):
            r, upto = pl.ds(start, CHUNK), start + CHUNK
            scores = dot_t(q[r, c], k[:upto, c]) * decay_of(rate[h], start, fall)
            intra[r, c] = dot(scores.astype(bf16), v[:upto, c])
    copy_end(copies)


def state_sum(arrived, count, h, rate, rows, dim, place, backward):
    if count != 4:
        return arrived[h]
    total = None
    for i in range(1, 4):
        distance = place - (place ^ i)
        distance = -distance if backward else distance
        steps = jnp.full((1, dim), rows * jnp.maximum(distance - 1, 0), jnp.int32).astype(f32)
        factor = jnp.where(jnp.full((1, dim), distance) > 0, jnp.exp(-rate[h] * steps), 0.0)
        term = factor * arrived[i, h].astype(f32)
        total = term if total is None else total + term
    return total


def attend(block, heads, dim, count, info, q, intra, contrib, rate, arrived, att, states):
    for h in range(heads):
        c = head(h, dim)
        first = state_sum(arrived, count, h, rate, 2 * block, dim, info[4], False)
        second = jnp.exp(wide(-rate[h] * block, dim)) * first + contrib[0, h]
        for b, state in enumerate((first, second)):
            states[b, h] = state.astype(bf16)
        for b in range(2):
            state = states[b, h]
            for start in range(0, block, CHUNK):
                r = pl.ds(b * block + start, CHUNK)
                entering = jnp.exp(-rate[h] * (row_numbers(start, CHUNK, dim) + 1.0))
                att[r, c] = (intra[r, c] + entering * dot(q[r, c], state)).astype(bf16)


def begin_back(rows, info, own, other, down, item_slot, item_length, g, turned, grad_inner, valid):
    i = pl.program_id(0)
    mine = i == info[0]
    limit = item_length[item_slot[info[3]]] - (2 * info[4] + i) * rows

    def read(r, start):
        value = jnp.where(mine, own[r, :].astype(f32), other[r, :].astype(f32))
        inside = lax.broadcasted_iota(jnp.int32, value.shape, 0) + start < limit
        g[r, :] = jnp.where(inside, value, 0.0).astype(bf16)

    loop(rows, 16, read)
    valid[...] = (lax.broadcasted_iota(jnp.int32, valid.shape, 0) < limit).astype(f32)
    grad_inner[...] = dot_t(g[...], down[...]).astype(bf16)
    turned[...] = g[...].T


def mix_out(rows, info, att_own, att_other, u_own, u_other, wo_own, wo_other, own, other, hidden, n2, turned, mixed, both):
    mine = pl.program_id(0) == info[0]
    half = att_own.shape[1]
    width = 2 * half

    def mix(r, _):
        a, b = att_own[r, :].astype(f32), att_other[r, :].astype(f32)
        scale = scale_of(row_sum(a * a) + row_sum(b * b), width)
        both[r, :half] = (a * scale * u_own[r, :].astype(f32)).astype(bf16)
        both[r, half:] = (b * scale * u_other[r, :].astype(f32)).astype(bf16)

    loop(rows, 16, mix)
    hidden[...] = dot(both[:, :half], wo_own[...]) + dot(both[:, half:], wo_other[...])
    mixed[...] = both[:, :half].T

    def norm(r, _):
        x = jnp.where(mine, own[r, :].astype(f32), other[r, :].astype(f32))
        x = hidden[r, :] + x
        hidden[r, :] = x
        n2[r, :] = (x * scale_of(row_sum(x * x), width)).astype(bf16)

    loop(rows, 16, norm)
    turned[...] = n2[...].T


def feed(rows, info, n2, up, gate, grad_inner, inner, grad_left, grad_right, left, right):
    left[...] = dot(n2[...], up[...])
    right[...] = dot(n2[...], gate[...])

    def join(r, _):
        a, b, g = left[r, :], right[r, :], grad_inner[r, :].astype(f32)
        inner[r, :] = (a * b).astype(bf16)
        grad_left[r, :] = (g * b).astype(bf16)
        grad_right[r, :] = (g * a).astype(bf16)

    loop(rows, 16, join)


def weight_half(info, lhs, rhs, out):
    out[...] = dot(lhs[...], rhs[...]).astype(bf16)


def weight_grad(info, lhs, rhs, send, keep):
    step = pl.program_id(0)

    @pl.when(step == 0)
    def _():
        send[...] = dot(lhs[...], rhs[...]).astype(bf16)

    @pl.when(step == 1)
    def _():
        keep[...] = dot(lhs[...], rhs[...]).astype(bf16)


def out_u_grad(info, mixed, branch, normed, dgates, send, keep):
    step = pl.program_id(0)
    half = dgates.shape[1]
    rows = mixed.shape[0] // 2

    def both(out):
        out[:, :half] = dot(normed[...], dgates[...]).astype(bf16)
        for quarter in range(2):
            for side in range(2):
                result = dot(mixed[pl.ds(quarter * rows, rows), :], branch[:, pl.ds(side * half, half)])
                out[pl.ds((2 * quarter + side) * rows, rows), half:] = result.astype(bf16)

    @pl.when(step == 0)
    def _():
        both(send)

    @pl.when(step == 1)
    def _():
        both(keep)


def back_two(info, grad_left, grad_right, up, gate, first, second):
    result = (dot_t(grad_left[...], up[...]) + dot_t(grad_right[...], gate[...])).astype(bf16)
    i = pl.program_id(0)

    @pl.when(i == 0)
    def _():
        first[...] = result

    @pl.when(i == 1)
    def _():
        second[...] = result


def split_product(info, inner, down, hidden, send, keep):
    result = dot(inner[...], down[...])
    i = pl.program_id(0)

    @pl.when(i == 0)
    def _():
        send[...] = result.astype(bf16)

    @pl.when(i == 1)
    def _():
        keep[...] = result + hidden[...]


def back_in(info, du, grads, w, send, keep):
    half = du.shape[1]
    i = pl.program_id(0)
    result = dot_t(du[...], w[3])
    for j in range(3):
        result = result + dot_t(grads[:, pl.ds(j * half, half)], w[j])
    result = result.astype(bf16)

    @pl.when(i == 0)
    def _():
        send[...] = result

    @pl.when(i == 1)
    def _():
        keep[...] = result


def back_mix(rows, block, heads, dim, info, own_0, own_1, other_0, other_1, hidden, g, att_own, att_other, u_own, u_other, wo_own, wo_other, q, rate, dh, branch, dgates, datt, direct, local, dm_own, dm_other, es):
    i = pl.program_id(0)
    b = jnp.where(i == 0, 1 - info[0], info[0])
    half = att_own.shape[1]
    width = 2 * half

    def hid(r, _):
        x = hidden[r, :]
        scale = scale_of(row_sum(x * x), width)
        dn = jnp.where(
            b == 0,
            own_0[r, :].astype(f32) + other_0[r, :].astype(f32),
            own_1[r, :].astype(f32) + other_1[r, :].astype(f32),
        )
        mean = row_sum(x * dn) / width
        d = g[r, :].astype(f32) + scale * dn - x * (scale * scale * scale * mean)
        dh[r, :] = d
        branch[r, :] = d.astype(bf16)

    loop(rows, 16, hid)
    dm_own[...] = dot_t(branch[...], wo_own[...])
    dm_other[...] = dot_t(branch[...], wo_other[...])

    def att(r, start):
        a, b = att_own[r, :].astype(f32), att_other[r, :].astype(f32)
        scale = scale_of(row_sum(a * a) + row_sum(b * b), width)
        m = dm_own[r, :]
        dgates[r, :] = (m * (a * scale)).astype(bf16)
        da = m * u_own[r, :].astype(f32)
        db = dm_other[r, :] * u_other[r, :].astype(f32)
        mean = (row_sum(a * da) + row_sum(b * db)) / width
        d = (scale * da - a * (scale * scale * scale * mean)).astype(bf16)
        datt[r, :] = d
        place = row_numbers(start + 1, 16, dim)
        for h in range(heads):
            dd = d[:, h * dim : (h + 1) * dim].astype(f32)
            es[r, head(h, dim)] = (dd * jnp.exp(-rate[h] * place)).astype(bf16)

    loop(rows, 16, att)
    for h in range(heads):
        c = head(h, dim)
        direct[b, h] = t_dot(q[:, c], es[:, c])

    @pl.when(i == 1)
    def _():
        for h in range(heads):
            carried = jnp.exp(wide(-rate[h] * block, dim))
            local[h] = (direct[0, h] + carried * direct[1, h]).astype(bf16)


def attend_back(block, heads, dim, info, q, k, v, datt, states, pq, cs, sn, rate, gq, dk, dv):
    for h in range(heads):
        c = head(h, dim)
        state = states[0, h]
        fall = fall_of(rate[h])
        for start in reversed(range(0, block, CHUNK)):
            r, upto = pl.ds(start, CHUNK), start + CHUNK
            decay = decay_of(rate[h], start, fall)
            qc, da = q[r, c], datt[r, c]
            weights = (dot_t(qc, k[:upto, c]) * decay).astype(bf16)
            dscore = (dot_t(da, v[:upto, c]) * decay).astype(bf16)
            entering = jnp.exp(-rate[h] * (row_numbers(start, CHUNK, dim) + 1.0))
            e = (da.astype(f32) * entering).astype(bf16)
            dq = dot(dscore, k[:upto, c]) + dot_t(e, state)
            slope = swish_slope(pq[r, c].astype(f32))
            gq[r, c] = (slope * rotate(dq, cs[r, :], -sn[r, :])).astype(bf16)
            dk_term, dv_term = t_dot(dscore, qc), t_dot(weights, da)
            if upto == block:
                dk[:, c] = dk_term
                dv[:, c] = dv_term
            else:
                dk[:upto, c] = dk[:upto, c] + dk_term
                dv[:upto, c] = dv[:upto, c] + dv_term


def finish_back(block, heads, dim, count, info, k, v, dk, dv, direct, pk, pv, cs, sn, rate, gq, arrived, out, after):
    b = pl.program_id(0)
    half = heads * dim
    out[:, :half] = gq[...]
    for h in range(heads):
        c = head(h, dim)
        last = state_sum(arrived, count, h, rate, 2 * block, dim, info[4], True)
        before = jnp.exp(wide(-rate[h] * block, dim)) * last + direct[1, h]
        after[...] = jnp.where(b == 1, last, before).astype(bf16)
        for start in range(0, block, CHUNK):
            r = pl.ds(start, CHUNK)
            leaving = jnp.exp(-rate[h] * (block - 1.0 - row_numbers(start, CHUNK, dim)))
            kd = (k[r, c].astype(f32) * leaving).astype(bf16)
            key_grad = dk[r, c] + leaving * dot_t(v[r, c], after[...])
            value_grad = dv[r, c] + dot(kd, after[...])
            gk = swish_slope(pk[r, c].astype(f32)) * rotate(key_grad, cs[r, :], -sn[r, :])
            out[r, pl.ds(half + h * dim, dim)] = gk.astype(bf16)
            out[r, pl.ds(2 * half + h * dim, dim)] = (
                swish_slope(pv[r, c].astype(f32)) * value_grad
            ).astype(bf16)


def add_kernel(info, *refs):
    *terms, out = refs

    def body(r, _):
        total = terms[0][r, :].astype(f32)
        for term in terms[1:]:
            total = total + term[r, :].astype(f32)
        out[r, :] = total.astype(bf16)

    loop(out.shape[0], 16, body)


def choose_kernel(info, mine, arrived, out):
    place = info[4]
    inner = (place == 1) | (place == 2)

    def body(r, _):
        value = jnp.where(inner, mine[r, :].astype(f32), arrived[r, :].astype(f32))
        out[r, :] = value.astype(bf16)

    loop(out.shape[0], 16, body)


def merge_kernel(info, mine, arrived, out):
    rows = mine.shape[0]
    for piece, place in ((mine, info[2]), (arrived, 1 - info[2])):
        def body(r, start, piece=piece, place=place):
            out[pl.ds(pl.multiple_of(place * rows + start, 16), 16), :] = piece[r, :]

        loop(rows, 16, body)


def choose(info, mine, arrived, use):
    step = pl.program_id(0)
    rows = mine.shape[0] // 2
    here = pl.ds(pl.multiple_of(lax.rem(step, 2) * rows, rows), rows)

    @pl.when(step // 2 == info[1])
    def _():
        use(mine, here)

    @pl.when(step // 2 != info[1])
    def _():
        use(arrived, here)


def place_whole(info, mine, arrived, out):
    def put(half, here):
        out[...] = half[here, :].astype(f32)

    choose(info, mine, arrived, put)


def place_turned(info, mine, arrived, out):
    def put(half, here):
        out[...] = half[here, :].astype(f32).T

    choose(info, mine, arrived, put)


def place_heads(info, mine, arrived, mine_u, arrived_u, out):
    width = out.shape[2]

    def put_qkv(half, here):
        for j in range(3):
            out[:, j, :] = half[here, pl.ds(j * width, width)].astype(f32)

    def put_gates(half, here):
        out[:, 3, :] = half[here, :width].astype(f32)

    choose(info, mine, arrived, put_qkv)
    choose(info, mine_u, arrived_u, put_gates)


def place_rows(info, mine, arrived, out):
    rows, width = out.shape[0], out.shape[1] // 2

    def put(half, here):
        piece = half[here, width:].astype(f32)
        out[:, :width] = piece[:rows, :]
        out[:, width:] = piece[rows:, :]

    choose(info, mine, arrived, put)


def swap(value, axis, bit):
    return lax.ppermute(value, axis, [(i, i ^ bit) for i in range(lax.axis_size(axis))])


def shift(value, axis, distance):
    count = lax.axis_size(axis)
    return lax.ppermute(
        value, axis, [(i, i + distance) for i in range(count) if 0 <= i + distance < count]
    )


def cross(value, turn):
    pairs = []
    for place in range(lax.axis_size("dp")):
        for core in range(2):
            pairs.append((2 * place + core, 2 * (place ^ (1 << (core ^ turn))) + core))
    return lax.ppermute(value, ("dp", "heads"), pairs)


def part(value, index, rows, axis=0):
    return lax.dynamic_slice_in_dim(value, index * rows, rows, axis)


def add(*terms):
    total = terms[0].astype(f32)
    for term in terms[1:]:
        total = total + term.astype(f32)
    return total.astype(bf16)


class States:
    def __init__(self, spine, local, rate, rows, backward):
        self.spine, self.rate, self.rows, self.backward = spine, rate, rows, backward
        self.count = lax.axis_size("seq")
        if self.count == 4:
            self.near = local, swap(local, "seq", 1)
        else:
            self.local = local

    def second(self):
        if self.count == 4:
            local, near = self.near
            (near,) = self.spine.wait(near)
            self.two = jnp.stack([local, near])
            self.far = swap(self.two, "seq", 2)

    def all(self):
        if self.count == 4:
            (far,) = self.spine.wait(self.far)
            return jnp.concatenate([self.two, far])
        sign = -1 if self.backward else 1
        total = shift(self.local.astype(f32), "seq", sign)
        distance = 1
        while distance < self.count - 1:
            power = jnp.exp(-self.rate * self.rows * distance)[:, None, None]
            total = total + power * shift(total, "seq", sign * distance)
            distance *= 2
        return total


class Sum:
    def __init__(self, spine, send, keep=None):
        self.spine, self.keep = spine, keep
        self.first = cross(send, 0)
        self.shape = send.shape[0] // 2, send.shape[1]
        self.four = lax.axis_size("seq") == 4

    def combine(self, body, *terms):
        rows = self.shape[0]

        def view(turn):
            if turn is None:
                return View(lambda ref, i, s: ref)
            return View(lambda ref, i, s: ref.at[span(1 - s[2] if turn else s[2], rows), :])

        ins = [(value, view(turn)) for value, turn in terms]
        outs = [(self.shape, bf16, view(None))]
        return self.spine.call(body, 1, ins, outs, name="combine")[0]

    def second(self):
        (self.first,) = self.spine.wait(self.first)
        self.across = cross(self.combine(add_kernel, (self.keep, True), (self.first, True)), 1)

    def line(self):
        (across,) = self.spine.wait(self.across)
        self.value = self.combine(
            add_kernel, (self.keep, False), (self.first, False), (across, None)
        )
        if self.four:
            self.inward = lax.ppermute(self.value, "seq", [(0, 1), (3, 2)])

    def line_across(self):
        if self.four:
            (inward,) = self.spine.wait(self.inward)
            self.value = self.combine(add_kernel, (self.value, None), (inward, None))
            self.middle = lax.ppermute(self.value, "seq", [(1, 2), (2, 1)])

    def line_back(self):
        if self.four:
            (middle,) = self.spine.wait(self.middle)
            self.value = self.combine(add_kernel, (self.value, None), (middle, None))
            self.outer = lax.ppermute(self.value, "seq", [(1, 0), (2, 3)])

    def spread(self):
        if self.four:
            (outer,) = self.spine.wait(self.outer)
            total = self.combine(choose_kernel, (self.value, None), (outer, None))
        else:
            total = lax.psum(self.value.astype(f32), "seq").astype(bf16)
            self.spine.after(total)
        self.value, self.second_half = total, cross(total, 1)

    def spread_on(self):
        (second,) = self.spine.wait(self.second_half)
        rows, columns = self.shape
        shape = 2 * rows, columns
        here = View(lambda ref, i, s: ref)
        ins, outs = [(self.value, here), (second, here)], [(shape, bf16, here)]
        self.value = self.spine.call(merge_kernel, 1, ins, outs, name="combine")[0]
        self.first_half = cross(self.value, 0)

    def arrive(self):
        (first,) = self.spine.wait(self.first_half)
        return [self.value, first]


def shards(
    tokens,
    cotangent,
    qkvu_weight,
    out_weight,
    up_weight,
    gate_weight,
    down_weight,
    decay_rate,
    item_length,
    item_slot,
):
    core = lax.axis_index("heads")
    seq_place = lax.axis_index("seq")
    data_place = lax.axis_index("dp")
    block, width = tokens.shape[1:]
    heads = decay_rate.shape[0]
    half = qkvu_weight.shape[2]
    dim = half // heads
    ff = up_weight.shape[1] // 2
    rows = 2 * block
    tile = block // 2
    rate = (decay_rate, SMEM)

    own, own_cot = tokens[0], cotangent[0]
    other = swap(own, "heads", 1)
    other_cot = swap(own_cot, "heads", 1)
    other_out = swap(out_weight, "heads", 1)
    weights = jnp.transpose(qkvu_weight, (1, 0, 2))
    fine = 32
    lanes = jnp.arange(dim)
    frequency = 10000.0 ** (-(lanes % (dim // 2)).astype(f32) / (dim // 2))
    coarse_steps = seq_place * rows + fine * jnp.arange(rows // fine)
    steps = jnp.concatenate([coarse_steps, jnp.arange(fine)]).astype(f32)
    angles = steps[:, None] * frequency[None, :]
    cosine, sine = lax.optimization_barrier((jnp.cos(angles), jnp.sin(angles)))
    c_far, s_far = cosine[:-fine, None, :], sine[:-fine, None, :]
    c_near, s_near = cosine[None, -fine:, :], sine[None, -fine:, :]
    sign = jnp.where(lanes < dim // 2, -1.0, 1.0)
    cs = (c_far * c_near - s_far * s_near).reshape(rows, dim)
    sn = (sign * (s_far * c_near + c_far * s_near)).reshape(rows, dim)

    def weight(j):
        return weights, View(lambda ref, i, s: ref.at[pl.ds(j, 1)])

    def by(value, size):
        return value, View(lambda ref, i, s: ref.at[span(i, size), :])

    def all_of(value):
        return value, View(lambda ref, i, s: ref)

    def out(columns, kind, size):
        return (rows, columns), kind, View(lambda ref, i, s: ref.at[span(i, size), :])

    def fixed(shape, kind):
        return shape, kind, View(lambda ref, i, s: ref)

    def fn(body, *sizes):
        return functools.partial(body, *sizes)

    spine = Spine()
    call = spine.call
    square = (heads, dim, dim)
    big, low = pltpu.VMEM((block, half), f32), pltpu.VMEM((block, half), bf16)

    def turned(columns):
        return (columns, rows), bf16, View(lambda ref, i, s: ref.at[:, span(i, block)])

    anywhere = pl.BlockSpec(memory_space=pltpu.HBM)
    normed, normed_t, k, v, pk, pv, contrib, local, down_half = call(
        fn(project_kv, block, heads, dim),
        2,
        [all_of(own), all_of(other), weight(1), weight(2), by(cs, block), by(sn, block)]
        + [rate, (down_weight, anywhere)],
        [out(width, bf16, block), turned(width)]
        + [out(half, bf16, block)] * 4
        + [fixed((2,) + square, f32), fixed(square, bf16), fixed((ff, width), bf16)],
        [big, big, low, pltpu.SemaphoreType.DMA((1,))],
        name="project_kv",
    )
    line = States(spine, local, decay_rate, rows, False)
    g, g_t, grad_inner, valid = call(
        fn(begin_back, block),
        2,
        [all_of(own_cot), all_of(other_cot), all_of(down_half)]
        + [(item_slot, SMEM), (item_length, SMEM)],
        [out(width, bf16, block), turned(width), out(ff, bf16, block), out(dim, f32, block)],
        name="begin_back",
    )
    line.second()
    q, pq, u_own, intra, up_half, gate_half = call(
        fn(project_qu, block, heads, dim),
        2,
        [by(normed, block), weight(0), weight(3), by(cs, block), by(sn, block), rate]
        + [by(k, block), by(v, block), (up_weight, anywhere), (gate_weight, anywhere)],
        [out(half, bf16, block)] * 3
        + [out(half, f32, block)]
        + [fixed((width, ff), bf16)] * 2,
        [big, pltpu.SemaphoreType.DMA((2,))],
        name="project_qu",
    )
    u_other = swap(u_own, "heads", 1)
    arrived = line.all()
    att_own, states = call(
        fn(attend, block, heads, dim, line.count),
        1,
        [all_of(q), all_of(intra), all_of(contrib), rate, all_of(arrived)],
        [fixed((rows, half), bf16), fixed((2,) + square, bf16)],
        name="attend",
    )
    att_other = swap(att_own, "heads", 1)
    att_u = [by(att_own, block), by(att_other, block), by(u_own, block), by(u_other, block)]
    out_both = [all_of(out_weight), all_of(other_out)]
    hidden, n2, n2_t, mixed_t = call(
        fn(mix_out, block),
        2,
        att_u + out_both + [all_of(own), all_of(other)],
        [out(width, f32, block), out(width, bf16, block), turned(width), turned(half)],
        [pltpu.VMEM((block, width), bf16)],
        name="mix_out",
    )
    inner, grad_left, grad_right = call(
        fn(feed, block),
        2,
        [by(n2, block), all_of(up_half), all_of(gate_half), by(grad_inner, block)],
        [out(ff, bf16, block)] * 3,
        [pltpu.VMEM((block, ff), f32)] * 2,
        name="feed",
    )

    def halves(value):
        size = value.shape[0] // 2

        def at(ref, i, s):
            return ref.at[span(jnp.where(i == 0, 1 - s[1], s[1]), size), :]

        return value, View(at)

    def grad(name, lhs, rhs):
        shape = lhs.shape[0] // 2, rhs.shape[1]
        return call(
            weight_grad, 2, [halves(lhs), all_of(rhs)], [fixed(shape, bf16)] * 2, name=name
        )

    def sides(value):
        def at(ref, i, s):
            return ref.at[span(jnp.where(i == 0, 1 - s[0], s[0]), block), :]

        return value, View(at)

    two_sides = [fixed((block, width), bf16)] * 2

    def half_grad(name, lhs, rhs, send):
        size = lhs.shape[0] // 2

        def at(ref, i, s):
            return ref.at[span(1 - s[1] if send else s[1], size), :]

        shape = size, rhs.shape[1]
        ins = [(lhs, View(at)), all_of(rhs)]
        return call(weight_half, 1, ins, [fixed(shape, bf16)], name=name)[0]

    down = Sum(spine, half_grad("down_send", g_t, inner, True))
    partial = call(
        back_two,
        2,
        [by(grad_left, block), by(grad_right, block), all_of(up_half), all_of(gate_half)],
        two_sides,
        name="back_two",
    )
    partial_other = [swap(value, "heads", 1) for value in partial]
    up = Sum(spine, *grad("up_grad", n2_t, grad_left))
    gate = Sum(spine, *grad("gate_grad", n2_t, grad_right))
    down.keep = half_grad("down_keep", g_t, inner, False)
    partial_other = spine.wait(*partial_other)
    down.second()
    dh, branch, dgates, datt, direct, local = call(
        fn(back_mix, block, block, heads, dim),
        2,
        [all_of(x) for x in (*partial, *partial_other)]
        + [sides(x) for x in (hidden, g, att_own, att_other, u_own, u_other)]
        + out_both
        + [sides(q), rate],
        [fixed((block, width), f32)]
        + [((rows, size), bf16, sides(None)[1]) for size in (width, half, half)]
        + [fixed((2,) + square, f32), fixed(square, bf16)],
        [pltpu.VMEM((block, half), f32)] * 2 + [pltpu.VMEM((block, half), bf16)],
        name="back_mix",
    )
    line = States(spine, local, decay_rate, rows, True)
    out_u = Sum(
        spine,
        *call(
            out_u_grad,
            2,
            [halves(mixed_t), all_of(branch), halves(normed_t), all_of(dgates)],
            [fixed((block, width), bf16)] * 2,
            name="out_u_grad",
        ),
    )
    line.second()
    gq, dk, dv = call(
        fn(attend_back, block, heads, dim),
        2,
        [by(q, block), by(k, block), by(v, block), by(datt, block)]
        + [(states, View(lambda ref, i, s: ref.at[pl.ds(i, 1)])), by(pq, block)]
        + [by(cs, block), by(sn, block), rate],
        [out(half, bf16, block), out(half, f32, block), out(half, f32, block)],
        name="attend_back",
    )
    down.line()
    up.second()
    arrived = line.all()
    grads = call(
        fn(finish_back, block, heads, dim, line.count),
        2,
        [by(k, block), by(v, block), by(dk, block), by(dv, block), all_of(direct)]
        + [by(pk, block), by(pv, block), by(cs, block), by(sn, block), rate]
        + [by(gq, block), all_of(arrived)],
        [out(3 * half, bf16, block)],
        [pltpu.VMEM((dim, dim), bf16)],
        name="finish_back",
    )[0]
    qkv = Sum(spine, *grad("qkv_grad", normed_t, grads))
    gate.second()
    send_in, keep_in = call(
        back_in,
        2,
        [sides(dgates), sides(grads), all_of(weights)],
        two_sides,
        name="back_in",
    )
    down.line_across()
    up.line()
    send_out, keep_out = call(
        split_product,
        2,
        [sides(inner), all_of(down_half), sides(hidden)],
        [fixed((block, width), bf16), fixed((block, width), f32)],
        name="split_product",
    )
    gate.line()
    out_u.second()
    down.line_back()
    up.line_across()
    out_u.line()
    gate.line_across()

    qkv.second()
    down.spread()
    up.line_back()
    qkv.line()
    out_u.line_across()
    gate.line_back()
    send_in, send_out = spine.wait(send_in, send_out)
    arrived_in, arrived_out = swap(send_in, "heads", 1), swap(send_out, "heads", 1)
    down.spread_on()
    up.spread()
    qkv.line_across()
    out_u.line_back()
    gate.spread()
    up.spread_on()
    arrived_in, arrived_out = spine.wait(arrived_in, arrived_out)
    def own_rows(value):
        return part(value, core, block)

    def add_wide(a, b):
        return a.astype(f32) + b.astype(f32)

    output = add_wide(keep_out, arrived_out)
    output = (output * own_rows(valid)[:, :1]).astype(bf16)
    x = own.astype(f32)
    scale = lax.rsqrt(jnp.mean(x * x, axis=-1, keepdims=True) + epsilon)
    dn = add_wide(keep_in, arrived_in)
    grad_inputs = (
        dh
        + scale * dn
        - x * (scale * scale * scale) * jnp.mean(x * dn, axis=-1, keepdims=True)
    )
    spine.after(output, grad_inputs)
    flat = pl.BlockSpec((width // 4, ff), lambda i: (i, 0))

    def place(body, pieces, shape, spec, name):
        return call(
            body, 4, [(p, whole(p)) for p in pieces], [(shape, f32, spec)], name=name
        )[0]

    down_grad = place(
        place_turned,
        down.arrive(),
        (ff, width),
        pl.BlockSpec((ff, width // 4), lambda i: (0, i)),
        "place_down",
    )
    qkv.line_back()
    out_u.spread()
    gate.spread_on()
    up_grad = place(place_whole, up.arrive(), (width, ff), flat, "place_up")
    qkv.spread()
    out_u.spread_on()
    gate_grad = place(place_whole, gate.arrive(), (width, ff), flat, "place_gate")
    qkv.spread_on()
    out_u_pieces = out_u.arrive()
    out_grad = place(
        place_rows,
        out_u_pieces,
        (half, width),
        pl.BlockSpec((half // 4, width), lambda i: (i, 0)),
        "place_out",
    )
    qkvu_grad = place(
        place_heads,
        qkv.arrive() + out_u_pieces,
        (width, 4, half),
        pl.BlockSpec((width // 4, 4, half), lambda i: (i, 0, 0)),
        "place_qkvu",
    )
    return output[None], grad_inputs[None], qkvu_grad, out_grad, up_grad, gate_grad, down_grad


def solution(mesh):
    placed = (
        P("dp", ("seq", "heads"), None),
        P("dp", ("seq", "heads"), None),
        P(None, None, "heads"),
        P("heads", None),
        P(),
        P(),
        P(),
        P("heads"),
        P(),
        P(),
    )
    return jax.shard_map(
        shards,
        mesh=mesh,
        in_specs=placed,
        out_specs=(
            P("dp", ("seq", "heads"), None),
            P("dp", ("seq", "heads"), None),
            P(None, None, "heads"),
            P("heads", None),
            P(None, "heads"),
            P(None, "heads"),
            P("heads", None),
        ),
        check_vma=False,
    )
```

```python
import functools
import math

import jax
import jax.numpy as jnp
from jax import lax
from jax.experimental import pallas as pl
from jax.experimental.pallas import tpu as pltpu
from jax.sharding import PartitionSpec as P

epsilon = 1e-06
f32 = jnp.float32
bf16 = jnp.bfloat16
CHUNK = 512


def dot(a, b):
    return jnp.dot(a, b, preferred_element_type=f32)


def dot_t(a, b):
    return lax.dot_general(a, b, (((1,), (1,)), ((), ())), preferred_element_type=f32)


def t_dot(a, b):
    return lax.dot_general(a, b, (((0,), (0,)), ((), ())), preferred_element_type=f32)


def whole(value):
    rank = value.ndim
    return pl.BlockSpec(value.shape, lambda i: (0,) * rank, pipeline_mode=pl.Buffered(1))


class View:
    block_shape = None

    def __init__(self, at):
        self.at = at


class Places:
    def __getitem__(self, index):
        core, data = lax.axis_index("heads"), lax.axis_index("dp")
        low, high = lax.rem(data, 2), data // 2
        if index == 0:
            return core
        if index == 1:
            return jnp.where(core == 0, low, high)
        if index == 2:
            return jnp.where(core == 0, high, low)
        return data if index == 3 else lax.axis_index("seq")


def span(index, size):
    return pl.ds(pl.multiple_of(index * size, size), size)


def spec_of(spec):
    return pl.BlockSpec(memory_space=pltpu.VMEM) if isinstance(spec, View) else spec


def room(blocks, scratch, name):
    total = 0
    for spec, kind in blocks:
        if spec.block_shape is not None:
            buffers = 1 if spec.pipeline_mode is not None else 2
            total += buffers * math.prod(spec.block_shape) * jnp.dtype(kind).itemsize
    for buffer in scratch:
        if buffer.dtype in (f32, bf16):
            total += math.prod(buffer.shape) * jnp.dtype(buffer.dtype).itemsize
    return total + SLACK.get(name, 4) * 2**20


SLACK = {"begin_back": 5, "attend_back": 5, "split_product": 6, "back_two": 8}


def tiles(value, rows):
    return pl.BlockSpec((rows, value.shape[1]), lambda i: (i, 0))


SMEM = pl.BlockSpec(memory_space=pltpu.SMEM)


class Spine:
    def __init__(self):
        self.token = None
        self.done = []

    def call(self, body, steps, ins, outs, scratch=(), name=None):
        after = self.done + ([] if self.token is None else [self.token])
        used, given = len(ins), len(outs)
        specs = [spec for _, spec in ins] + [spec for _, _, spec in outs]
        blocks = [(spec, value.dtype) for value, spec in ins]
        blocks += [(spec, kind) for _, kind, spec in outs]

        def kernel(*refs):
            rest = refs[used + len(after) :]
            rest[given][...] = jnp.zeros((8, 128), f32)
            step, places = pl.program_id(0), Places()
            given_refs = [
                spec.at(ref, step, places) if isinstance(spec, View) else ref
                for spec, ref in zip(specs, list(refs[:used]) + list(rest[:given]))
            ]
            body(places, *given_refs, *rest[given + 1 :])

        results = pl.pallas_call(
            kernel,
            grid=(steps,),
            in_specs=[spec_of(spec) for _, spec in ins]
            + [pl.BlockSpec(memory_space=pl.ANY)] * len(after),
            out_specs=[spec_of(spec) for _, _, spec in outs]
            + [pl.BlockSpec(memory_space=pltpu.VMEM)],
            scratch_shapes=list(scratch),
            out_shape=[jax.ShapeDtypeStruct(shape, kind) for shape, kind, _ in outs]
            + [jax.ShapeDtypeStruct((8, 128), f32)],
            compiler_params=pltpu.CompilerParams(vmem_limit_bytes=room(blocks, scratch, name)),
            cost_estimate=pl.CostEstimate(flops=0, bytes_accessed=0, transcendentals=0),
            name=name,
        )(*[value for value, _ in ins], *after)
        self.token, self.done = results[-1], []
        return results[:-1]

    def after(self, *values):
        self.done += values

    def wait(self, *values):
        if self.done:
            token = self.token
            for value in self.done:
                token = token + value[:8, :128].astype(f32)
            self.token, self.done = token, []
        results = lax.optimization_barrier((self.token,) + values)
        self.token = results[0]
        return results[1:]


def loop(count, step, body, unroll=True):
    def turn(i, _):
        body(pl.ds(pl.multiple_of(i * step, step), step), i * step)
        return 0

    lax.fori_loop(0, count // step, turn, 0, unroll=unroll)


def head(h, dim):
    return pl.ds(h * dim, dim)


def rotate(value, cosine, sine):
    return value * cosine + pltpu.roll(value, value.shape[1] // 2, 1) * sine


def sigmoid(value):
    return 0.5 * jnp.tanh(0.5 * value) + 0.5


def swish(value):
    return value * sigmoid(value)


def swish_slope(value):
    s = sigmoid(value)
    y = value * s
    return y + s * (1.0 - y)


def row_numbers(start, rows, columns):
    return (lax.broadcasted_iota(jnp.int32, (rows, columns), 0) + start).astype(f32)


def fall_of(rate):
    return jnp.exp(-rate * row_numbers(0, CHUNK, CHUNK))


def decay_of(rate, start, fall):
    upto = start + CHUNK
    columns = lax.broadcasted_iota(jnp.int32, (1, upto), 1).astype(f32)
    rise = jnp.exp(rate * (columns - float(start)))
    tiles = [rise[:, j : j + CHUNK] * fall for j in range(0, upto, CHUNK)]
    rows = lax.broadcasted_iota(jnp.int32, (CHUNK, CHUNK), 0)
    inside = rows >= lax.broadcasted_iota(jnp.int32, (CHUNK, CHUNK), 1)
    tiles[-1] = jnp.where(inside, tiles[-1], 0.0)
    return jnp.concatenate(tiles, 1) if start else tiles[0]


def scale_of(total, width):
    return lax.rsqrt(total / width + epsilon)


def row_sum(value):
    return jnp.sum(value, axis=-1, keepdims=True)


def wide(scalar, dim):
    return jnp.full((1, dim), scalar, f32)


def project_kv(block, heads, dim, info, own, other, wk, wv, cs, sn, rate, normed, turned, k, v, pk, pv, contrib, local, sk, sv, kd):
    b = pl.program_id(0)
    mine = b == info[0]
    width = own.shape[1]

    def norm(r, _):
        x = jnp.where(mine, own[r, :].astype(f32), other[r, :].astype(f32))
        normed[r, :] = (x * scale_of(row_sum(x * x), width)).astype(bf16)

    loop(block, 16, norm)
    sk[...] = dot(normed[...], wk[0])
    sv[...] = dot(normed[...], wv[0])
    turned[...] = normed[...].T

    def act(r, start):
        cosine, sine = cs[r, :], sn[r, :]
        steps = block - 1.0 - row_numbers(start, 64, dim)
        for h in range(heads):
            c = head(h, dim)
            p = sk[r, c]
            pk[r, c] = p.astype(bf16)
            key = rotate(swish(p), cosine, sine).astype(bf16)
            k[r, c] = key
            kd[r, c] = (key.astype(f32) * jnp.exp(-rate[h] * steps)).astype(bf16)
            p = sv[r, c]
            pv[r, c] = p.astype(bf16)
            v[r, c] = swish(p).astype(bf16)

    loop(block, 64, act)
    for h in range(heads):
        c = head(h, dim)
        contrib[b, h] = t_dot(kd[:, c], v[:, c])

    @pl.when(b == 1)
    def _():
        for h in range(heads):
            carried = jnp.exp(wide(-rate[h] * block, dim))
            local[h] = (carried * contrib[0, h] + contrib[1, h]).astype(bf16)


def project_qu(block, heads, dim, info, normed, wq, wu, cs, sn, rate, k, v, q, pq, u, intra, sq):
    sq[...] = dot(normed[...], wq[0])
    u[...] = dot(normed[...], wu[0]).astype(bf16)

    def act(r, start):
        cosine, sine = cs[r, :], sn[r, :]
        for h in range(heads):
            c = head(h, dim)
            p = sq[r, c]
            pq[r, c] = p.astype(bf16)
            q[r, c] = rotate(swish(p), cosine, sine).astype(bf16)

    loop(block, 64, act)
    for h in range(heads):
        c = head(h, dim)
        fall = fall_of(rate[h])
        for start in range(0, block, CHUNK):
            r, upto = pl.ds(start, CHUNK), start + CHUNK
            scores = dot_t(q[r, c], k[:upto, c]) * decay_of(rate[h], start, fall)
            intra[r, c] = dot(scores.astype(bf16), v[:upto, c])


def pair_states(info, count, heads, dim, rows, backward, own, near, rate, out):
    even = lax.rem(info[4], 2) == 0
    for h in range(heads):
        decay = jnp.exp(wide(-rate[h] * rows, dim))
        a, b = own[h].astype(f32), near[h].astype(f32)
        plain, decayed = (a, b) if backward else (b, a)
        other = (b, a) if backward else (a, b)
        out[h] = jnp.where(even, plain + decay * decayed, other[0] + decay * other[1]).astype(bf16)


def state_sum(near, far, count, h, rate, rows, dim, place, backward):
    if count != 4:
        return near[h]
    side = lax.rem(place, 2) == (0 if backward else 1)
    pair = place < 2 if backward else place >= 2
    decay = jnp.where(side, jnp.exp(wide(-rate[h] * rows, dim)), 1.0)
    first = jnp.where(side, near[h].astype(f32), 0.0)
    return first + jnp.where(pair, decay * far[h].astype(f32), 0.0)


def attend(block, heads, dim, count, info, q, intra, contrib, rate, near, far, att, states):
    for h in range(heads):
        c = head(h, dim)
        first = state_sum(near, far, count, h, rate, 2 * block, dim, info[4], False)
        second = jnp.exp(wide(-rate[h] * block, dim)) * first + contrib[0, h]
        for b, state in enumerate((first, second)):
            states[b, h] = state.astype(bf16)
        for b in range(2):
            state = states[b, h]
            for start in range(0, block, CHUNK):
                r = pl.ds(b * block + start, CHUNK)
                entering = jnp.exp(-rate[h] * (row_numbers(start, CHUNK, dim) + 1.0))
                att[r, c] = (intra[r, c] + entering * dot(q[r, c], state)).astype(bf16)


def begin_back(rows, info, own, other, down, item_slot, item_length, g, turned, grad_inner, valid):
    i = pl.program_id(0)
    mine = i == info[0]
    limit = item_length[item_slot[info[3]]] - (2 * info[4] + i) * rows

    def read(r, start):
        value = jnp.where(mine, own[r, :].astype(f32), other[r, :].astype(f32))
        inside = lax.broadcasted_iota(jnp.int32, value.shape, 0) + start < limit
        g[r, :] = jnp.where(inside, value, 0.0).astype(bf16)

    loop(rows, 16, read)
    valid[...] = (lax.broadcasted_iota(jnp.int32, valid.shape, 0) < limit).astype(f32)
    grad_inner[...] = dot_t(g[...], down[...]).astype(bf16)
    turned[...] = g[...].T


def mix_out(rows, info, att_own, att_other, u_own, u_other, wo_own, wo_other, own, other, hidden, n2, turned, mixed, both):
    mine = pl.program_id(0) == info[0]
    half = att_own.shape[1]
    width = 2 * half

    def mix(r, _):
        a, b = att_own[r, :].astype(f32), att_other[r, :].astype(f32)
        scale = scale_of(row_sum(a * a) + row_sum(b * b), width)
        both[r, :half] = (a * scale * u_own[r, :].astype(f32)).astype(bf16)
        both[r, half:] = (b * scale * u_other[r, :].astype(f32)).astype(bf16)

    loop(rows, 16, mix)
    hidden[...] = dot(both[:, :half], wo_own[...]) + dot(both[:, half:], wo_other[...])
    mixed[...] = both[:, :half].T

    def norm(r, _):
        x = jnp.where(mine, own[r, :].astype(f32), other[r, :].astype(f32))
        x = hidden[r, :] + x
        hidden[r, :] = x
        n2[r, :] = (x * scale_of(row_sum(x * x), width)).astype(bf16)

    loop(rows, 16, norm)
    turned[...] = n2[...].T


def feed(rows, info, n2, up, gate, grad_inner, inner, grad_left, grad_right, left, right):
    left[...] = dot(n2[...], up[...])
    right[...] = dot(n2[...], gate[...])

    def join(r, _):
        a, b, g = left[r, :], right[r, :], grad_inner[r, :].astype(f32)
        inner[r, :] = (a * b).astype(bf16)
        grad_left[r, :] = (g * b).astype(bf16)
        grad_right[r, :] = (g * a).astype(bf16)

    loop(rows, 16, join)


def weight_half(info, lhs, rhs, out):
    out[...] = dot(lhs[...], rhs[...]).astype(bf16)


def weight_grad(info, lhs, rhs, send, keep):
    step = pl.program_id(0)

    @pl.when(step == 0)
    def _():
        send[...] = dot(lhs[...], rhs[...]).astype(bf16)

    @pl.when(step == 1)
    def _():
        keep[...] = dot(lhs[...], rhs[...]).astype(bf16)


def weight_grad_cut(info, lhs, rhs, on, there, keep, last_send, last_keep):
    step = pl.program_id(0)
    columns, rows = keep.shape[1], on.shape[0]

    @pl.when(step == 0)
    def _():
        for out, place in ((on, 1 - info[2]), (there, info[2])):
            out[...] = dot(lhs[span(place, rows), :], rhs[:, :columns]).astype(bf16)
        last_send[...] = dot(lhs[...], rhs[:, columns:]).astype(bf16)

    @pl.when(step == 1)
    def _():
        keep[...] = dot(lhs[...], rhs[:, :columns]).astype(bf16)
        last_keep[...] = dot(lhs[...], rhs[:, columns:]).astype(bf16)


def out_u_grad(info, mixed, branch, normed, dgates, send, keep):
    step = pl.program_id(0)
    half = dgates.shape[1]
    rows = mixed.shape[0] // 2

    def both(out):
        out[:, :half] = dot(normed[...], dgates[...]).astype(bf16)
        for side in range(2):
            result = dot(mixed[...], branch[:, pl.ds(side * half, half)]).astype(bf16)
            for quarter in range(2):
                piece = result[quarter * rows : (quarter + 1) * rows, :]
                out[pl.ds((2 * quarter + side) * rows, rows), half:] = piece

    @pl.when(step == 0)
    def _():
        both(send)

    @pl.when(step == 1)
    def _():
        both(keep)


def back_two(info, grad_left, grad_right, up, gate, first, second):
    result = (dot_t(grad_left[...], up[...]) + dot_t(grad_right[...], gate[...])).astype(bf16)
    i = pl.program_id(0)

    @pl.when(i == 0)
    def _():
        first[...] = result

    @pl.when(i == 1)
    def _():
        second[...] = result


def split_product(info, inner, down, hidden, send_in, sends, keep):
    result = dot(inner[...], down[...])
    i = pl.program_id(0)

    @pl.when(i == 0)
    def _():
        sends[0] = send_in[...]
        sends[1] = result.astype(bf16)

    @pl.when(i == 1)
    def _():
        keep[...] = result + hidden[...]


def back_in(info, du, grads, w, send, keep):
    half = du.shape[1]
    i = pl.program_id(0)
    result = dot_t(du[...], w[3])
    for j in range(3):
        result = result + dot_t(grads[:, pl.ds(j * half, half)], w[j])
    result = result.astype(bf16)

    @pl.when(i == 0)
    def _():
        send[...] = result

    @pl.when(i == 1)
    def _():
        keep[...] = result


def back_mix(rows, block, heads, dim, info, own_0, own_1, other_0, other_1, hidden, g, att_own, att_other, u_own, u_other, wo_own, wo_other, q, rate, dh, branch, dgates, datt, direct, local, dm_own, dm_other, es):
    i = pl.program_id(0)
    b = jnp.where(i == 0, 1 - info[0], info[0])
    half = att_own.shape[1]
    width = 2 * half

    def hid(r, _):
        x = hidden[r, :]
        scale = scale_of(row_sum(x * x), width)
        dn = jnp.where(
            b == 0,
            own_0[r, :].astype(f32) + other_0[r, :].astype(f32),
            own_1[r, :].astype(f32) + other_1[r, :].astype(f32),
        )
        mean = row_sum(x * dn) / width
        d = g[r, :].astype(f32) + scale * dn - x * (scale * scale * scale * mean)
        dh[r, :] = d
        branch[r, :] = d.astype(bf16)

    loop(rows, 16, hid)
    dm_own[...] = dot_t(branch[...], wo_own[...])
    dm_other[...] = dot_t(branch[...], wo_other[...])

    def att(r, start):
        a, b = att_own[r, :].astype(f32), att_other[r, :].astype(f32)
        scale = scale_of(row_sum(a * a) + row_sum(b * b), width)
        m = dm_own[r, :]
        dgates[r, :] = (m * (a * scale)).astype(bf16)
        da = m * u_own[r, :].astype(f32)
        db = dm_other[r, :] * u_other[r, :].astype(f32)
        mean = (row_sum(a * da) + row_sum(b * db)) / width
        d = (scale * da - a * (scale * scale * scale * mean)).astype(bf16)
        datt[r, :] = d
        place = row_numbers(start + 1, 16, dim)
        for h in range(heads):
            dd = d[:, h * dim : (h + 1) * dim].astype(f32)
            es[r, head(h, dim)] = (dd * jnp.exp(-rate[h] * place)).astype(bf16)

    loop(rows, 16, att)
    for h in range(heads):
        c = head(h, dim)
        direct[b, h] = t_dot(q[:, c], es[:, c])

    @pl.when(i == 1)
    def _():
        for h in range(heads):
            carried = jnp.exp(wide(-rate[h] * block, dim))
            local[h] = (direct[0, h] + carried * direct[1, h]).astype(bf16)


def attend_back(block, heads, dim, info, q, k, v, datt, states, pq, cs, sn, rate, gq, dk, dv):
    for h in range(heads):
        c = head(h, dim)
        state = states[0, h]
        fall = fall_of(rate[h])
        for start in reversed(range(0, block, CHUNK)):
            r, upto = pl.ds(start, CHUNK), start + CHUNK
            decay = decay_of(rate[h], start, fall)
            qc, da = q[r, c], datt[r, c]
            weights = (dot_t(qc, k[:upto, c]) * decay).astype(bf16)
            dscore = (dot_t(da, v[:upto, c]) * decay).astype(bf16)
            entering = jnp.exp(-rate[h] * (row_numbers(start, CHUNK, dim) + 1.0))
            e = (da.astype(f32) * entering).astype(bf16)
            dq = dot(dscore, k[:upto, c]) + dot_t(e, state)
            slope = swish_slope(pq[r, c].astype(f32))
            gq[r, c] = (slope * rotate(dq, cs[r, :], -sn[r, :])).astype(bf16)
            dk_term, dv_term = t_dot(dscore, qc), t_dot(weights, da)
            if upto == block:
                dk[:, c] = dk_term
                dv[:, c] = dv_term
            else:
                dk[:upto, c] = dk[:upto, c] + dk_term
                dv[:upto, c] = dv[:upto, c] + dv_term


def finish_back(block, heads, dim, count, info, k, v, dk, dv, direct, pk, pv, cs, sn, rate, gq, near, far, out, after):
    b = pl.program_id(0)
    half = heads * dim
    out[:, :half] = gq[...]
    for h in range(heads):
        c = head(h, dim)
        last = state_sum(near, far, count, h, rate, 2 * block, dim, info[4], True)
        before = jnp.exp(wide(-rate[h] * block, dim)) * last + direct[1, h]
        after[...] = jnp.where(b == 1, last, before).astype(bf16)
        for start in range(0, block, CHUNK):
            r = pl.ds(start, CHUNK)
            leaving = jnp.exp(-rate[h] * (block - 1.0 - row_numbers(start, CHUNK, dim)))
            kd = (k[r, c].astype(f32) * leaving).astype(bf16)
            key_grad = dk[r, c] + leaving * dot_t(v[r, c], after[...])
            value_grad = dv[r, c] + dot(kd, after[...])
            gk = swish_slope(pk[r, c].astype(f32)) * rotate(key_grad, cs[r, :], -sn[r, :])
            out[r, pl.ds(half + h * dim, dim)] = gk.astype(bf16)
            out[r, pl.ds(2 * half + h * dim, dim)] = (
                swish_slope(pv[r, c].astype(f32)) * value_grad
            ).astype(bf16)


def add_kernel(info, *refs):
    *terms, out = refs

    def body(r, _):
        total = terms[0][r, :].astype(f32)
        for term in terms[1:]:
            total = total + term[r, :].astype(f32)
        out[r, :] = total.astype(bf16)

    loop(out.shape[0], 16, body)


def join_kernel(info, *refs):
    out = refs[6]
    cut = refs[0].shape[1]
    add_kernel(info, *refs[:3], out.at[:, pl.ds(0, cut)])
    add_kernel(info, *refs[3:6], out.at[:, pl.ds(cut, out.shape[1] - cut)])


def choose_kernel(info, mine, arrived, out):
    place = info[4]
    inner = (place == 1) | (place == 2)

    def body(r, _):
        value = jnp.where(inner, mine[r, :].astype(f32), arrived[r, :].astype(f32))
        out[r, :] = value.astype(bf16)

    loop(out.shape[0], 16, body)


def choose(info, pieces, use):
    step = pl.program_id(0)
    first = (step // 2) != info[1]
    second = lax.rem(step, 2) != info[2]
    for index, piece in enumerate(pieces):
        at_first, at_second = index >= 2, index % 2 == 1

        @pl.when((first == at_first) & (second == at_second))
        def _(piece=piece):
            use(piece)


def place_whole(info, *refs):
    pieces, out = refs[:4], refs[4]

    def put(piece):
        out[...] = piece[...].astype(f32)

    choose(info, pieces, put)


def place_turned(info, *refs):
    pieces, out = refs[:4], refs[4]

    def put(piece):
        out[...] = piece[...].astype(f32).T

    choose(info, pieces, put)


def place_heads(info, *refs):
    qkv, others, out = refs[:4], refs[4:8], refs[8]
    width = out.shape[2]
    last = qkv[0].shape[1] - 2 * width

    def put_qkv(piece):
        for j in range(2):
            out[:, j, :] = piece[:, pl.ds(j * width, width)].astype(f32)
        out[:, 2, :last] = piece[:, 2 * width :].astype(f32)

    def put_others(piece):
        out[:, 3, :] = piece[:, :width].astype(f32)
        out[:, 2, last:] = piece[:, 2 * width :].astype(f32)

    choose(info, qkv, put_qkv)
    choose(info, others, put_others)


def place_rows(info, *refs):
    pieces, out = refs[:4], refs[4]
    rows, width = out.shape[0], out.shape[1] // 2

    def put(piece):
        out[:, :width] = piece[:rows, width : 2 * width].astype(f32)
        out[:, width:] = piece[rows:, width : 2 * width].astype(f32)

    choose(info, pieces, put)


def swap(value, axis, bit):
    return lax.ppermute(value, axis, [(i, i ^ bit) for i in range(lax.axis_size(axis))])


def shift(value, axis, distance):
    count = lax.axis_size(axis)
    return lax.ppermute(
        value, axis, [(i, i + distance) for i in range(count) if 0 <= i + distance < count]
    )


def cross(value, turn):
    pairs = []
    for place in range(lax.axis_size("dp")):
        for core in range(2):
            pairs.append((2 * place + core, 2 * (place ^ (1 << (core ^ turn))) + core))
    return lax.ppermute(value, ("dp", "heads"), pairs)


def part(value, index, rows, axis=0):
    return lax.dynamic_slice_in_dim(value, index * rows, rows, axis)


def add(*terms):
    total = terms[0].astype(f32)
    for term in terms[1:]:
        total = total + term.astype(f32)
    return total.astype(bf16)


class States:
    def __init__(self, spine, local, rate, rows, backward):
        self.spine, self.local, self.rate = spine, local, rate
        self.rows, self.backward = rows, backward
        self.count = lax.axis_size("seq")
        if self.count == 4:
            self.near = swap(local, "seq", 1)

    def second(self):
        if self.count == 4:
            (self.near,) = self.spine.wait(self.near)
            here = View(lambda ref, i, s: ref)
            heads, dim = self.local.shape[:2]
            body = functools.partial(pair_states, heads=heads, dim=dim, rows=self.rows, backward=self.backward, count=4)

            def kernel(info, own, near, rate, out):
                body(info, own=own, near=near, rate=rate, out=out)

            ins = [(self.local, here), (self.near, here), (self.rate, SMEM)]
            outs = [(self.local.shape, bf16, here)]
            self.far = swap(self.spine.call(kernel, 1, ins, outs, name="pair_states")[0], "seq", 2)

    def all(self):
        if self.count == 4:
            (far,) = self.spine.wait(self.far)
            return self.near, far
        sign = -1 if self.backward else 1
        total = shift(self.local.astype(f32), "seq", sign)
        distance = 1
        while distance < self.count - 1:
            power = jnp.exp(-self.rate * self.rows * distance)[:, None, None]
            total = total + power * shift(total, "seq", sign * distance)
            distance *= 2
        return total, total


class Sum:
    last = None

    def __init__(self, spine, send, keep=None, there=None):
        self.spine, self.keep, self.cut = spine, keep, there is not None
        self.first = cross(send, 0)
        self.second_part = cross(there, 0) if self.cut else None
        self.shape = send.shape[0] if self.cut else send.shape[0] // 2, send.shape[1]
        self.four = lax.axis_size("seq") == 4

    def combine(self, body, *terms):
        rows = self.shape[0]

        def view(turn):
            if turn is None:
                return View(lambda ref, i, s: ref)
            return View(lambda ref, i, s: ref.at[span(1 - s[2] if turn else s[2], rows), :])

        ins = [(value, view(turn)) for value, turn in terms]
        outs = [(self.shape, bf16, view(None))]
        return self.spine.call(body, 1, ins, outs, name="combine")[0]

    def second(self):
        (self.first,) = self.spine.wait(self.first)
        turn = None if self.cut else True
        self.across = cross(self.combine(add_kernel, (self.keep, True), (self.first, turn)), 1)

    def last_second(self):
        self.last.second()

    def last_wait(self):
        (self.last.across,) = self.spine.wait(self.last.across)

    def line(self):
        if self.cut:
            across, first = self.spine.wait(self.across, self.second_part)
            first = first, None
        else:
            (across,) = self.spine.wait(self.across)
            first = self.first, False
        terms = [(self.keep, False), first, (across, None)]
        if self.last is None:
            self.value = self.combine(add_kernel, *terms)
        else:
            last = self.last
            terms += [(last.keep, False), (last.first, False), (last.across, None)]
            self.shape = self.shape[0], self.shape[1] + self.last.shape[1]
            self.value = self.combine(join_kernel, *terms)
        if self.four:
            self.inward = lax.ppermute(self.value, "seq", [(0, 1), (3, 2)])

    def line_across(self):
        if self.four:
            (inward,) = self.spine.wait(self.inward)
            self.value = self.combine(add_kernel, (self.value, None), (inward, None))
            self.middle = lax.ppermute(self.value, "seq", [(1, 2), (2, 1)])

    def line_back(self):
        if self.four:
            (middle,) = self.spine.wait(self.middle)
            self.value = self.combine(add_kernel, (self.value, None), (middle, None))
            self.outer = lax.ppermute(self.value, "seq", [(1, 0), (2, 3)])

    def spread(self):
        if self.four:
            (outer,) = self.spine.wait(self.outer)
            total = self.combine(choose_kernel, (self.value, None), (outer, None))
        else:
            total = lax.psum(self.value.astype(f32), "seq").astype(bf16)
            self.spine.after(total)
        self.value, self.second_half, self.own_first = total, cross(total, 1), cross(total, 0)

    def spread_on(self):
        (second,) = self.spine.wait(self.second_half)
        self.pieces = [self.value, second, self.own_first, cross(second, 0)]

    def arrive(self):
        self.pieces[2:] = self.spine.wait(*self.pieces[2:])
        return self.pieces


def shards(
    tokens,
    cotangent,
    qkvu_weight,
    out_weight,
    up_weight,
    gate_weight,
    down_weight,
    decay_rate,
    item_length,
    item_slot,
):
    core = lax.axis_index("heads")
    seq_place = lax.axis_index("seq")
    data_place = lax.axis_index("dp")
    block, width = tokens.shape[1:]
    heads = decay_rate.shape[0]
    half = qkvu_weight.shape[2]
    dim = half // heads
    ff = up_weight.shape[1] // 2
    rows = 2 * block
    tile = block // 2
    rate = (decay_rate, SMEM)

    own, own_cot = tokens[0], cotangent[0]
    other = swap(own, "heads", 1)
    other_cot = swap(own_cot, "heads", 1)
    other_out = swap(out_weight, "heads", 1)
    weights = jnp.transpose(qkvu_weight, (1, 0, 2))
    fine = 32
    lanes = jnp.arange(dim)
    frequency = 10000.0 ** (-(lanes % (dim // 2)).astype(f32) / (dim // 2))
    coarse_steps = seq_place * rows + fine * jnp.arange(rows // fine)
    steps = jnp.concatenate([coarse_steps, jnp.arange(fine)]).astype(f32)
    angles = steps[:, None] * frequency[None, :]
    cosine, sine = lax.optimization_barrier((jnp.cos(angles), jnp.sin(angles)))
    c_far, s_far = cosine[:-fine, None, :], sine[:-fine, None, :]
    c_near, s_near = cosine[None, -fine:, :], sine[None, -fine:, :]
    sign = jnp.where(lanes < dim // 2, -1.0, 1.0)
    cs = (c_far * c_near - s_far * s_near).reshape(rows, dim)
    sn = (sign * (s_far * c_near + c_far * s_near)).reshape(rows, dim)

    def weight(j):
        return weights, View(lambda ref, i, s: ref.at[pl.ds(j, 1)])

    def by(value, size):
        return value, View(lambda ref, i, s: ref.at[span(i, size), :])

    def all_of(value):
        return value, View(lambda ref, i, s: ref)

    def out(columns, kind, size):
        return (rows, columns), kind, View(lambda ref, i, s: ref.at[span(i, size), :])

    def fixed(shape, kind):
        return shape, kind, View(lambda ref, i, s: ref)

    def fn(body, *sizes):
        return functools.partial(body, *sizes)

    down_half = down_weight, View(lambda ref, i, s: ref.at[span(s[0], ff), :])
    columns = View(lambda ref, i, s: ref.at[:, span(s[0], ff)])
    up_half, gate_half = (up_weight, columns), (gate_weight, columns)
    spine = Spine()
    call = spine.call
    square = (heads, dim, dim)
    big, low = pltpu.VMEM((block, half), f32), pltpu.VMEM((block, half), bf16)

    def turned(columns):
        return (columns, rows), bf16, View(lambda ref, i, s: ref.at[:, span(i, block)])

    normed, normed_t, k, v, pk, pv, contrib, local = call(
        fn(project_kv, block, heads, dim),
        2,
        [all_of(own), all_of(other), weight(1), weight(2), by(cs, block), by(sn, block)]
        + [rate],
        [out(width, bf16, block), turned(width)]
        + [out(half, bf16, block)] * 4
        + [fixed((2,) + square, f32), fixed(square, bf16)],
        [big, big, low],
        name="project_kv",
    )
    line = States(spine, local, decay_rate, rows, False)
    g, g_t, grad_inner, valid = call(
        fn(begin_back, block),
        2,
        [all_of(own_cot), all_of(other_cot), down_half]
        + [(item_slot, SMEM), (item_length, SMEM)],
        [out(width, bf16, block), turned(width), out(ff, bf16, block), out(dim, f32, block)],
        name="begin_back",
    )
    line.second()
    q, pq, u_own, intra = call(
        fn(project_qu, block, heads, dim),
        2,
        [by(normed, block), weight(0), weight(3), by(cs, block), by(sn, block), rate]
        + [by(k, block), by(v, block)],
        [out(half, bf16, block)] * 3 + [out(half, f32, block)],
        [big],
        name="project_qu",
    )
    u_other = swap(u_own, "heads", 1)
    near, far = line.all()
    att_own, states = call(
        fn(attend, block, heads, dim, line.count),
        1,
        [all_of(q), all_of(intra), all_of(contrib), rate, all_of(near), all_of(far)],
        [fixed((rows, half), bf16), fixed((2,) + square, bf16)],
        name="attend",
    )
    att_other = swap(att_own, "heads", 1)
    att_u = [by(att_own, block), by(att_other, block), by(u_own, block), by(u_other, block)]
    out_both = [all_of(out_weight), all_of(other_out)]
    hidden, n2, n2_t, mixed_t = call(
        fn(mix_out, block),
        2,
        att_u + out_both + [all_of(own), all_of(other)],
        [out(width, f32, block), out(width, bf16, block), turned(width), turned(half)],
        [pltpu.VMEM((block, width), bf16)],
        name="mix_out",
    )
    inner, grad_left, grad_right = call(
        fn(feed, block),
        2,
        [by(n2, block), up_half, gate_half, by(grad_inner, block)],
        [out(ff, bf16, block)] * 3,
        [pltpu.VMEM((block, ff), f32)] * 2,
        name="feed",
    )

    def halves(value):
        size = value.shape[0] // 2

        def at(ref, i, s):
            return ref.at[span(jnp.where(i == 0, 1 - s[1], s[1]), size), :]

        return value, View(at)

    def grad(name, lhs, rhs):
        shape = lhs.shape[0] // 2, rhs.shape[1]
        return call(
            weight_grad, 2, [halves(lhs), all_of(rhs)], [fixed(shape, bf16)] * 2, name=name
        )

    def sides(value):
        def at(ref, i, s):
            return ref.at[span(jnp.where(i == 0, 1 - s[0], s[0]), block), :]

        return value, View(at)

    two_sides = [fixed((block, width), bf16)] * 2

    def half_grad(name, lhs, rhs, send):
        size = lhs.shape[0] // 2

        def at(ref, i, s):
            return ref.at[span(1 - s[1] if send else s[1], size), :]

        shape = size, rhs.shape[1]
        ins = [(lhs, View(at)), all_of(rhs)]
        return call(weight_half, 1, ins, [fixed(shape, bf16)], name=name)[0]

    down = Sum(spine, half_grad("down_send", g_t, inner, True))
    partial = call(
        back_two,
        2,
        [by(grad_left, block), by(grad_right, block), up_half, gate_half],
        two_sides,
        name="back_two",
    )
    partial_other = [swap(value, "heads", 1) for value in partial]
    up = Sum(spine, *grad("up_grad", n2_t, grad_left))
    gate = Sum(spine, *grad("gate_grad", n2_t, grad_right))
    down.keep = half_grad("down_keep", g_t, inner, False)
    partial_other = spine.wait(*partial_other)
    down.second()
    dh, branch, dgates, datt, direct, local = call(
        fn(back_mix, block, block, heads, dim),
        2,
        [all_of(x) for x in (*partial, *partial_other)]
        + [sides(x) for x in (hidden, g, att_own, att_other, u_own, u_other)]
        + out_both
        + [sides(q), rate],
        [fixed((block, width), f32)]
        + [((rows, size), bf16, sides(None)[1]) for size in (width, half, half)]
        + [fixed((2,) + square, f32), fixed(square, bf16)],
        [pltpu.VMEM((block, half), f32)] * 2 + [pltpu.VMEM((block, half), bf16)],
        name="back_mix",
    )
    flat = pl.BlockSpec((width // 4, ff), lambda i: (i, 0))

    def place(body, pieces, shape, spec, name):
        return call(
            body, 4, [(p, whole(p)) for p in pieces], [(shape, f32, spec)], name=name
        )[0]
    line = States(spine, local, decay_rate, rows, True)
    out_u = call(
        out_u_grad,
        2,
        [halves(mixed_t), all_of(branch), halves(normed_t), all_of(dgates)],
        [fixed((block, width), bf16)] * 2,
        name="out_u_grad",
    )
    out_u = Sum(spine, *out_u)
    line.second()
    up.second()
    down.line()
    gq, dk, dv = call(
        fn(attend_back, block, heads, dim),
        2,
        [by(q, block), by(k, block), by(v, block), by(datt, block)]
        + [(states, View(lambda ref, i, s: ref.at[pl.ds(i, 1)])), by(pq, block)]
        + [by(cs, block), by(sn, block), rate],
        [out(half, bf16, block), out(half, f32, block), out(half, f32, block)],
        name="attend_back",
    )
    near, far = line.all()
    down.line_across()
    up.line()
    grads = call(
        fn(finish_back, block, heads, dim, line.count),
        2,
        [by(k, block), by(v, block), by(dk, block), by(dv, block), all_of(direct)]
        + [by(pk, block), by(pv, block), by(cs, block), by(sn, block), rate]
        + [by(gq, block), all_of(near), all_of(far)],
        [out(3 * half, bf16, block)],
        [pltpu.VMEM((dim, dim), bf16)],
        name="finish_back",
    )[0]
    flat = pl.BlockSpec((width // 4, ff), lambda i: (i, 0))

    def place(body, pieces, shape, spec, name):
        return call(
            body, 4, [(p, whole(p)) for p in pieces], [(shape, f32, spec)], name=name
        )[0]

    quarter = rows // 4
    on, there, keep, last_send, last_keep = call(
        weight_grad_cut,
        2,
        [halves(normed_t), all_of(grads)],
        [fixed((quarter, ff), bf16)] * 2
        + [fixed((block, ff), bf16)]
        + [fixed((block, 3 * half - ff), bf16)] * 2,
        name="qkv_grad",
    )
    qkv = Sum(spine, on, keep, there)
    out_u.last = Sum(spine, last_send, last_keep)
    gate.second()
    send_in, keep_in = call(
        back_in,
        2,
        [sides(dgates), sides(grads), all_of(weights)],
        two_sides,
        name="back_in",
    )
    out_u.second()
    down.line_back()
    up.line_across()
    sends, keep_out = call(
        split_product,
        2,
        [sides(inner), down_half, sides(hidden), all_of(send_in)],
        [fixed((2, block, width), bf16), fixed((block, width), f32)],
        name="split_product",
    )
    gate.line()
    qkv.second()
    down.spread()
    up.line_back()
    qkv.line()
    gate.line_across()
    out_u.last_second()
    down.spread_on()
    up.spread()
    qkv.line_across()
    gate.line_back()
    out_u.last_wait()
    out_u.line()
    down_grad = place(
        place_turned,
        down.arrive(),
        (ff, width),
        pl.BlockSpec((ff, width // 4), lambda i: (0, i)),
        "place_down",
    )
    (sends,) = spine.wait(sends)
    arrived_both = [swap(sends[n], "heads", 1) for n in range(2)]
    up.spread_on()
    qkv.line_back()
    gate.spread()
    out_u.line_across()
    up_grad = place(place_whole, up.arrive(), (width, ff), flat, "place_up")
    gate.spread_on()
    qkv.spread()
    out_u.line_back()
    qkv.spread_on()
    out_u.spread()
    gate_grad = place(place_whole, gate.arrive(), (width, ff), flat, "place_gate")
    out_u.spread_on()
    arrived_in, arrived_out = spine.wait(*arrived_both)
    def own_rows(value):
        return part(value, core, block)

    def add_wide(a, b):
        return a.astype(f32) + b.astype(f32)

    output = add_wide(keep_out, arrived_out)
    output = (output * own_rows(valid)[:, :1]).astype(bf16)
    x = own.astype(f32)
    scale = lax.rsqrt(jnp.mean(x * x, axis=-1, keepdims=True) + epsilon)
    dn = add_wide(keep_in, arrived_in)
    grad_inputs = (
        dh
        + scale * dn
        - x * (scale * scale * scale) * jnp.mean(x * dn, axis=-1, keepdims=True)
    )
    spine.after(output, grad_inputs)
    out_u_pieces = out_u.arrive()
    out_grad = place(
        place_rows,
        out_u_pieces,
        (half, width),
        pl.BlockSpec((half // 4, width), lambda i: (i, 0)),
        "place_out",
    )
    qkvu_grad = place(
        place_heads,
        qkv.arrive() + out_u_pieces,
        (width, 4, half),
        pl.BlockSpec((width // 4, 4, half), lambda i: (i, 0, 0)),
        "place_qkvu",
    )
    return output[None], grad_inputs[None], qkvu_grad, out_grad, up_grad, gate_grad, down_grad


def solution(mesh):
    placed = (
        P("dp", ("seq", "heads"), None),
        P("dp", ("seq", "heads"), None),
        P(None, None, "heads"),
        P("heads", None),
        P(),
        P(),
        P(),
        P("heads"),
        P(),
        P(),
    )
    return jax.shard_map(
        shards,
        mesh=mesh,
        in_specs=placed,
        out_specs=(
            P("dp", ("seq", "heads"), None),
            P("dp", ("seq", "heads"), None),
            P(None, None, "heads"),
            P("heads", None),
            P(None, "heads"),
            P(None, "heads"),
            P("heads", None),
        ),
        check_vma=False,
    )
```

```python
import functools
import math

import jax
import jax.numpy as jnp
from jax import lax
from jax.experimental import pallas as pl
from jax.experimental.pallas import tpu as pltpu
from jax.sharding import PartitionSpec as P

epsilon = 1e-06
f32 = jnp.float32
bf16 = jnp.bfloat16
CHUNK = 512


def dot(a, b):
    return jnp.dot(a, b, preferred_element_type=f32)


def dot_t(a, b):
    return lax.dot_general(a, b, (((1,), (1,)), ((), ())), preferred_element_type=f32)


def t_dot(a, b):
    return lax.dot_general(a, b, (((0,), (0,)), ((), ())), preferred_element_type=f32)


def whole(value):
    rank = value.ndim
    return pl.BlockSpec(value.shape, lambda i: (0,) * rank, pipeline_mode=pl.Buffered(1))


class View:
    block_shape = None

    def __init__(self, at):
        self.at = at


class Places:
    def __getitem__(self, index):
        core, data = lax.axis_index("heads"), lax.axis_index("dp")
        low, high = lax.rem(data, 2), data // 2
        if index == 0:
            return core
        if index == 1:
            return jnp.where(core == 0, low, high)
        if index == 2:
            return jnp.where(core == 0, high, low)
        return data if index == 3 else lax.axis_index("seq")


def span(index, size):
    return pl.ds(pl.multiple_of(index * size, size), size)


def spec_of(spec):
    return pl.BlockSpec(memory_space=pltpu.VMEM) if isinstance(spec, View) else spec


def room(blocks, scratch, name):
    total = 0
    for spec, kind in blocks:
        if spec.block_shape is not None:
            buffers = 1 if spec.pipeline_mode is not None else 2
            total += buffers * math.prod(spec.block_shape) * jnp.dtype(kind).itemsize
    for buffer in scratch:
        if buffer.dtype in (f32, bf16):
            total += math.prod(buffer.shape) * jnp.dtype(buffer.dtype).itemsize
    return total + SLACK.get(name, 4) * 2**20


SLACK = {"begin_back": 5, "attend_back": 5, "split_product": 6, "back_two": 8}


def tiles(value, rows):
    return pl.BlockSpec((rows, value.shape[1]), lambda i: (i, 0))


SMEM = pl.BlockSpec(memory_space=pltpu.SMEM)


class Spine:
    def __init__(self):
        self.token = None
        self.done = []

    def call(self, body, steps, ins, outs, scratch=(), name=None):
        after = self.done + ([] if self.token is None else [self.token])
        used, given = len(ins), len(outs)
        specs = [spec for _, spec in ins] + [spec for _, _, spec in outs]
        blocks = [(spec, value.dtype) for value, spec in ins]
        blocks += [(spec, kind) for _, kind, spec in outs]

        def kernel(*refs):
            rest = refs[used + len(after) :]
            rest[given][...] = jnp.zeros((8, 128), f32)
            step, places = pl.program_id(0), Places()
            given_refs = [
                spec.at(ref, step, places) if isinstance(spec, View) else ref
                for spec, ref in zip(specs, list(refs[:used]) + list(rest[:given]))
            ]
            body(places, *given_refs, *rest[given + 1 :])

        results = pl.pallas_call(
            kernel,
            grid=(steps,),
            in_specs=[spec_of(spec) for _, spec in ins]
            + [pl.BlockSpec(memory_space=pl.ANY)] * len(after),
            out_specs=[spec_of(spec) for _, _, spec in outs]
            + [pl.BlockSpec(memory_space=pltpu.VMEM)],
            scratch_shapes=list(scratch),
            out_shape=[jax.ShapeDtypeStruct(shape, kind) for shape, kind, _ in outs]
            + [jax.ShapeDtypeStruct((8, 128), f32)],
            compiler_params=pltpu.CompilerParams(vmem_limit_bytes=room(blocks, scratch, name)),
            cost_estimate=pl.CostEstimate(flops=0, bytes_accessed=0, transcendentals=0),
            name=name,
        )(*[value for value, _ in ins], *after)
        self.token, self.done = results[-1], []
        return results[:-1]

    def after(self, *values):
        self.done += values

    def wait(self, *values):
        if self.done:
            token = self.token
            for value in self.done:
                token = token + value[:8, :128].astype(f32)
            self.token, self.done = token, []
        results = lax.optimization_barrier((self.token,) + values)
        self.token = results[0]
        return results[1:]


def loop(count, step, body, unroll=True):
    def turn(i, _):
        body(pl.ds(pl.multiple_of(i * step, step), step), i * step)
        return 0

    lax.fori_loop(0, count // step, turn, 0, unroll=unroll)


def head(h, dim):
    return pl.ds(h * dim, dim)


def rotate(value, cosine, sine):
    return value * cosine + pltpu.roll(value, value.shape[1] // 2, 1) * sine


def sigmoid(value):
    return 0.5 * jnp.tanh(0.5 * value) + 0.5


def swish(value):
    return value * sigmoid(value)


def swish_slope(value):
    s = sigmoid(value)
    y = value * s
    return y + s * (1.0 - y)


def row_numbers(start, rows, columns):
    return (lax.broadcasted_iota(jnp.int32, (rows, columns), 0) + start).astype(f32)


def fall_of(rate):
    return jnp.exp(-rate * row_numbers(0, CHUNK, CHUNK))


def decay_of(rate, start, fall):
    upto = start + CHUNK
    columns = lax.broadcasted_iota(jnp.int32, (1, upto), 1).astype(f32)
    rise = jnp.exp(rate * (columns - float(start)))
    tiles = [rise[:, j : j + CHUNK] * fall for j in range(0, upto, CHUNK)]
    rows = lax.broadcasted_iota(jnp.int32, (CHUNK, CHUNK), 0)
    inside = rows >= lax.broadcasted_iota(jnp.int32, (CHUNK, CHUNK), 1)
    tiles[-1] = jnp.where(inside, tiles[-1], 0.0)
    return jnp.concatenate(tiles, 1) if start else tiles[0]


def scale_of(total, width):
    return lax.rsqrt(total / width + epsilon)


def row_sum(value):
    return jnp.sum(value, axis=-1, keepdims=True)


def wide(scalar, dim):
    return jnp.full((1, dim), scalar, f32)


def project_kv(block, heads, dim, info, own, other, wk, wv, cs, sn, rate, normed, turned, k, v, pk, pv, contrib, local, sk, sv, kd):
    b = pl.program_id(0)
    mine = b == info[0]
    width = own.shape[1]

    def norm(r, _):
        x = jnp.where(mine, own[r, :].astype(f32), other[r, :].astype(f32))
        normed[r, :] = (x * scale_of(row_sum(x * x), width)).astype(bf16)

    loop(block, 16, norm)
    sk[...] = dot(normed[...], wk[0])
    sv[...] = dot(normed[...], wv[0])
    turned[...] = normed[...].T

    def act(r, start):
        cosine, sine = cs[r, :], sn[r, :]
        steps = block - 1.0 - row_numbers(start, 64, dim)
        for h in range(heads):
            c = head(h, dim)
            p = sk[r, c]
            pk[r, c] = p.astype(bf16)
            key = rotate(swish(p), cosine, sine).astype(bf16)
            k[r, c] = key
            kd[r, c] = (key.astype(f32) * jnp.exp(-rate[h] * steps)).astype(bf16)
            p = sv[r, c]
            pv[r, c] = p.astype(bf16)
            v[r, c] = swish(p).astype(bf16)

    loop(block, 64, act)
    for h in range(heads):
        c = head(h, dim)
        contrib[b, h] = t_dot(kd[:, c], v[:, c])

    @pl.when(b == 1)
    def _():
        for h in range(heads):
            carried = jnp.exp(wide(-rate[h] * block, dim))
            local[h] = (carried * contrib[0, h] + contrib[1, h]).astype(bf16)


def project_qu(block, heads, dim, info, normed, wq, wu, cs, sn, rate, k, v, q, pq, u, intra, sq):
    sq[...] = dot(normed[...], wq[0])
    u[...] = dot(normed[...], wu[0]).astype(bf16)

    def act(r, start):
        cosine, sine = cs[r, :], sn[r, :]
        for h in range(heads):
            c = head(h, dim)
            p = sq[r, c]
            pq[r, c] = p.astype(bf16)
            q[r, c] = rotate(swish(p), cosine, sine).astype(bf16)

    loop(block, 64, act)
    for h in range(heads):
        c = head(h, dim)
        fall = fall_of(rate[h])
        for start in range(0, block, CHUNK):
            r, upto = pl.ds(start, CHUNK), start + CHUNK
            scores = dot_t(q[r, c], k[:upto, c]) * decay_of(rate[h], start, fall)
            intra[r, c] = dot(scores.astype(bf16), v[:upto, c])


def pair_states(info, count, heads, dim, rows, backward, own, near, rate, out):
    even = lax.rem(info[4], 2) == 0
    for h in range(heads):
        decay = jnp.exp(wide(-rate[h] * rows, dim))
        a, b = own[h].astype(f32), near[h].astype(f32)
        plain, decayed = (a, b) if backward else (b, a)
        other = (b, a) if backward else (a, b)
        out[h] = jnp.where(even, plain + decay * decayed, other[0] + decay * other[1]).astype(bf16)


def state_sum(near, far, count, h, rate, rows, dim, place, backward):
    if count != 4:
        return near[h]
    side = lax.rem(place, 2) == (0 if backward else 1)
    pair = place < 2 if backward else place >= 2
    decay = jnp.where(side, jnp.exp(wide(-rate[h] * rows, dim)), 1.0)
    first = jnp.where(side, near[h].astype(f32), 0.0)
    return first + jnp.where(pair, decay * far[h].astype(f32), 0.0)


def attend(block, heads, dim, count, info, q, intra, contrib, rate, near, far, att, states):
    for h in range(heads):
        c = head(h, dim)
        first = state_sum(near, far, count, h, rate, 2 * block, dim, info[4], False)
        second = jnp.exp(wide(-rate[h] * block, dim)) * first + contrib[0, h]
        for b, state in enumerate((first, second)):
            states[b, h] = state.astype(bf16)
        for b in range(2):
            state = states[b, h]
            for start in range(0, block, CHUNK):
                r = pl.ds(b * block + start, CHUNK)
                entering = jnp.exp(-rate[h] * (row_numbers(start, CHUNK, dim) + 1.0))
                att[r, c] = (intra[r, c] + entering * dot(q[r, c], state)).astype(bf16)


def begin_back(rows, info, own, other, down, item_slot, item_length, g, turned, grad_inner, valid):
    i = pl.program_id(0)
    mine = i == info[0]
    limit = item_length[item_slot[info[3]]] - (2 * info[4] + i) * rows

    def read(r, start):
        value = jnp.where(mine, own[r, :].astype(f32), other[r, :].astype(f32))
        inside = lax.broadcasted_iota(jnp.int32, value.shape, 0) + start < limit
        g[r, :] = jnp.where(inside, value, 0.0).astype(bf16)

    loop(rows, 16, read)
    valid[...] = (lax.broadcasted_iota(jnp.int32, valid.shape, 0) < limit).astype(f32)
    grad_inner[...] = dot_t(g[...], down[...]).astype(bf16)
    turned[...] = g[...].T


def mix_out(rows, info, att_own, att_other, u_own, u_other, wo_own, wo_other, own, other, hidden, n2, mixed, both):
    mine = pl.program_id(0) == info[0]
    half = att_own.shape[1]
    width = 2 * half

    def mix(r, _):
        a, b = att_own[r, :].astype(f32), att_other[r, :].astype(f32)
        scale = scale_of(row_sum(a * a) + row_sum(b * b), width)
        both[r, :half] = (a * scale * u_own[r, :].astype(f32)).astype(bf16)
        both[r, half:] = (b * scale * u_other[r, :].astype(f32)).astype(bf16)

    loop(rows, 16, mix)
    hidden[...] = dot(both[:, :half], wo_own[...]) + dot(both[:, half:], wo_other[...])
    mixed[...] = both[:, :half]

    def norm(r, _):
        x = jnp.where(mine, own[r, :].astype(f32), other[r, :].astype(f32))
        x = hidden[r, :] + x
        hidden[r, :] = x
        n2[r, :] = (x * scale_of(row_sum(x * x), width)).astype(bf16)

    loop(rows, 16, norm)


def feed(rows, info, n2, up, gate, grad_inner, inner, grad_left, grad_right, left, right):
    left[...] = dot(n2[...], up[...])
    right[...] = dot(n2[...], gate[...])

    def join(r, _):
        a, b, g = left[r, :], right[r, :], grad_inner[r, :].astype(f32)
        inner[r, :] = (a * b).astype(bf16)
        grad_left[r, :] = (g * b).astype(bf16)
        grad_right[r, :] = (g * a).astype(bf16)

    loop(rows, 16, join)


def weight_half(info, lhs, rhs, out):
    out[...] = dot(lhs[...], rhs[...]).astype(bf16)


def weight_grad(info, lhs, rhs, send, keep):
    step = pl.program_id(0)

    @pl.when(step == 0)
    def _():
        send[...] = dot(lhs[...], rhs[...]).astype(bf16)

    @pl.when(step == 1)
    def _():
        keep[...] = dot(lhs[...], rhs[...]).astype(bf16)


def weight_grad_cut(info, lhs, rhs, on, there, keep, last_send, last_keep):
    step = pl.program_id(0)
    columns, rows = keep.shape[1], on.shape[0]

    @pl.when(step == 0)
    def _():
        for out, place in ((on, 1 - info[2]), (there, info[2])):
            out[...] = dot(lhs[span(place, rows), :], rhs[:, :columns]).astype(bf16)
        last_send[...] = dot(lhs[...], rhs[:, columns:]).astype(bf16)

    @pl.when(step == 1)
    def _():
        keep[...] = dot(lhs[...], rhs[:, :columns]).astype(bf16)
        last_keep[...] = dot(lhs[...], rhs[:, columns:]).astype(bf16)


def out_u_grad(info, mixed, branch, normed, dgates, send, keep):
    step = pl.program_id(0)
    half = dgates.shape[1]
    rows = mixed.shape[0] // 2

    def both(out):
        out[:, :half] = dot(normed[...], dgates[...]).astype(bf16)
        for side in range(2):
            result = dot(mixed[...], branch[:, pl.ds(side * half, half)]).astype(bf16)
            for quarter in range(2):
                piece = result[quarter * rows : (quarter + 1) * rows, :]
                out[pl.ds((2 * quarter + side) * rows, rows), half:] = piece

    @pl.when(step == 0)
    def _():
        both(send)

    @pl.when(step == 1)
    def _():
        both(keep)


def back_two(info, grad_left, grad_right, up, gate, n2, mixed, first, second, n2_turned, mixed_turned):
    n2_turned[...] = n2[...].T
    mixed_turned[...] = mixed[...].T
    result = (dot_t(grad_left[...], up[...]) + dot_t(grad_right[...], gate[...])).astype(bf16)
    i = pl.program_id(0)

    @pl.when(i == 0)
    def _():
        first[...] = result

    @pl.when(i == 1)
    def _():
        second[...] = result


def split_product(info, inner, down, hidden, send_in, sends, keep):
    result = dot(inner[...], down[...])
    i = pl.program_id(0)

    @pl.when(i == 0)
    def _():
        sends[0] = send_in[...]
        sends[1] = result.astype(bf16)

    @pl.when(i == 1)
    def _():
        keep[...] = result + hidden[...]


def back_in(info, du, grads, w, send, keep):
    half = du.shape[1]
    i = pl.program_id(0)
    result = dot_t(du[...], w[3])
    for j in range(3):
        result = result + dot_t(grads[:, pl.ds(j * half, half)], w[j])
    result = result.astype(bf16)

    @pl.when(i == 0)
    def _():
        send[...] = result

    @pl.when(i == 1)
    def _():
        keep[...] = result


def back_mix(rows, block, heads, dim, info, own_0, own_1, other_0, other_1, hidden, g, att_own, att_other, u_own, u_other, wo_own, wo_other, q, rate, dh, branch, dgates, datt, direct, local, dm_own, dm_other, es):
    i = pl.program_id(0)
    b = jnp.where(i == 0, 1 - info[0], info[0])
    half = att_own.shape[1]
    width = 2 * half

    def hid(r, _):
        x = hidden[r, :]
        scale = scale_of(row_sum(x * x), width)
        dn = jnp.where(
            b == 0,
            own_0[r, :].astype(f32) + other_0[r, :].astype(f32),
            own_1[r, :].astype(f32) + other_1[r, :].astype(f32),
        )
        mean = row_sum(x * dn) / width
        d = g[r, :].astype(f32) + scale * dn - x * (scale * scale * scale * mean)
        dh[r, :] = d
        branch[r, :] = d.astype(bf16)

    loop(rows, 16, hid)
    dm_own[...] = dot_t(branch[...], wo_own[...])
    dm_other[...] = dot_t(branch[...], wo_other[...])

    def att(r, start):
        a, b = att_own[r, :].astype(f32), att_other[r, :].astype(f32)
        scale = scale_of(row_sum(a * a) + row_sum(b * b), width)
        m = dm_own[r, :]
        dgates[r, :] = (m * (a * scale)).astype(bf16)
        da = m * u_own[r, :].astype(f32)
        db = dm_other[r, :] * u_other[r, :].astype(f32)
        mean = (row_sum(a * da) + row_sum(b * db)) / width
        d = (scale * da - a * (scale * scale * scale * mean)).astype(bf16)
        datt[r, :] = d
        place = row_numbers(start + 1, 16, dim)
        for h in range(heads):
            dd = d[:, h * dim : (h + 1) * dim].astype(f32)
            es[r, head(h, dim)] = (dd * jnp.exp(-rate[h] * place)).astype(bf16)

    loop(rows, 16, att)
    for h in range(heads):
        c = head(h, dim)
        direct[b, h] = t_dot(q[:, c], es[:, c])

    @pl.when(i == 1)
    def _():
        for h in range(heads):
            carried = jnp.exp(wide(-rate[h] * block, dim))
            local[h] = (direct[0, h] + carried * direct[1, h]).astype(bf16)


def attend_back(block, heads, dim, info, q, k, v, datt, states, pq, cs, sn, rate, gq, dk, dv):
    for h in range(heads):
        c = head(h, dim)
        state = states[0, h]
        fall = fall_of(rate[h])
        for start in reversed(range(0, block, CHUNK)):
            r, upto = pl.ds(start, CHUNK), start + CHUNK
            decay = decay_of(rate[h], start, fall)
            qc, da = q[r, c], datt[r, c]
            weights = (dot_t(qc, k[:upto, c]) * decay).astype(bf16)
            dscore = (dot_t(da, v[:upto, c]) * decay).astype(bf16)
            entering = jnp.exp(-rate[h] * (row_numbers(start, CHUNK, dim) + 1.0))
            e = (da.astype(f32) * entering).astype(bf16)
            dq = dot(dscore, k[:upto, c]) + dot_t(e, state)
            slope = swish_slope(pq[r, c].astype(f32))
            gq[r, c] = (slope * rotate(dq, cs[r, :], -sn[r, :])).astype(bf16)
            dk_term, dv_term = t_dot(dscore, qc), t_dot(weights, da)
            if upto == block:
                dk[:, c] = dk_term
                dv[:, c] = dv_term
            else:
                dk[:upto, c] = dk[:upto, c] + dk_term
                dv[:upto, c] = dv[:upto, c] + dv_term


def finish_back(block, heads, dim, count, info, k, v, dk, dv, direct, pk, pv, cs, sn, rate, gq, near, far, out, after):
    b = pl.program_id(0)
    half = heads * dim
    out[:, :half] = gq[...]
    for h in range(heads):
        c = head(h, dim)
        last = state_sum(near, far, count, h, rate, 2 * block, dim, info[4], True)
        before = jnp.exp(wide(-rate[h] * block, dim)) * last + direct[1, h]
        after[...] = jnp.where(b == 1, last, before).astype(bf16)
        for start in range(0, block, CHUNK):
            r = pl.ds(start, CHUNK)
            leaving = jnp.exp(-rate[h] * (block - 1.0 - row_numbers(start, CHUNK, dim)))
            kd = (k[r, c].astype(f32) * leaving).astype(bf16)
            key_grad = dk[r, c] + leaving * dot_t(v[r, c], after[...])
            value_grad = dv[r, c] + dot(kd, after[...])
            gk = swish_slope(pk[r, c].astype(f32)) * rotate(key_grad, cs[r, :], -sn[r, :])
            out[r, pl.ds(half + h * dim, dim)] = gk.astype(bf16)
            out[r, pl.ds(2 * half + h * dim, dim)] = (
                swish_slope(pv[r, c].astype(f32)) * value_grad
            ).astype(bf16)


def add_kernel(info, *refs):
    *terms, out = refs

    def body(r, _):
        total = terms[0][r, :].astype(f32)
        for term in terms[1:]:
            total = total + term[r, :].astype(f32)
        out[r, :] = total.astype(bf16)

    loop(out.shape[0], 16, body)


def join_kernel(info, *refs):
    out = refs[6]
    cut = refs[0].shape[1]
    add_kernel(info, *refs[:3], out.at[:, pl.ds(0, cut)])
    add_kernel(info, *refs[3:6], out.at[:, pl.ds(cut, out.shape[1] - cut)])


def choose_kernel(info, mine, arrived, out):
    place = info[4]
    inner = (place == 1) | (place == 2)

    def body(r, _):
        value = jnp.where(inner, mine[r, :].astype(f32), arrived[r, :].astype(f32))
        out[r, :] = value.astype(bf16)

    loop(out.shape[0], 16, body)


def choose(info, pieces, use):
    step = pl.program_id(0)
    first = (step // 2) != info[1]
    second = lax.rem(step, 2) != info[2]
    for index, piece in enumerate(pieces):
        at_first, at_second = index >= 2, index % 2 == 1

        @pl.when((first == at_first) & (second == at_second))
        def _(piece=piece):
            use(piece)


def place_whole(info, *refs):
    pieces, out = refs[:4], refs[4]

    def put(piece):
        out[...] = piece[...].astype(f32)

    choose(info, pieces, put)


def place_turned(info, *refs):
    pieces, out = refs[:4], refs[4]

    def put(piece):
        out[...] = piece[...].astype(f32).T

    choose(info, pieces, put)


def place_heads(info, *refs):
    qkv, others, out = refs[:4], refs[4:8], refs[8]
    width = out.shape[2]
    last = qkv[0].shape[1] - 2 * width

    def put_qkv(piece):
        for j in range(2):
            out[:, j, :] = piece[:, pl.ds(j * width, width)].astype(f32)
        out[:, 2, :last] = piece[:, 2 * width :].astype(f32)

    def put_others(piece):
        out[:, 3, :] = piece[:, :width].astype(f32)
        out[:, 2, last:] = piece[:, 2 * width :].astype(f32)

    choose(info, qkv, put_qkv)
    choose(info, others, put_others)


def place_rows(info, *refs):
    pieces, out = refs[:4], refs[4]
    rows, width = out.shape[0], out.shape[1] // 2

    def put(piece):
        out[:, :width] = piece[:rows, width : 2 * width].astype(f32)
        out[:, width:] = piece[rows:, width : 2 * width].astype(f32)

    choose(info, pieces, put)


def swap(value, axis, bit):
    return lax.ppermute(value, axis, [(i, i ^ bit) for i in range(lax.axis_size(axis))])


def shift(value, axis, distance):
    count = lax.axis_size(axis)
    return lax.ppermute(
        value, axis, [(i, i + distance) for i in range(count) if 0 <= i + distance < count]
    )


def cross(value, turn):
    pairs = []
    for place in range(lax.axis_size("dp")):
        for core in range(2):
            pairs.append((2 * place + core, 2 * (place ^ (1 << (core ^ turn))) + core))
    return lax.ppermute(value, ("dp", "heads"), pairs)


def part(value, index, rows, axis=0):
    return lax.dynamic_slice_in_dim(value, index * rows, rows, axis)


def add(*terms):
    total = terms[0].astype(f32)
    for term in terms[1:]:
        total = total + term.astype(f32)
    return total.astype(bf16)


class States:
    def __init__(self, spine, local, rate, rows, backward):
        self.spine, self.local, self.rate = spine, local, rate
        self.rows, self.backward = rows, backward
        self.count = lax.axis_size("seq")
        if self.count == 4:
            self.near = swap(local, "seq", 1)

    def second(self):
        if self.count == 4:
            (self.near,) = self.spine.wait(self.near)
            here = View(lambda ref, i, s: ref)
            heads, dim = self.local.shape[:2]
            body = functools.partial(pair_states, heads=heads, dim=dim, rows=self.rows, backward=self.backward, count=4)

            def kernel(info, own, near, rate, out):
                body(info, own=own, near=near, rate=rate, out=out)

            ins = [(self.local, here), (self.near, here), (self.rate, SMEM)]
            outs = [(self.local.shape, bf16, here)]
            self.far = swap(self.spine.call(kernel, 1, ins, outs, name="pair_states")[0], "seq", 2)

    def all(self):
        if self.count == 4:
            (far,) = self.spine.wait(self.far)
            return self.near, far
        sign = -1 if self.backward else 1
        total = shift(self.local.astype(f32), "seq", sign)
        distance = 1
        while distance < self.count - 1:
            power = jnp.exp(-self.rate * self.rows * distance)[:, None, None]
            total = total + power * shift(total, "seq", sign * distance)
            distance *= 2
        return total, total


class Sum:
    last = None

    def __init__(self, spine, send, keep=None, there=None):
        self.spine, self.keep, self.cut = spine, keep, there is not None
        self.first = cross(send, 0)
        self.second_part = cross(there, 0) if self.cut else None
        self.shape = send.shape[0] if self.cut else send.shape[0] // 2, send.shape[1]
        self.four = lax.axis_size("seq") == 4

    def combine(self, body, *terms):
        rows = self.shape[0]

        def view(turn):
            if turn is None:
                return View(lambda ref, i, s: ref)
            return View(lambda ref, i, s: ref.at[span(1 - s[2] if turn else s[2], rows), :])

        ins = [(value, view(turn)) for value, turn in terms]
        outs = [(self.shape, bf16, view(None))]
        return self.spine.call(body, 1, ins, outs, name="combine")[0]

    def second(self):
        (self.first,) = self.spine.wait(self.first)
        turn = None if self.cut else True
        self.across = cross(self.combine(add_kernel, (self.keep, True), (self.first, turn)), 1)

    def last_second(self):
        self.last.second()

    def last_wait(self):
        (self.last.across,) = self.spine.wait(self.last.across)

    def line(self):
        if self.cut:
            across, first = self.spine.wait(self.across, self.second_part)
            first = first, None
        else:
            (across,) = self.spine.wait(self.across)
            first = self.first, False
        terms = [(self.keep, False), first, (across, None)]
        if self.last is None:
            self.value = self.combine(add_kernel, *terms)
        else:
            last = self.last
            terms += [(last.keep, False), (last.first, False), (last.across, None)]
            self.shape = self.shape[0], self.shape[1] + self.last.shape[1]
            self.value = self.combine(join_kernel, *terms)
        if self.four:
            self.inward = lax.ppermute(self.value, "seq", [(0, 1), (3, 2)])

    def line_across(self):
        if self.four:
            (inward,) = self.spine.wait(self.inward)
            self.value = self.combine(add_kernel, (self.value, None), (inward, None))
            self.middle = lax.ppermute(self.value, "seq", [(1, 2), (2, 1)])

    def line_back(self):
        if self.four:
            (middle,) = self.spine.wait(self.middle)
            self.value = self.combine(add_kernel, (self.value, None), (middle, None))
            self.outer = lax.ppermute(self.value, "seq", [(1, 0), (2, 3)])

    def spread(self):
        if self.four:
            (outer,) = self.spine.wait(self.outer)
            total = self.combine(choose_kernel, (self.value, None), (outer, None))
        else:
            total = lax.psum(self.value.astype(f32), "seq").astype(bf16)
            self.spine.after(total)
        self.value, self.second_half, self.own_first = total, cross(total, 1), cross(total, 0)

    def spread_on(self):
        (second,) = self.spine.wait(self.second_half)
        self.pieces = [self.value, second, self.own_first, cross(second, 0)]

    def arrive(self):
        self.pieces[2:] = self.spine.wait(*self.pieces[2:])
        return self.pieces


def shards(
    tokens,
    cotangent,
    qkvu_weight,
    out_weight,
    up_weight,
    gate_weight,
    down_weight,
    decay_rate,
    item_length,
    item_slot,
):
    core = lax.axis_index("heads")
    seq_place = lax.axis_index("seq")
    data_place = lax.axis_index("dp")
    block, width = tokens.shape[1:]
    heads = decay_rate.shape[0]
    half = qkvu_weight.shape[2]
    dim = half // heads
    ff = up_weight.shape[1] // 2
    rows = 2 * block
    tile = block // 2
    rate = (decay_rate, SMEM)

    own, own_cot = tokens[0], cotangent[0]
    other = swap(own, "heads", 1)
    other_cot = swap(own_cot, "heads", 1)
    other_out = swap(out_weight, "heads", 1)
    weights = jnp.transpose(qkvu_weight, (1, 0, 2))
    fine = 32
    lanes = jnp.arange(dim)
    frequency = 10000.0 ** (-(lanes % (dim // 2)).astype(f32) / (dim // 2))
    coarse_steps = seq_place * rows + fine * jnp.arange(rows // fine)
    steps = jnp.concatenate([coarse_steps, jnp.arange(fine)]).astype(f32)
    angles = steps[:, None] * frequency[None, :]
    cosine, sine = lax.optimization_barrier((jnp.cos(angles), jnp.sin(angles)))
    c_far, s_far = cosine[:-fine, None, :], sine[:-fine, None, :]
    c_near, s_near = cosine[None, -fine:, :], sine[None, -fine:, :]
    sign = jnp.where(lanes < dim // 2, -1.0, 1.0)
    cs = (c_far * c_near - s_far * s_near).reshape(rows, dim)
    sn = (sign * (s_far * c_near + c_far * s_near)).reshape(rows, dim)

    def weight(j):
        return weights, View(lambda ref, i, s: ref.at[pl.ds(j, 1)])

    def by(value, size):
        return value, View(lambda ref, i, s: ref.at[span(i, size), :])

    def all_of(value):
        return value, View(lambda ref, i, s: ref)

    def out(columns, kind, size):
        return (rows, columns), kind, View(lambda ref, i, s: ref.at[span(i, size), :])

    def fixed(shape, kind):
        return shape, kind, View(lambda ref, i, s: ref)

    def fn(body, *sizes):
        return functools.partial(body, *sizes)

    down_half = down_weight, View(lambda ref, i, s: ref.at[span(s[0], ff), :])
    columns = View(lambda ref, i, s: ref.at[:, span(s[0], ff)])
    up_half, gate_half = (up_weight, columns), (gate_weight, columns)
    spine = Spine()
    call = spine.call
    square = (heads, dim, dim)
    big, low = pltpu.VMEM((block, half), f32), pltpu.VMEM((block, half), bf16)

    def turned(columns):
        return (columns, rows), bf16, View(lambda ref, i, s: ref.at[:, span(i, block)])

    normed, normed_t, k, v, pk, pv, contrib, local = call(
        fn(project_kv, block, heads, dim),
        2,
        [all_of(own), all_of(other), weight(1), weight(2), by(cs, block), by(sn, block)]
        + [rate],
        [out(width, bf16, block), turned(width)]
        + [out(half, bf16, block)] * 4
        + [fixed((2,) + square, f32), fixed(square, bf16)],
        [big, big, low],
        name="project_kv",
    )
    line = States(spine, local, decay_rate, rows, False)
    g, g_t, grad_inner, valid = call(
        fn(begin_back, block),
        2,
        [all_of(own_cot), all_of(other_cot), down_half]
        + [(item_slot, SMEM), (item_length, SMEM)],
        [out(width, bf16, block), turned(width), out(ff, bf16, block), out(dim, f32, block)],
        name="begin_back",
    )
    line.second()
    q, pq, u_own, intra = call(
        fn(project_qu, block, heads, dim),
        2,
        [by(normed, block), weight(0), weight(3), by(cs, block), by(sn, block), rate]
        + [by(k, block), by(v, block)],
        [out(half, bf16, block)] * 3 + [out(half, f32, block)],
        [big],
        name="project_qu",
    )
    u_other = swap(u_own, "heads", 1)
    near, far = line.all()
    att_own, states = call(
        fn(attend, block, heads, dim, line.count),
        1,
        [all_of(q), all_of(intra), all_of(contrib), rate, all_of(near), all_of(far)],
        [fixed((rows, half), bf16), fixed((2,) + square, bf16)],
        name="attend",
    )
    att_other = swap(att_own, "heads", 1)
    att_u = [by(att_own, block), by(att_other, block), by(u_own, block), by(u_other, block)]
    out_both = [all_of(out_weight), all_of(other_out)]
    hidden, n2, mixed = call(
        fn(mix_out, block),
        2,
        att_u + out_both + [all_of(own), all_of(other)],
        [out(width, f32, block), out(width, bf16, block), out(half, bf16, block)],
        [pltpu.VMEM((block, width), bf16)],
        name="mix_out",
    )
    inner, grad_left, grad_right = call(
        fn(feed, block),
        2,
        [by(n2, block), up_half, gate_half, by(grad_inner, block)],
        [out(ff, bf16, block)] * 3,
        [pltpu.VMEM((block, ff), f32)] * 2,
        name="feed",
    )

    def halves(value):
        size = value.shape[0] // 2

        def at(ref, i, s):
            return ref.at[span(jnp.where(i == 0, 1 - s[1], s[1]), size), :]

        return value, View(at)

    def grad(name, lhs, rhs):
        shape = lhs.shape[0] // 2, rhs.shape[1]
        return call(
            weight_grad, 2, [halves(lhs), all_of(rhs)], [fixed(shape, bf16)] * 2, name=name
        )

    def sides(value):
        def at(ref, i, s):
            return ref.at[span(jnp.where(i == 0, 1 - s[0], s[0]), block), :]

        return value, View(at)

    two_sides = [fixed((block, width), bf16)] * 2

    def half_grad(name, lhs, rhs, send):
        size = lhs.shape[0] // 2

        def at(ref, i, s):
            return ref.at[span(1 - s[1] if send else s[1], size), :]

        shape = size, rhs.shape[1]
        ins = [(lhs, View(at)), all_of(rhs)]
        return call(weight_half, 1, ins, [fixed(shape, bf16)], name=name)[0]

    down = Sum(spine, half_grad("down_send", g_t, inner, True))
    *partial, n2_t, mixed_t = call(
        back_two,
        2,
        [by(grad_left, block), by(grad_right, block), up_half, gate_half]
        + [by(n2, block), by(mixed, block)],
        two_sides + [turned(width), turned(half)],
        name="back_two",
    )
    partial_other = [swap(value, "heads", 1) for value in partial]
    up = Sum(spine, *grad("up_grad", n2_t, grad_left))
    gate = Sum(spine, *grad("gate_grad", n2_t, grad_right))
    down.keep = half_grad("down_keep", g_t, inner, False)
    partial_other = spine.wait(*partial_other)
    down.second()
    dh, branch, dgates, datt, direct, local = call(
        fn(back_mix, block, block, heads, dim),
        2,
        [all_of(x) for x in (*partial, *partial_other)]
        + [sides(x) for x in (hidden, g, att_own, att_other, u_own, u_other)]
        + out_both
        + [sides(q), rate],
        [fixed((block, width), f32)]
        + [((rows, size), bf16, sides(None)[1]) for size in (width, half, half)]
        + [fixed((2,) + square, f32), fixed(square, bf16)],
        [pltpu.VMEM((block, half), f32)] * 2 + [pltpu.VMEM((block, half), bf16)],
        name="back_mix",
    )
    flat = pl.BlockSpec((width // 4, ff), lambda i: (i, 0))

    def place(body, pieces, shape, spec, name):
        return call(
            body, 4, [(p, whole(p)) for p in pieces], [(shape, f32, spec)], name=name
        )[0]
    line = States(spine, local, decay_rate, rows, True)
    out_u = call(
        out_u_grad,
        2,
        [halves(mixed_t), all_of(branch), halves(normed_t), all_of(dgates)],
        [fixed((block, width), bf16)] * 2,
        name="out_u_grad",
    )
    out_u = Sum(spine, *out_u)
    line.second()
    up.second()
    down.line()
    gq, dk, dv = call(
        fn(attend_back, block, heads, dim),
        2,
        [by(q, block), by(k, block), by(v, block), by(datt, block)]
        + [(states, View(lambda ref, i, s: ref.at[pl.ds(i, 1)])), by(pq, block)]
        + [by(cs, block), by(sn, block), rate],
        [out(half, bf16, block), out(half, f32, block), out(half, f32, block)],
        name="attend_back",
    )
    near, far = line.all()
    down.line_across()
    up.line()
    grads = call(
        fn(finish_back, block, heads, dim, line.count),
        2,
        [by(k, block), by(v, block), by(dk, block), by(dv, block), all_of(direct)]
        + [by(pk, block), by(pv, block), by(cs, block), by(sn, block), rate]
        + [by(gq, block), all_of(near), all_of(far)],
        [out(3 * half, bf16, block)],
        [pltpu.VMEM((dim, dim), bf16)],
        name="finish_back",
    )[0]
    flat = pl.BlockSpec((width // 4, ff), lambda i: (i, 0))

    def place(body, pieces, shape, spec, name):
        return call(
            body, 4, [(p, whole(p)) for p in pieces], [(shape, f32, spec)], name=name
        )[0]

    quarter = rows // 4
    on, there, keep, last_send, last_keep = call(
        weight_grad_cut,
        2,
        [halves(normed_t), all_of(grads)],
        [fixed((quarter, ff), bf16)] * 2
        + [fixed((block, ff), bf16)]
        + [fixed((block, 3 * half - ff), bf16)] * 2,
        name="qkv_grad",
    )
    qkv = Sum(spine, on, keep, there)
    out_u.last = Sum(spine, last_send, last_keep)
    gate.second()
    send_in, keep_in = call(
        back_in,
        2,
        [sides(dgates), sides(grads), all_of(weights)],
        two_sides,
        name="back_in",
    )
    out_u.second()
    down.line_back()
    up.line_across()
    sends, keep_out = call(
        split_product,
        2,
        [sides(inner), down_half, sides(hidden), all_of(send_in)],
        [fixed((2, block, width), bf16), fixed((block, width), f32)],
        name="split_product",
    )
    gate.line()
    qkv.second()
    down.spread()
    up.line_back()
    qkv.line()
    gate.line_across()
    out_u.last_second()
    down.spread_on()
    up.spread()
    qkv.line_across()
    gate.line_back()
    out_u.last_wait()
    out_u.line()
    down_grad = place(
        place_turned,
        down.arrive(),
        (ff, width),
        pl.BlockSpec((ff, width // 4), lambda i: (0, i)),
        "place_down",
    )
    (sends,) = spine.wait(sends)
    arrived_both = [swap(sends[n], "heads", 1) for n in range(2)]
    up.spread_on()
    qkv.line_back()
    gate.spread()
    out_u.line_across()
    up_grad = place(place_whole, up.arrive(), (width, ff), flat, "place_up")
    gate.spread_on()
    qkv.spread()
    out_u.line_back()
    qkv.spread_on()
    out_u.spread()
    gate_grad = place(place_whole, gate.arrive(), (width, ff), flat, "place_gate")
    out_u.spread_on()
    arrived_in, arrived_out = spine.wait(*arrived_both)
    def own_rows(value):
        return part(value, core, block)

    def add_wide(a, b):
        return a.astype(f32) + b.astype(f32)

    output = add_wide(keep_out, arrived_out)
    output = (output * own_rows(valid)[:, :1]).astype(bf16)
    x = own.astype(f32)
    scale = lax.rsqrt(jnp.mean(x * x, axis=-1, keepdims=True) + epsilon)
    dn = add_wide(keep_in, arrived_in)
    grad_inputs = (
        dh
        + scale * dn
        - x * (scale * scale * scale) * jnp.mean(x * dn, axis=-1, keepdims=True)
    )
    spine.after(output, grad_inputs)
    out_u_pieces = out_u.arrive()
    out_grad = place(
        place_rows,
        out_u_pieces,
        (half, width),
        pl.BlockSpec((half // 4, width), lambda i: (i, 0)),
        "place_out",
    )
    qkvu_grad = place(
        place_heads,
        qkv.arrive() + out_u_pieces,
        (width, 4, half),
        pl.BlockSpec((width // 4, 4, half), lambda i: (i, 0, 0)),
        "place_qkvu",
    )
    return output[None], grad_inputs[None], qkvu_grad, out_grad, up_grad, gate_grad, down_grad


def solution(mesh):
    placed = (
        P("dp", ("seq", "heads"), None),
        P("dp", ("seq", "heads"), None),
        P(None, None, "heads"),
        P("heads", None),
        P(),
        P(),
        P(),
        P("heads"),
        P(),
        P(),
    )
    return jax.shard_map(
        shards,
        mesh=mesh,
        in_specs=placed,
        out_specs=(
            P("dp", ("seq", "heads"), None),
            P("dp", ("seq", "heads"), None),
            P(None, None, "heads"),
            P("heads", None),
            P(None, "heads"),
            P(None, "heads"),
            P("heads", None),
        ),
        check_vma=False,
    )
```

```python
import functools
import math

import jax
import jax.numpy as jnp
from jax import lax
from jax.experimental import pallas as pl
from jax.experimental.pallas import tpu as pltpu
from jax.sharding import PartitionSpec as P

epsilon = 1e-06
f32 = jnp.float32
bf16 = jnp.bfloat16
CHUNK = 512


def dot(a, b):
    return jnp.dot(a, b, preferred_element_type=f32)


def dot_t(a, b):
    return lax.dot_general(a, b, (((1,), (1,)), ((), ())), preferred_element_type=f32)


def t_dot(a, b):
    return lax.dot_general(a, b, (((0,), (0,)), ((), ())), preferred_element_type=f32)


def whole(value):
    rank = value.ndim
    return pl.BlockSpec(value.shape, lambda i: (0,) * rank, pipeline_mode=pl.Buffered(1))


class View:
    block_shape = None

    def __init__(self, at):
        self.at = at


class Places:
    def __getitem__(self, index):
        core, data = lax.axis_index("heads"), lax.axis_index("dp")
        low, high = lax.rem(data, 2), data // 2
        if index == 0:
            return core
        if index == 1:
            return jnp.where(core == 0, low, high)
        if index == 2:
            return jnp.where(core == 0, high, low)
        return data if index == 3 else lax.axis_index("seq")


def span(index, size):
    return pl.ds(pl.multiple_of(index * size, size), size)


def spec_of(spec):
    return pl.BlockSpec(memory_space=pltpu.VMEM) if isinstance(spec, View) else spec


def room(blocks, scratch, name):
    total = 0
    for spec, kind in blocks:
        if spec.block_shape is not None:
            buffers = 1 if spec.pipeline_mode is not None else 2
            total += buffers * math.prod(spec.block_shape) * jnp.dtype(kind).itemsize
    for buffer in scratch:
        if buffer.dtype in (f32, bf16):
            total += math.prod(buffer.shape) * jnp.dtype(buffer.dtype).itemsize
    return total + SLACK.get(name, 4) * 2**20


SLACK = {"begin_back": 5, "attend_back": 5, "split_product": 6, "back_two": 8}


def tiles(value, rows):
    return pl.BlockSpec((rows, value.shape[1]), lambda i: (i, 0))


SMEM = pl.BlockSpec(memory_space=pltpu.SMEM)


class Spine:
    def __init__(self):
        self.token = None
        self.done = []

    def call(self, body, steps, ins, outs, scratch=(), name=None):
        after = self.done + ([] if self.token is None else [self.token])
        used, given = len(ins), len(outs)
        specs = [spec for _, spec in ins] + [spec for _, _, spec in outs]
        blocks = [(spec, value.dtype) for value, spec in ins]
        blocks += [(spec, kind) for _, kind, spec in outs]

        def kernel(*refs):
            rest = refs[used + len(after) :]
            rest[given][...] = jnp.zeros((8, 128), f32)
            step, places = pl.program_id(0), Places()
            given_refs = [
                spec.at(ref, step, places) if isinstance(spec, View) else ref
                for spec, ref in zip(specs, list(refs[:used]) + list(rest[:given]))
            ]
            body(places, *given_refs, *rest[given + 1 :])

        results = pl.pallas_call(
            kernel,
            grid=(steps,),
            in_specs=[spec_of(spec) for _, spec in ins]
            + [pl.BlockSpec(memory_space=pl.ANY)] * len(after),
            out_specs=[spec_of(spec) for _, _, spec in outs]
            + [pl.BlockSpec(memory_space=pltpu.VMEM)],
            scratch_shapes=list(scratch),
            out_shape=[jax.ShapeDtypeStruct(shape, kind) for shape, kind, _ in outs]
            + [jax.ShapeDtypeStruct((8, 128), f32)],
            compiler_params=pltpu.CompilerParams(vmem_limit_bytes=room(blocks, scratch, name)),
            cost_estimate=pl.CostEstimate(flops=0, bytes_accessed=0, transcendentals=0),
            name=name,
        )(*[value for value, _ in ins], *after)
        self.token, self.done = results[-1], []
        return results[:-1]

    def after(self, *values):
        self.done += values

    def wait(self, *values):
        if self.done:
            token = self.token
            for value in self.done:
                token = token + value[:8, :128].astype(f32)
            self.token, self.done = token, []
        results = lax.optimization_barrier((self.token,) + values)
        self.token = results[0]
        return results[1:]


def loop(count, step, body, unroll=True):
    def turn(i, _):
        body(pl.ds(pl.multiple_of(i * step, step), step), i * step)
        return 0

    lax.fori_loop(0, count // step, turn, 0, unroll=unroll)


def head(h, dim):
    return pl.ds(h * dim, dim)


def rotate(value, cosine, sine):
    return value * cosine + pltpu.roll(value, value.shape[1] // 2, 1) * sine


def sigmoid(value):
    return 0.5 * jnp.tanh(0.5 * value) + 0.5


def swish(value):
    return value * sigmoid(value)


def swish_slope(value):
    s = sigmoid(value)
    y = value * s
    return y + s * (1.0 - y)


def row_numbers(start, rows, columns):
    return (lax.broadcasted_iota(jnp.int32, (rows, columns), 0) + start).astype(f32)


def fall_of(rate):
    return jnp.exp(-rate * row_numbers(0, CHUNK, CHUNK))


def decay_of(rate, start, fall):
    upto = start + CHUNK
    columns = lax.broadcasted_iota(jnp.int32, (1, upto), 1).astype(f32)
    rise = jnp.exp(rate * (columns - float(start)))
    tiles = [rise[:, j : j + CHUNK] * fall for j in range(0, upto, CHUNK)]
    rows = lax.broadcasted_iota(jnp.int32, (CHUNK, CHUNK), 0)
    inside = rows >= lax.broadcasted_iota(jnp.int32, (CHUNK, CHUNK), 1)
    tiles[-1] = jnp.where(inside, tiles[-1], 0.0)
    return jnp.concatenate(tiles, 1) if start else tiles[0]


def scale_of(total, width):
    return lax.rsqrt(total / width + epsilon)


def row_sum(value):
    return jnp.sum(value, axis=-1, keepdims=True)


def wide(scalar, dim):
    return jnp.full((1, dim), scalar, f32)


def project_kv(block, heads, dim, info, own, other, wk, wv, cs, sn, rate, normed, k, v, pk, pv, contrib, local, sk, sv, kd):
    b = pl.program_id(0)
    mine = b == info[0]
    width = own.shape[1]

    def norm(r, _):
        x = jnp.where(mine, own[r, :].astype(f32), other[r, :].astype(f32))
        normed[r, :] = (x * scale_of(row_sum(x * x), width)).astype(bf16)

    loop(block, 16, norm)
    sk[...] = dot(normed[...], wk[0])
    sv[...] = dot(normed[...], wv[0])

    def act(r, start):
        cosine, sine = cs[r, :], sn[r, :]
        steps = block - 1.0 - row_numbers(start, 64, dim)
        for h in range(heads):
            c = head(h, dim)
            p = sk[r, c]
            pk[r, c] = p.astype(bf16)
            key = rotate(swish(p), cosine, sine).astype(bf16)
            k[r, c] = key
            kd[r, c] = (key.astype(f32) * jnp.exp(-rate[h] * steps)).astype(bf16)
            p = sv[r, c]
            pv[r, c] = p.astype(bf16)
            v[r, c] = swish(p).astype(bf16)

    loop(block, 64, act)
    for h in range(heads):
        c = head(h, dim)
        contrib[b, h] = t_dot(kd[:, c], v[:, c])

    @pl.when(b == 1)
    def _():
        for h in range(heads):
            carried = jnp.exp(wide(-rate[h] * block, dim))
            local[h] = (carried * contrib[0, h] + contrib[1, h]).astype(bf16)


def project_qu(block, heads, dim, info, normed, wq, wu, cs, sn, rate, k, v, q, pq, u, intra, sq):
    sq[...] = dot(normed[...], wq[0])
    u[...] = dot(normed[...], wu[0]).astype(bf16)

    def act(r, start):
        cosine, sine = cs[r, :], sn[r, :]
        for h in range(heads):
            c = head(h, dim)
            p = sq[r, c]
            pq[r, c] = p.astype(bf16)
            q[r, c] = rotate(swish(p), cosine, sine).astype(bf16)

    loop(block, 64, act)
    for h in range(heads):
        c = head(h, dim)
        fall = fall_of(rate[h])
        for start in range(0, block, CHUNK):
            r, upto = pl.ds(start, CHUNK), start + CHUNK
            scores = dot_t(q[r, c], k[:upto, c]) * decay_of(rate[h], start, fall)
            intra[r, c] = dot(scores.astype(bf16), v[:upto, c])


def pair_states(info, count, heads, dim, rows, backward, own, near, rate, out):
    even = lax.rem(info[4], 2) == 0
    for h in range(heads):
        decay = jnp.exp(wide(-rate[h] * rows, dim))
        a, b = own[h].astype(f32), near[h].astype(f32)
        plain, decayed = (a, b) if backward else (b, a)
        other = (b, a) if backward else (a, b)
        out[h] = jnp.where(even, plain + decay * decayed, other[0] + decay * other[1]).astype(bf16)


def state_sum(near, far, count, h, rate, rows, dim, place, backward):
    if count != 4:
        return near[h]
    side = lax.rem(place, 2) == (0 if backward else 1)
    pair = place < 2 if backward else place >= 2
    decay = jnp.where(side, jnp.exp(wide(-rate[h] * rows, dim)), 1.0)
    first = jnp.where(side, near[h].astype(f32), 0.0)
    return first + jnp.where(pair, decay * far[h].astype(f32), 0.0)


def attend(block, heads, dim, count, info, q, intra, contrib, rate, near, far, att, states):
    for h in range(heads):
        c = head(h, dim)
        first = state_sum(near, far, count, h, rate, 2 * block, dim, info[4], False)
        second = jnp.exp(wide(-rate[h] * block, dim)) * first + contrib[0, h]
        for b, state in enumerate((first, second)):
            states[b, h] = state.astype(bf16)
        for b in range(2):
            state = states[b, h]
            for start in range(0, block, CHUNK):
                r = pl.ds(b * block + start, CHUNK)
                entering = jnp.exp(-rate[h] * (row_numbers(start, CHUNK, dim) + 1.0))
                att[r, c] = (intra[r, c] + entering * dot(q[r, c], state)).astype(bf16)


def begin_back(rows, info, own, other, down, item_slot, item_length, g, turned, grad_inner, valid):
    i = pl.program_id(0)
    mine = i == info[0]
    limit = item_length[item_slot[info[3]]] - (2 * info[4] + i) * rows

    def read(r, start):
        value = jnp.where(mine, own[r, :].astype(f32), other[r, :].astype(f32))
        inside = lax.broadcasted_iota(jnp.int32, value.shape, 0) + start < limit
        g[r, :] = jnp.where(inside, value, 0.0).astype(bf16)

    loop(rows, 16, read)
    valid[...] = (lax.broadcasted_iota(jnp.int32, valid.shape, 0) < limit).astype(f32)
    grad_inner[...] = dot_t(g[...], down[...]).astype(bf16)
    turned[...] = g[...].T


def mix_out(rows, info, att_own, att_other, u_own, u_other, wo_own, wo_other, own, other, hidden, n2, mixed, both):
    mine = pl.program_id(0) == info[0]
    half = att_own.shape[1]
    width = 2 * half

    def mix(r, _):
        a, b = att_own[r, :].astype(f32), att_other[r, :].astype(f32)
        scale = scale_of(row_sum(a * a) + row_sum(b * b), width)
        both[r, :half] = (a * scale * u_own[r, :].astype(f32)).astype(bf16)
        both[r, half:] = (b * scale * u_other[r, :].astype(f32)).astype(bf16)

    loop(rows, 16, mix)
    hidden[...] = dot(both[:, :half], wo_own[...]) + dot(both[:, half:], wo_other[...])
    mixed[...] = both[:, :half]

    def norm(r, _):
        x = jnp.where(mine, own[r, :].astype(f32), other[r, :].astype(f32))
        x = hidden[r, :] + x
        hidden[r, :] = x
        n2[r, :] = (x * scale_of(row_sum(x * x), width)).astype(bf16)

    loop(rows, 16, norm)


def feed(rows, info, n2, up, gate, grad_inner, inner, grad_left, grad_right, left, right):
    left[...] = dot(n2[...], up[...])
    right[...] = dot(n2[...], gate[...])

    def join(r, _):
        a, b, g = left[r, :], right[r, :], grad_inner[r, :].astype(f32)
        inner[r, :] = (a * b).astype(bf16)
        grad_left[r, :] = (g * b).astype(bf16)
        grad_right[r, :] = (g * a).astype(bf16)

    loop(rows, 16, join)


def weight_half(info, lhs, rhs, out):
    out[...] = dot(lhs[...], rhs[...]).astype(bf16)


def weight_grad(info, lhs, rhs, send, keep):
    step = pl.program_id(0)

    @pl.when(step == 0)
    def _():
        send[...] = dot(lhs[...], rhs[...]).astype(bf16)

    @pl.when(step == 1)
    def _():
        keep[...] = dot(lhs[...], rhs[...]).astype(bf16)


def weight_grad_cut(info, lhs, rhs, on, there, keep, last_send, last_keep):
    step = pl.program_id(0)
    columns, rows = keep.shape[1], on.shape[0]

    @pl.when(step == 0)
    def _():
        for out, place in ((on, 1 - info[2]), (there, info[2])):
            out[...] = dot(lhs[span(place, rows), :], rhs[:, :columns]).astype(bf16)
        last_send[...] = dot(lhs[...], rhs[:, columns:]).astype(bf16)

    @pl.when(step == 1)
    def _():
        keep[...] = dot(lhs[...], rhs[:, :columns]).astype(bf16)
        last_keep[...] = dot(lhs[...], rhs[:, columns:]).astype(bf16)


def out_u_grad(info, mixed, branch, normed, dgates, send, keep):
    step = pl.program_id(0)
    half = dgates.shape[1]
    rows = mixed.shape[0] // 2

    def both(out):
        out[:, :half] = dot(normed[...], dgates[...]).astype(bf16)
        for side in range(2):
            result = dot(mixed[...], branch[:, pl.ds(side * half, half)]).astype(bf16)
            for quarter in range(2):
                piece = result[quarter * rows : (quarter + 1) * rows, :]
                out[pl.ds((2 * quarter + side) * rows, rows), half:] = piece

    @pl.when(step == 0)
    def _():
        both(send)

    @pl.when(step == 1)
    def _():
        both(keep)


def back_two(info, grad_left, grad_right, up, gate, n2, mixed, normed, first, second, n2_turned, mixed_turned, normed_turned):
    normed_turned[...] = normed[...].T
    n2_turned[...] = n2[...].T
    mixed_turned[...] = mixed[...].T
    result = (dot_t(grad_left[...], up[...]) + dot_t(grad_right[...], gate[...])).astype(bf16)
    i = pl.program_id(0)

    @pl.when(i == 0)
    def _():
        first[...] = result

    @pl.when(i == 1)
    def _():
        second[...] = result


def split_product(info, inner, down, hidden, send_in, sends, keep):
    result = dot(inner[...], down[...])
    i = pl.program_id(0)

    @pl.when(i == 0)
    def _():
        sends[0] = send_in[...]
        sends[1] = result.astype(bf16)

    @pl.when(i == 1)
    def _():
        keep[...] = result + hidden[...]


def back_in(info, du, grads, w, send, keep):
    half = du.shape[1]
    i = pl.program_id(0)
    result = dot_t(du[...], w[3])
    for j in range(3):
        result = result + dot_t(grads[:, pl.ds(j * half, half)], w[j])
    result = result.astype(bf16)

    @pl.when(i == 0)
    def _():
        send[...] = result

    @pl.when(i == 1)
    def _():
        keep[...] = result


def back_mix(rows, block, heads, dim, info, own_0, own_1, other_0, other_1, hidden, g, att_own, att_other, u_own, u_other, wo_own, wo_other, q, rate, dh, branch, dgates, datt, direct, local, dm_own, dm_other, es):
    i = pl.program_id(0)
    b = jnp.where(i == 0, 1 - info[0], info[0])
    half = att_own.shape[1]
    width = 2 * half

    def hid(r, _):
        x = hidden[r, :]
        scale = scale_of(row_sum(x * x), width)
        dn = jnp.where(
            b == 0,
            own_0[r, :].astype(f32) + other_0[r, :].astype(f32),
            own_1[r, :].astype(f32) + other_1[r, :].astype(f32),
        )
        mean = row_sum(x * dn) / width
        d = g[r, :].astype(f32) + scale * dn - x * (scale * scale * scale * mean)
        dh[r, :] = d
        branch[r, :] = d.astype(bf16)

    loop(rows, 16, hid)
    dm_own[...] = dot_t(branch[...], wo_own[...])
    dm_other[...] = dot_t(branch[...], wo_other[...])

    def att(r, start):
        a, b = att_own[r, :].astype(f32), att_other[r, :].astype(f32)
        scale = scale_of(row_sum(a * a) + row_sum(b * b), width)
        m = dm_own[r, :]
        dgates[r, :] = (m * (a * scale)).astype(bf16)
        da = m * u_own[r, :].astype(f32)
        db = dm_other[r, :] * u_other[r, :].astype(f32)
        mean = (row_sum(a * da) + row_sum(b * db)) / width
        d = (scale * da - a * (scale * scale * scale * mean)).astype(bf16)
        datt[r, :] = d
        place = row_numbers(start + 1, 16, dim)
        for h in range(heads):
            dd = d[:, h * dim : (h + 1) * dim].astype(f32)
            es[r, head(h, dim)] = (dd * jnp.exp(-rate[h] * place)).astype(bf16)

    loop(rows, 16, att)
    for h in range(heads):
        c = head(h, dim)
        direct[b, h] = t_dot(q[:, c], es[:, c])

    @pl.when(i == 1)
    def _():
        for h in range(heads):
            carried = jnp.exp(wide(-rate[h] * block, dim))
            local[h] = (direct[0, h] + carried * direct[1, h]).astype(bf16)


def attend_back(block, heads, dim, info, q, k, v, datt, states, pq, cs, sn, rate, gq, dk, dv):
    for h in range(heads):
        c = head(h, dim)
        state = states[0, h]
        fall = fall_of(rate[h])
        for start in reversed(range(0, block, CHUNK)):
            r, upto = pl.ds(start, CHUNK), start + CHUNK
            decay = decay_of(rate[h], start, fall)
            qc, da = q[r, c], datt[r, c]
            weights = (dot_t(qc, k[:upto, c]) * decay).astype(bf16)
            dscore = (dot_t(da, v[:upto, c]) * decay).astype(bf16)
            entering = jnp.exp(-rate[h] * (row_numbers(start, CHUNK, dim) + 1.0))
            e = (da.astype(f32) * entering).astype(bf16)
            dq = dot(dscore, k[:upto, c]) + dot_t(e, state)
            slope = swish_slope(pq[r, c].astype(f32))
            gq[r, c] = (slope * rotate(dq, cs[r, :], -sn[r, :])).astype(bf16)
            dk_term, dv_term = t_dot(dscore, qc), t_dot(weights, da)
            if upto == block:
                dk[:, c] = dk_term
                dv[:, c] = dv_term
            else:
                dk[:upto, c] = dk[:upto, c] + dk_term
                dv[:upto, c] = dv[:upto, c] + dv_term


def finish_back(block, heads, dim, count, info, k, v, dk, dv, direct, pk, pv, cs, sn, rate, gq, near, far, out, after):
    b = pl.program_id(0)
    half = heads * dim
    out[:, :half] = gq[...]
    for h in range(heads):
        c = head(h, dim)
        last = state_sum(near, far, count, h, rate, 2 * block, dim, info[4], True)
        before = jnp.exp(wide(-rate[h] * block, dim)) * last + direct[1, h]
        after[...] = jnp.where(b == 1, last, before).astype(bf16)
        for start in range(0, block, CHUNK):
            r = pl.ds(start, CHUNK)
            leaving = jnp.exp(-rate[h] * (block - 1.0 - row_numbers(start, CHUNK, dim)))
            kd = (k[r, c].astype(f32) * leaving).astype(bf16)
            key_grad = dk[r, c] + leaving * dot_t(v[r, c], after[...])
            value_grad = dv[r, c] + dot(kd, after[...])
            gk = swish_slope(pk[r, c].astype(f32)) * rotate(key_grad, cs[r, :], -sn[r, :])
            out[r, pl.ds(half + h * dim, dim)] = gk.astype(bf16)
            out[r, pl.ds(2 * half + h * dim, dim)] = (
                swish_slope(pv[r, c].astype(f32)) * value_grad
            ).astype(bf16)


def add_kernel(info, *refs):
    *terms, out = refs

    def body(r, _):
        total = terms[0][r, :].astype(f32)
        for term in terms[1:]:
            total = total + term[r, :].astype(f32)
        out[r, :] = total.astype(bf16)

    loop(out.shape[0], 16, body)


def join_kernel(info, *refs):
    out = refs[6]
    cut = refs[0].shape[1]
    add_kernel(info, *refs[:3], out.at[:, pl.ds(0, cut)])
    add_kernel(info, *refs[3:6], out.at[:, pl.ds(cut, out.shape[1] - cut)])


def choose_kernel(info, mine, arrived, out):
    place = info[4]
    inner = (place == 1) | (place == 2)

    def body(r, _):
        value = jnp.where(inner, mine[r, :].astype(f32), arrived[r, :].astype(f32))
        out[r, :] = value.astype(bf16)

    loop(out.shape[0], 16, body)


def choose(info, pieces, use):
    step = pl.program_id(0)
    first = (step // 2) != info[1]
    second = lax.rem(step, 2) != info[2]
    for index, piece in enumerate(pieces):
        at_first, at_second = index >= 2, index % 2 == 1

        @pl.when((first == at_first) & (second == at_second))
        def _(piece=piece):
            use(piece)


def place_whole(info, *refs):
    pieces, out = refs[:4], refs[4]

    def put(piece):
        out[...] = piece[...].astype(f32)

    choose(info, pieces, put)


def place_turned(info, *refs):
    pieces, out = refs[:4], refs[4]

    def put(piece):
        out[...] = piece[...].astype(f32).T

    choose(info, pieces, put)


def place_heads(info, *refs):
    qkv, others, out = refs[:4], refs[4:8], refs[8]
    width = out.shape[2]
    last = qkv[0].shape[1] - 2 * width

    def put_qkv(piece):
        for j in range(2):
            out[:, j, :] = piece[:, pl.ds(j * width, width)].astype(f32)
        out[:, 2, :last] = piece[:, 2 * width :].astype(f32)

    def put_others(piece):
        out[:, 3, :] = piece[:, :width].astype(f32)
        out[:, 2, last:] = piece[:, 2 * width :].astype(f32)

    choose(info, qkv, put_qkv)
    choose(info, others, put_others)


def place_rows(info, *refs):
    pieces, out = refs[:4], refs[4]
    rows, width = out.shape[0], out.shape[1] // 2

    def put(piece):
        out[:, :width] = piece[:rows, width : 2 * width].astype(f32)
        out[:, width:] = piece[rows:, width : 2 * width].astype(f32)

    choose(info, pieces, put)


def swap(value, axis, bit):
    return lax.ppermute(value, axis, [(i, i ^ bit) for i in range(lax.axis_size(axis))])


def shift(value, axis, distance):
    count = lax.axis_size(axis)
    return lax.ppermute(
        value, axis, [(i, i + distance) for i in range(count) if 0 <= i + distance < count]
    )


def cross(value, turn):
    pairs = []
    for place in range(lax.axis_size("dp")):
        for core in range(2):
            pairs.append((2 * place + core, 2 * (place ^ (1 << (core ^ turn))) + core))
    return lax.ppermute(value, ("dp", "heads"), pairs)


def part(value, index, rows, axis=0):
    return lax.dynamic_slice_in_dim(value, index * rows, rows, axis)


def add(*terms):
    total = terms[0].astype(f32)
    for term in terms[1:]:
        total = total + term.astype(f32)
    return total.astype(bf16)


class States:
    def __init__(self, spine, local, rate, rows, backward):
        self.spine, self.local, self.rate = spine, local, rate
        self.rows, self.backward = rows, backward
        self.count = lax.axis_size("seq")
        if self.count == 4:
            self.near = swap(local, "seq", 1)

    def second(self):
        if self.count == 4:
            (self.near,) = self.spine.wait(self.near)
            here = View(lambda ref, i, s: ref)
            heads, dim = self.local.shape[:2]
            body = functools.partial(pair_states, heads=heads, dim=dim, rows=self.rows, backward=self.backward, count=4)

            def kernel(info, own, near, rate, out):
                body(info, own=own, near=near, rate=rate, out=out)

            ins = [(self.local, here), (self.near, here), (self.rate, SMEM)]
            outs = [(self.local.shape, bf16, here)]
            self.far = swap(self.spine.call(kernel, 1, ins, outs, name="pair_states")[0], "seq", 2)

    def all(self):
        if self.count == 4:
            (far,) = self.spine.wait(self.far)
            return self.near, far
        sign = -1 if self.backward else 1
        total = shift(self.local.astype(f32), "seq", sign)
        distance = 1
        while distance < self.count - 1:
            power = jnp.exp(-self.rate * self.rows * distance)[:, None, None]
            total = total + power * shift(total, "seq", sign * distance)
            distance *= 2
        return total, total


class Sum:
    last = None

    def __init__(self, spine, send, keep=None, there=None):
        self.spine, self.keep, self.cut = spine, keep, there is not None
        self.first = cross(send, 0)
        self.second_part = cross(there, 0) if self.cut else None
        self.shape = send.shape[0] if self.cut else send.shape[0] // 2, send.shape[1]
        self.four = lax.axis_size("seq") == 4

    def combine(self, body, *terms):
        rows = self.shape[0]

        def view(turn):
            if turn is None:
                return View(lambda ref, i, s: ref)
            return View(lambda ref, i, s: ref.at[span(1 - s[2] if turn else s[2], rows), :])

        ins = [(value, view(turn)) for value, turn in terms]
        outs = [(self.shape, bf16, view(None))]
        return self.spine.call(body, 1, ins, outs, name="combine")[0]

    def second(self):
        (self.first,) = self.spine.wait(self.first)
        turn = None if self.cut else True
        self.across = cross(self.combine(add_kernel, (self.keep, True), (self.first, turn)), 1)

    def last_second(self):
        self.last.second()

    def last_wait(self):
        (self.last.across,) = self.spine.wait(self.last.across)

    def line(self):
        if self.cut:
            across, first = self.spine.wait(self.across, self.second_part)
            first = first, None
        else:
            (across,) = self.spine.wait(self.across)
            first = self.first, False
        terms = [(self.keep, False), first, (across, None)]
        if self.last is None:
            self.value = self.combine(add_kernel, *terms)
        else:
            last = self.last
            terms += [(last.keep, False), (last.first, False), (last.across, None)]
            self.shape = self.shape[0], self.shape[1] + self.last.shape[1]
            self.value = self.combine(join_kernel, *terms)
        if self.four:
            self.inward = lax.ppermute(self.value, "seq", [(0, 1), (3, 2)])

    def line_across(self):
        if self.four:
            (inward,) = self.spine.wait(self.inward)
            self.value = self.combine(add_kernel, (self.value, None), (inward, None))
            self.middle = lax.ppermute(self.value, "seq", [(1, 2), (2, 1)])

    def line_back(self):
        if self.four:
            (middle,) = self.spine.wait(self.middle)
            self.value = self.combine(add_kernel, (self.value, None), (middle, None))
            self.outer = lax.ppermute(self.value, "seq", [(1, 0), (2, 3)])

    def spread(self):
        if self.four:
            (outer,) = self.spine.wait(self.outer)
            total = self.combine(choose_kernel, (self.value, None), (outer, None))
        else:
            total = lax.psum(self.value.astype(f32), "seq").astype(bf16)
            self.spine.after(total)
        self.value, self.second_half, self.own_first = total, cross(total, 1), cross(total, 0)

    def spread_on(self):
        (second,) = self.spine.wait(self.second_half)
        self.pieces = [self.value, second, self.own_first, cross(second, 0)]

    def arrive(self):
        self.pieces[2:] = self.spine.wait(*self.pieces[2:])
        return self.pieces


def shards(
    tokens,
    cotangent,
    qkvu_weight,
    out_weight,
    up_weight,
    gate_weight,
    down_weight,
    decay_rate,
    item_length,
    item_slot,
):
    core = lax.axis_index("heads")
    seq_place = lax.axis_index("seq")
    data_place = lax.axis_index("dp")
    block, width = tokens.shape[1:]
    heads = decay_rate.shape[0]
    half = qkvu_weight.shape[2]
    dim = half // heads
    ff = up_weight.shape[1] // 2
    rows = 2 * block
    tile = block // 2
    rate = (decay_rate, SMEM)

    own, own_cot = tokens[0], cotangent[0]
    other = swap(own, "heads", 1)
    other_cot = swap(own_cot, "heads", 1)
    other_out = swap(out_weight, "heads", 1)
    weights = jnp.transpose(qkvu_weight, (1, 0, 2))
    fine = 32
    lanes = jnp.arange(dim)
    frequency = 10000.0 ** (-(lanes % (dim // 2)).astype(f32) / (dim // 2))
    coarse_steps = seq_place * rows + fine * jnp.arange(rows // fine)
    steps = jnp.concatenate([coarse_steps, jnp.arange(fine)]).astype(f32)
    angles = steps[:, None] * frequency[None, :]
    cosine, sine = lax.optimization_barrier((jnp.cos(angles), jnp.sin(angles)))
    c_far, s_far = cosine[:-fine, None, :], sine[:-fine, None, :]
    c_near, s_near = cosine[None, -fine:, :], sine[None, -fine:, :]
    sign = jnp.where(lanes < dim // 2, -1.0, 1.0)
    cs = (c_far * c_near - s_far * s_near).reshape(rows, dim)
    sn = (sign * (s_far * c_near + c_far * s_near)).reshape(rows, dim)

    def weight(j):
        return weights, View(lambda ref, i, s: ref.at[pl.ds(j, 1)])

    def by(value, size):
        return value, View(lambda ref, i, s: ref.at[span(i, size), :])

    def all_of(value):
        return value, View(lambda ref, i, s: ref)

    def out(columns, kind, size):
        return (rows, columns), kind, View(lambda ref, i, s: ref.at[span(i, size), :])

    def fixed(shape, kind):
        return shape, kind, View(lambda ref, i, s: ref)

    def fn(body, *sizes):
        return functools.partial(body, *sizes)

    down_half = down_weight, View(lambda ref, i, s: ref.at[span(s[0], ff), :])
    columns = View(lambda ref, i, s: ref.at[:, span(s[0], ff)])
    up_half, gate_half = (up_weight, columns), (gate_weight, columns)
    spine = Spine()
    call = spine.call
    square = (heads, dim, dim)
    big, low = pltpu.VMEM((block, half), f32), pltpu.VMEM((block, half), bf16)

    def turned(columns):
        return (columns, rows), bf16, View(lambda ref, i, s: ref.at[:, span(i, block)])

    normed, k, v, pk, pv, contrib, local = call(
        fn(project_kv, block, heads, dim),
        2,
        [all_of(own), all_of(other), weight(1), weight(2), by(cs, block), by(sn, block)]
        + [rate],
        [out(width, bf16, block)]
        + [out(half, bf16, block)] * 4
        + [fixed((2,) + square, f32), fixed(square, bf16)],
        [big, big, low],
        name="project_kv",
    )
    line = States(spine, local, decay_rate, rows, False)
    g, g_t, grad_inner, valid = call(
        fn(begin_back, block),
        2,
        [all_of(own_cot), all_of(other_cot), down_half]
        + [(item_slot, SMEM), (item_length, SMEM)],
        [out(width, bf16, block), turned(width), out(ff, bf16, block), out(dim, f32, block)],
        name="begin_back",
    )
    line.second()
    q, pq, u_own, intra = call(
        fn(project_qu, block, heads, dim),
        2,
        [by(normed, block), weight(0), weight(3), by(cs, block), by(sn, block), rate]
        + [by(k, block), by(v, block)],
        [out(half, bf16, block)] * 3 + [out(half, f32, block)],
        [big],
        name="project_qu",
    )
    u_other = swap(u_own, "heads", 1)
    near, far = line.all()
    att_own, states = call(
        fn(attend, block, heads, dim, line.count),
        1,
        [all_of(q), all_of(intra), all_of(contrib), rate, all_of(near), all_of(far)],
        [fixed((rows, half), bf16), fixed((2,) + square, bf16)],
        name="attend",
    )
    att_other = swap(att_own, "heads", 1)
    att_u = [by(att_own, block), by(att_other, block), by(u_own, block), by(u_other, block)]
    out_both = [all_of(out_weight), all_of(other_out)]
    hidden, n2, mixed = call(
        fn(mix_out, block),
        2,
        att_u + out_both + [all_of(own), all_of(other)],
        [out(width, f32, block), out(width, bf16, block), out(half, bf16, block)],
        [pltpu.VMEM((block, width), bf16)],
        name="mix_out",
    )
    inner, grad_left, grad_right = call(
        fn(feed, block),
        2,
        [by(n2, block), up_half, gate_half, by(grad_inner, block)],
        [out(ff, bf16, block)] * 3,
        [pltpu.VMEM((block, ff), f32)] * 2,
        name="feed",
    )

    def halves(value):
        size = value.shape[0] // 2

        def at(ref, i, s):
            return ref.at[span(jnp.where(i == 0, 1 - s[1], s[1]), size), :]

        return value, View(at)

    def grad(name, lhs, rhs):
        shape = lhs.shape[0] // 2, rhs.shape[1]
        return call(
            weight_grad, 2, [halves(lhs), all_of(rhs)], [fixed(shape, bf16)] * 2, name=name
        )

    def sides(value):
        def at(ref, i, s):
            return ref.at[span(jnp.where(i == 0, 1 - s[0], s[0]), block), :]

        return value, View(at)

    two_sides = [fixed((block, width), bf16)] * 2

    def half_grad(name, lhs, rhs, send):
        size = lhs.shape[0] // 2

        def at(ref, i, s):
            return ref.at[span(1 - s[1] if send else s[1], size), :]

        shape = size, rhs.shape[1]
        ins = [(lhs, View(at)), all_of(rhs)]
        return call(weight_half, 1, ins, [fixed(shape, bf16)], name=name)[0]

    down = Sum(spine, half_grad("down_send", g_t, inner, True))
    *partial, n2_t, mixed_t, normed_t = call(
        back_two,
        2,
        [by(grad_left, block), by(grad_right, block), up_half, gate_half]
        + [by(n2, block), by(mixed, block), by(normed, block)],
        two_sides + [turned(width), turned(half), turned(width)],
        name="back_two",
    )
    partial_other = [swap(value, "heads", 1) for value in partial]
    up = Sum(spine, *grad("up_grad", n2_t, grad_left))
    gate = Sum(spine, *grad("gate_grad", n2_t, grad_right))
    down.keep = half_grad("down_keep", g_t, inner, False)
    partial_other = spine.wait(*partial_other)
    down.second()
    dh, branch, dgates, datt, direct, local = call(
        fn(back_mix, block, block, heads, dim),
        2,
        [all_of(x) for x in (*partial, *partial_other)]
        + [sides(x) for x in (hidden, g, att_own, att_other, u_own, u_other)]
        + out_both
        + [sides(q), rate],
        [fixed((block, width), f32)]
        + [((rows, size), bf16, sides(None)[1]) for size in (width, half, half)]
        + [fixed((2,) + square, f32), fixed(square, bf16)],
        [pltpu.VMEM((block, half), f32)] * 2 + [pltpu.VMEM((block, half), bf16)],
        name="back_mix",
    )
    flat = pl.BlockSpec((width // 4, ff), lambda i: (i, 0))

    def place(body, pieces, shape, spec, name):
        return call(
            body, 4, [(p, whole(p)) for p in pieces], [(shape, f32, spec)], name=name
        )[0]
    line = States(spine, local, decay_rate, rows, True)
    out_u = call(
        out_u_grad,
        2,
        [halves(mixed_t), all_of(branch), halves(normed_t), all_of(dgates)],
        [fixed((block, width), bf16)] * 2,
        name="out_u_grad",
    )
    out_u = Sum(spine, *out_u)
    line.second()
    up.second()
    down.line()
    gq, dk, dv = call(
        fn(attend_back, block, heads, dim),
        2,
        [by(q, block), by(k, block), by(v, block), by(datt, block)]
        + [(states, View(lambda ref, i, s: ref.at[pl.ds(i, 1)])), by(pq, block)]
        + [by(cs, block), by(sn, block), rate],
        [out(half, bf16, block), out(half, f32, block), out(half, f32, block)],
        name="attend_back",
    )
    near, far = line.all()
    down.line_across()
    up.line()
    grads = call(
        fn(finish_back, block, heads, dim, line.count),
        2,
        [by(k, block), by(v, block), by(dk, block), by(dv, block), all_of(direct)]
        + [by(pk, block), by(pv, block), by(cs, block), by(sn, block), rate]
        + [by(gq, block), all_of(near), all_of(far)],
        [out(3 * half, bf16, block)],
        [pltpu.VMEM((dim, dim), bf16)],
        name="finish_back",
    )[0]
    flat = pl.BlockSpec((width // 4, ff), lambda i: (i, 0))

    def place(body, pieces, shape, spec, name):
        return call(
            body, 4, [(p, whole(p)) for p in pieces], [(shape, f32, spec)], name=name
        )[0]

    quarter = rows // 4
    on, there, keep, last_send, last_keep = call(
        weight_grad_cut,
        2,
        [halves(normed_t), all_of(grads)],
        [fixed((quarter, ff), bf16)] * 2
        + [fixed((block, ff), bf16)]
        + [fixed((block, 3 * half - ff), bf16)] * 2,
        name="qkv_grad",
    )
    qkv = Sum(spine, on, keep, there)
    out_u.last = Sum(spine, last_send, last_keep)
    gate.second()
    send_in, keep_in = call(
        back_in,
        2,
        [sides(dgates), sides(grads), all_of(weights)],
        two_sides,
        name="back_in",
    )
    out_u.second()
    down.line_back()
    up.line_across()
    sends, keep_out = call(
        split_product,
        2,
        [sides(inner), down_half, sides(hidden), all_of(send_in)],
        [fixed((2, block, width), bf16), fixed((block, width), f32)],
        name="split_product",
    )
    gate.line()
    qkv.second()
    down.spread()
    up.line_back()
    qkv.line()
    gate.line_across()
    out_u.last_second()
    down.spread_on()
    up.spread()
    qkv.line_across()
    gate.line_back()
    out_u.last_wait()
    out_u.line()
    down_grad = place(
        place_turned,
        down.arrive(),
        (ff, width),
        pl.BlockSpec((ff, width // 4), lambda i: (0, i)),
        "place_down",
    )
    (sends,) = spine.wait(sends)
    arrived_both = [swap(sends[n], "heads", 1) for n in range(2)]
    up.spread_on()
    qkv.line_back()
    gate.spread()
    out_u.line_across()
    up_grad = place(place_whole, up.arrive(), (width, ff), flat, "place_up")
    gate.spread_on()
    qkv.spread()
    out_u.line_back()
    qkv.spread_on()
    out_u.spread()
    gate_grad = place(place_whole, gate.arrive(), (width, ff), flat, "place_gate")
    out_u.spread_on()
    arrived_in, arrived_out = spine.wait(*arrived_both)
    def own_rows(value):
        return part(value, core, block)

    def add_wide(a, b):
        return a.astype(f32) + b.astype(f32)

    output = add_wide(keep_out, arrived_out)
    output = (output * own_rows(valid)[:, :1]).astype(bf16)
    x = own.astype(f32)
    scale = lax.rsqrt(jnp.mean(x * x, axis=-1, keepdims=True) + epsilon)
    dn = add_wide(keep_in, arrived_in)
    grad_inputs = (
        dh
        + scale * dn
        - x * (scale * scale * scale) * jnp.mean(x * dn, axis=-1, keepdims=True)
    )
    spine.after(output, grad_inputs)
    out_u_pieces = out_u.arrive()
    out_grad = place(
        place_rows,
        out_u_pieces,
        (half, width),
        pl.BlockSpec((half // 4, width), lambda i: (i, 0)),
        "place_out",
    )
    qkvu_grad = place(
        place_heads,
        qkv.arrive() + out_u_pieces,
        (width, 4, half),
        pl.BlockSpec((width // 4, 4, half), lambda i: (i, 0, 0)),
        "place_qkvu",
    )
    return output[None], grad_inputs[None], qkvu_grad, out_grad, up_grad, gate_grad, down_grad


def solution(mesh):
    placed = (
        P("dp", ("seq", "heads"), None),
        P("dp", ("seq", "heads"), None),
        P(None, None, "heads"),
        P("heads", None),
        P(),
        P(),
        P(),
        P("heads"),
        P(),
        P(),
    )
    return jax.shard_map(
        shards,
        mesh=mesh,
        in_specs=placed,
        out_specs=(
            P("dp", ("seq", "heads"), None),
            P("dp", ("seq", "heads"), None),
            P(None, None, "heads"),
            P("heads", None),
            P(None, "heads"),
            P(None, "heads"),
            P("heads", None),
        ),
        check_vma=False,
    )
```

```python
import functools
import math

import jax
import jax.numpy as jnp
from jax import lax
from jax.experimental import pallas as pl
from jax.experimental.pallas import tpu as pltpu
from jax.sharding import PartitionSpec as P

epsilon = 1e-06
f32 = jnp.float32
bf16 = jnp.bfloat16
CHUNK = 512


def dot(a, b):
    return jnp.dot(a, b, preferred_element_type=f32)


def dot_t(a, b):
    return lax.dot_general(a, b, (((1,), (1,)), ((), ())), preferred_element_type=f32)


def t_dot(a, b):
    return lax.dot_general(a, b, (((0,), (0,)), ((), ())), preferred_element_type=f32)


def whole(value):
    rank = value.ndim
    return pl.BlockSpec(value.shape, lambda i: (0,) * rank, pipeline_mode=pl.Buffered(1))


class View:
    block_shape = None

    def __init__(self, at):
        self.at = at


class Places:
    def __getitem__(self, index):
        core, data = lax.axis_index("heads"), lax.axis_index("dp")
        low, high = lax.rem(data, 2), data // 2
        if index == 0:
            return core
        if index == 1:
            return jnp.where(core == 0, low, high)
        if index == 2:
            return jnp.where(core == 0, high, low)
        return data if index == 3 else lax.axis_index("seq")


def span(index, size):
    return pl.ds(pl.multiple_of(index * size, size), size)


def spec_of(spec):
    return pl.BlockSpec(memory_space=pltpu.VMEM) if isinstance(spec, View) else spec


def room(blocks, scratch, name):
    total = 0
    for spec, kind in blocks:
        if spec.block_shape is not None:
            buffers = 1 if spec.pipeline_mode is not None else 2
            total += buffers * math.prod(spec.block_shape) * jnp.dtype(kind).itemsize
    for buffer in scratch:
        if buffer.dtype in (f32, bf16):
            total += math.prod(buffer.shape) * jnp.dtype(buffer.dtype).itemsize
    return total + SLACK.get(name, 4) * 2**20


SLACK = {"begin_back": 5, "attend_back": 5, "split_product": 6, "back_two": 8}


def tiles(value, rows):
    return pl.BlockSpec((rows, value.shape[1]), lambda i: (i, 0))


SMEM = pl.BlockSpec(memory_space=pltpu.SMEM)


class Spine:
    def __init__(self):
        self.token = None
        self.done = []

    def call(self, body, steps, ins, outs, scratch=(), name=None):
        after = self.done + ([] if self.token is None else [self.token])
        used, given = len(ins), len(outs)
        specs = [spec for _, spec in ins] + [spec for _, _, spec in outs]
        blocks = [(spec, value.dtype) for value, spec in ins]
        blocks += [(spec, kind) for _, kind, spec in outs]

        def kernel(*refs):
            rest = refs[used + len(after) :]
            rest[given][...] = jnp.zeros((8, 128), f32)
            step, places = pl.program_id(0), Places()
            given_refs = [
                spec.at(ref, step, places) if isinstance(spec, View) else ref
                for spec, ref in zip(specs, list(refs[:used]) + list(rest[:given]))
            ]
            body(places, *given_refs, *rest[given + 1 :])

        results = pl.pallas_call(
            kernel,
            grid=(steps,),
            in_specs=[spec_of(spec) for _, spec in ins]
            + [pl.BlockSpec(memory_space=pl.ANY)] * len(after),
            out_specs=[spec_of(spec) for _, _, spec in outs]
            + [pl.BlockSpec(memory_space=pltpu.VMEM)],
            scratch_shapes=list(scratch),
            out_shape=[jax.ShapeDtypeStruct(shape, kind) for shape, kind, _ in outs]
            + [jax.ShapeDtypeStruct((8, 128), f32)],
            compiler_params=pltpu.CompilerParams(vmem_limit_bytes=room(blocks, scratch, name)),
            cost_estimate=pl.CostEstimate(flops=0, bytes_accessed=0, transcendentals=0),
            name=name,
        )(*[value for value, _ in ins], *after)
        self.token, self.done = results[-1], []
        return results[:-1]

    def after(self, *values):
        self.done += values

    def wait(self, *values):
        if self.done:
            token = self.token
            for value in self.done:
                token = token + value[:8, :128].astype(f32)
            self.token, self.done = token, []
        results = lax.optimization_barrier((self.token,) + values)
        self.token = results[0]
        return results[1:]


def loop(count, step, body, unroll=True):
    def turn(i, _):
        body(pl.ds(pl.multiple_of(i * step, step), step), i * step)
        return 0

    lax.fori_loop(0, count // step, turn, 0, unroll=unroll)


def head(h, dim):
    return pl.ds(h * dim, dim)


def rotate(value, cosine, sine):
    return value * cosine + pltpu.roll(value, value.shape[1] // 2, 1) * sine


def sigmoid(value):
    return 0.5 * jnp.tanh(0.5 * value) + 0.5


def swish(value):
    return value * sigmoid(value)


def swish_slope(value):
    s = sigmoid(value)
    y = value * s
    return y + s * (1.0 - y)


def row_numbers(start, rows, columns):
    return (lax.broadcasted_iota(jnp.int32, (rows, columns), 0) + start).astype(f32)


def fall_of(rate):
    return jnp.exp(-rate * row_numbers(0, CHUNK, CHUNK))


def decay_of(rate, start, fall):
    upto = start + CHUNK
    columns = lax.broadcasted_iota(jnp.int32, (1, upto), 1).astype(f32)
    rise = jnp.exp(rate * (columns - float(start)))
    tiles = [rise[:, j : j + CHUNK] * fall for j in range(0, upto, CHUNK)]
    rows = lax.broadcasted_iota(jnp.int32, (CHUNK, CHUNK), 0)
    inside = rows >= lax.broadcasted_iota(jnp.int32, (CHUNK, CHUNK), 1)
    tiles[-1] = jnp.where(inside, tiles[-1], 0.0)
    return jnp.concatenate(tiles, 1) if start else tiles[0]


def scale_of(total, width):
    return lax.rsqrt(total / width + epsilon)


def row_sum(value):
    return jnp.sum(value, axis=-1, keepdims=True)


def wide(scalar, dim):
    return jnp.full((1, dim), scalar, f32)


def project_kv(block, heads, dim, info, own, other, wk, wv, cs, sn, rate, normed, k, v, pk, pv, contrib, local, sk, sv, kd):
    b = pl.program_id(0)
    mine = b == info[0]
    width = own.shape[1]

    def norm(r, _):
        x = jnp.where(mine, own[r, :].astype(f32), other[r, :].astype(f32))
        normed[r, :] = (x * scale_of(row_sum(x * x), width)).astype(bf16)

    loop(block, 16, norm)
    sk[...] = dot(normed[...], wk[0])
    sv[...] = dot(normed[...], wv[0])

    def act(r, start):
        cosine, sine = cs[r, :], sn[r, :]
        steps = block - 1.0 - row_numbers(start, 64, dim)
        for h in range(heads):
            c = head(h, dim)
            p = sk[r, c]
            pk[r, c] = p.astype(bf16)
            key = rotate(swish(p), cosine, sine).astype(bf16)
            k[r, c] = key
            kd[r, c] = (key.astype(f32) * jnp.exp(-rate[h] * steps)).astype(bf16)
            p = sv[r, c]
            pv[r, c] = p.astype(bf16)
            v[r, c] = swish(p).astype(bf16)

    loop(block, 64, act)
    for h in range(heads):
        c = head(h, dim)
        contrib[b, h] = t_dot(kd[:, c], v[:, c])

    @pl.when(b == 1)
    def _():
        for h in range(heads):
            carried = jnp.exp(wide(-rate[h] * block, dim))
            local[h] = (carried * contrib[0, h] + contrib[1, h]).astype(bf16)


def project_qu(block, heads, dim, info, normed, wq, wu, cs, sn, rate, k, v, q, pq, u, intra, sq):
    sq[...] = dot(normed[...], wq[0])
    u[...] = dot(normed[...], wu[0]).astype(bf16)

    def act(r, start):
        cosine, sine = cs[r, :], sn[r, :]
        for h in range(heads):
            c = head(h, dim)
            p = sq[r, c]
            pq[r, c] = p.astype(bf16)
            q[r, c] = rotate(swish(p), cosine, sine).astype(bf16)

    loop(block, 64, act)
    for h in range(heads):
        c = head(h, dim)
        fall = fall_of(rate[h])
        for start in range(0, block, CHUNK):
            r, upto = pl.ds(start, CHUNK), start + CHUNK
            scores = dot_t(q[r, c], k[:upto, c]) * decay_of(rate[h], start, fall)
            intra[r, c] = dot(scores.astype(bf16), v[:upto, c])


def pair_states(info, count, heads, dim, rows, backward, own, near, rate, out):
    even = lax.rem(info[4], 2) == 0
    for h in range(heads):
        decay = jnp.exp(wide(-rate[h] * rows, dim))
        a, b = own[h].astype(f32), near[h].astype(f32)
        plain, decayed = (a, b) if backward else (b, a)
        other = (b, a) if backward else (a, b)
        out[h] = jnp.where(even, plain + decay * decayed, other[0] + decay * other[1]).astype(bf16)


def state_sum(near, far, count, h, rate, rows, dim, place, backward):
    if count != 4:
        return near[h]
    side = lax.rem(place, 2) == (0 if backward else 1)
    pair = place < 2 if backward else place >= 2
    decay = jnp.where(side, jnp.exp(wide(-rate[h] * rows, dim)), 1.0)
    first = jnp.where(side, near[h].astype(f32), 0.0)
    return first + jnp.where(pair, decay * far[h].astype(f32), 0.0)


def attend(block, heads, dim, count, info, q, intra, contrib, rate, near, far, att, states):
    for h in range(heads):
        c = head(h, dim)
        first = state_sum(near, far, count, h, rate, 2 * block, dim, info[4], False)
        second = jnp.exp(wide(-rate[h] * block, dim)) * first + contrib[0, h]
        for b, state in enumerate((first, second)):
            states[b, h] = state.astype(bf16)
        for b in range(2):
            state = states[b, h]
            for start in range(0, block, CHUNK):
                r = pl.ds(b * block + start, CHUNK)
                entering = jnp.exp(-rate[h] * (row_numbers(start, CHUNK, dim) + 1.0))
                att[r, c] = (intra[r, c] + entering * dot(q[r, c], state)).astype(bf16)


def begin_back(rows, info, own, other, down, item_slot, item_length, g, turned, grad_inner, valid):
    i = pl.program_id(0)
    mine = i == info[0]
    limit = item_length[item_slot[info[3]]] - (2 * info[4] + i) * rows

    def read(r, start):
        value = jnp.where(mine, own[r, :].astype(f32), other[r, :].astype(f32))
        inside = lax.broadcasted_iota(jnp.int32, value.shape, 0) + start < limit
        g[r, :] = jnp.where(inside, value, 0.0).astype(bf16)

    loop(rows, 16, read)
    valid[...] = (lax.broadcasted_iota(jnp.int32, valid.shape, 0) < limit).astype(f32)
    grad_inner[...] = dot_t(g[...], down[...]).astype(bf16)
    turned[...] = g[...].T


def mix_out(rows, info, att_own, att_other, u_own, u_other, wo_own, wo_other, own, other, hidden, n2, mixed, both):
    mine = pl.program_id(0) == info[0]
    half = att_own.shape[1]
    width = 2 * half

    def mix(r, _):
        a, b = att_own[r, :].astype(f32), att_other[r, :].astype(f32)
        scale = scale_of(row_sum(a * a) + row_sum(b * b), width)
        both[r, :half] = (a * scale * u_own[r, :].astype(f32)).astype(bf16)
        both[r, half:] = (b * scale * u_other[r, :].astype(f32)).astype(bf16)

    loop(rows, 16, mix)
    hidden[...] = dot(both[:, :half], wo_own[...]) + dot(both[:, half:], wo_other[...])
    mixed[...] = both[:, :half]

    def norm(r, _):
        x = jnp.where(mine, own[r, :].astype(f32), other[r, :].astype(f32))
        x = hidden[r, :] + x
        hidden[r, :] = x
        n2[r, :] = (x * scale_of(row_sum(x * x), width)).astype(bf16)

    loop(rows, 16, norm)


def feed(rows, info, n2, up, gate, grad_inner, inner, grad_left, grad_right, left, right):
    left[...] = dot(n2[...], up[...])
    right[...] = dot(n2[...], gate[...])

    def join(r, _):
        a, b, g = left[r, :], right[r, :], grad_inner[r, :].astype(f32)
        inner[r, :] = (a * b).astype(bf16)
        grad_left[r, :] = (g * b).astype(bf16)
        grad_right[r, :] = (g * a).astype(bf16)

    loop(rows, 16, join)


def turn_kernel(info, mixed, normed, mixed_turned, normed_turned):
    mixed_turned[...] = mixed[...].T
    normed_turned[...] = normed[...].T


def weight_half(info, lhs, rhs, out):
    out[...] = dot(lhs[...], rhs[...]).astype(bf16)


def weight_grad(info, lhs, rhs, send, keep):
    step = pl.program_id(0)

    @pl.when(step == 0)
    def _():
        send[...] = dot(lhs[...], rhs[...]).astype(bf16)

    @pl.when(step == 1)
    def _():
        keep[...] = dot(lhs[...], rhs[...]).astype(bf16)


def weight_grad_cut(info, lhs, rhs, on, there, keep, last_send, last_keep):
    step = pl.program_id(0)
    columns, rows = keep.shape[1], on.shape[0]

    @pl.when(step == 0)
    def _():
        for out, place in ((on, 1 - info[2]), (there, info[2])):
            out[...] = dot(lhs[span(place, rows), :], rhs[:, :columns]).astype(bf16)
        last_send[...] = dot(lhs[...], rhs[:, columns:]).astype(bf16)

    @pl.when(step == 1)
    def _():
        keep[...] = dot(lhs[...], rhs[:, :columns]).astype(bf16)
        last_keep[...] = dot(lhs[...], rhs[:, columns:]).astype(bf16)


def out_u_grad(info, mixed, branch, normed, dgates, send, keep):
    step = pl.program_id(0)
    half = dgates.shape[1]
    rows = mixed.shape[0] // 2

    def both(out):
        out[:, :half] = dot(normed[...], dgates[...]).astype(bf16)
        for side in range(2):
            result = dot(mixed[...], branch[:, pl.ds(side * half, half)]).astype(bf16)
            for quarter in range(2):
                piece = result[quarter * rows : (quarter + 1) * rows, :]
                out[pl.ds((2 * quarter + side) * rows, rows), half:] = piece

    @pl.when(step == 0)
    def _():
        both(send)

    @pl.when(step == 1)
    def _():
        both(keep)


def back_two(info, grad_left, grad_right, up, gate, n2, first, second, n2_turned):
    n2_turned[...] = n2[...].T
    result = (dot_t(grad_left[...], up[...]) + dot_t(grad_right[...], gate[...])).astype(bf16)
    i = pl.program_id(0)

    @pl.when(i == 0)
    def _():
        first[...] = result

    @pl.when(i == 1)
    def _():
        second[...] = result


def split_product(info, inner, down, hidden, send_in, sends, keep):
    result = dot(inner[...], down[...])
    i = pl.program_id(0)

    @pl.when(i == 0)
    def _():
        sends[0] = send_in[...]
        sends[1] = result.astype(bf16)

    @pl.when(i == 1)
    def _():
        keep[...] = result + hidden[...]


def back_in(info, du, grads, w, send, keep):
    half = du.shape[1]
    i = pl.program_id(0)
    result = dot_t(du[...], w[3])
    for j in range(3):
        result = result + dot_t(grads[:, pl.ds(j * half, half)], w[j])
    result = result.astype(bf16)

    @pl.when(i == 0)
    def _():
        send[...] = result

    @pl.when(i == 1)
    def _():
        keep[...] = result


def back_mix(rows, block, heads, dim, info, own_0, own_1, other_0, other_1, hidden, g, att_own, att_other, u_own, u_other, wo_own, wo_other, q, rate, dh, branch, dgates, datt, direct, local, dm_own, dm_other, es):
    i = pl.program_id(0)
    b = jnp.where(i == 0, 1 - info[0], info[0])
    half = att_own.shape[1]
    width = 2 * half

    def hid(r, _):
        x = hidden[r, :]
        scale = scale_of(row_sum(x * x), width)
        dn = jnp.where(
            b == 0,
            own_0[r, :].astype(f32) + other_0[r, :].astype(f32),
            own_1[r, :].astype(f32) + other_1[r, :].astype(f32),
        )
        mean = row_sum(x * dn) / width
        d = g[r, :].astype(f32) + scale * dn - x * (scale * scale * scale * mean)
        dh[r, :] = d
        branch[r, :] = d.astype(bf16)

    loop(rows, 16, hid)
    dm_own[...] = dot_t(branch[...], wo_own[...])
    dm_other[...] = dot_t(branch[...], wo_other[...])

    def att(r, start):
        a, b = att_own[r, :].astype(f32), att_other[r, :].astype(f32)
        scale = scale_of(row_sum(a * a) + row_sum(b * b), width)
        m = dm_own[r, :]
        dgates[r, :] = (m * (a * scale)).astype(bf16)
        da = m * u_own[r, :].astype(f32)
        db = dm_other[r, :] * u_other[r, :].astype(f32)
        mean = (row_sum(a * da) + row_sum(b * db)) / width
        d = (scale * da - a * (scale * scale * scale * mean)).astype(bf16)
        datt[r, :] = d
        place = row_numbers(start + 1, 16, dim)
        for h in range(heads):
            dd = d[:, h * dim : (h + 1) * dim].astype(f32)
            es[r, head(h, dim)] = (dd * jnp.exp(-rate[h] * place)).astype(bf16)

    loop(rows, 16, att)
    for h in range(heads):
        c = head(h, dim)
        direct[b, h] = t_dot(q[:, c], es[:, c])

    @pl.when(i == 1)
    def _():
        for h in range(heads):
            carried = jnp.exp(wide(-rate[h] * block, dim))
            local[h] = (direct[0, h] + carried * direct[1, h]).astype(bf16)


def attend_back(block, heads, dim, info, q, k, v, datt, states, pq, cs, sn, rate, gq, dk, dv):
    for h in range(heads):
        c = head(h, dim)
        state = states[0, h]
        fall = fall_of(rate[h])
        for start in reversed(range(0, block, CHUNK)):
            r, upto = pl.ds(start, CHUNK), start + CHUNK
            decay = decay_of(rate[h], start, fall)
            qc, da = q[r, c], datt[r, c]
            weights = (dot_t(qc, k[:upto, c]) * decay).astype(bf16)
            dscore = (dot_t(da, v[:upto, c]) * decay).astype(bf16)
            entering = jnp.exp(-rate[h] * (row_numbers(start, CHUNK, dim) + 1.0))
            e = (da.astype(f32) * entering).astype(bf16)
            dq = dot(dscore, k[:upto, c]) + dot_t(e, state)
            slope = swish_slope(pq[r, c].astype(f32))
            gq[r, c] = (slope * rotate(dq, cs[r, :], -sn[r, :])).astype(bf16)
            dk_term, dv_term = t_dot(dscore, qc), t_dot(weights, da)
            if upto == block:
                dk[:, c] = dk_term
                dv[:, c] = dv_term
            else:
                dk[:upto, c] = dk[:upto, c] + dk_term
                dv[:upto, c] = dv[:upto, c] + dv_term


def finish_back(block, heads, dim, count, info, k, v, dk, dv, direct, pk, pv, cs, sn, rate, gq, near, far, out, after):
    b = pl.program_id(0)
    half = heads * dim
    out[:, :half] = gq[...]
    for h in range(heads):
        c = head(h, dim)
        last = state_sum(near, far, count, h, rate, 2 * block, dim, info[4], True)
        before = jnp.exp(wide(-rate[h] * block, dim)) * last + direct[1, h]
        after[...] = jnp.where(b == 1, last, before).astype(bf16)
        for start in range(0, block, CHUNK):
            r = pl.ds(start, CHUNK)
            leaving = jnp.exp(-rate[h] * (block - 1.0 - row_numbers(start, CHUNK, dim)))
            kd = (k[r, c].astype(f32) * leaving).astype(bf16)
            key_grad = dk[r, c] + leaving * dot_t(v[r, c], after[...])
            value_grad = dv[r, c] + dot(kd, after[...])
            gk = swish_slope(pk[r, c].astype(f32)) * rotate(key_grad, cs[r, :], -sn[r, :])
            out[r, pl.ds(half + h * dim, dim)] = gk.astype(bf16)
            out[r, pl.ds(2 * half + h * dim, dim)] = (
                swish_slope(pv[r, c].astype(f32)) * value_grad
            ).astype(bf16)


def add_kernel(info, *refs):
    *terms, out = refs

    def body(r, _):
        total = terms[0][r, :].astype(f32)
        for term in terms[1:]:
            total = total + term[r, :].astype(f32)
        out[r, :] = total.astype(bf16)

    loop(out.shape[0], 16, body)


def join_kernel(info, *refs):
    out = refs[6]
    cut = refs[0].shape[1]
    add_kernel(info, *refs[:3], out.at[:, pl.ds(0, cut)])
    add_kernel(info, *refs[3:6], out.at[:, pl.ds(cut, out.shape[1] - cut)])


def choose_kernel(info, mine, arrived, out):
    place = info[4]
    inner = (place == 1) | (place == 2)

    def body(r, _):
        value = jnp.where(inner, mine[r, :].astype(f32), arrived[r, :].astype(f32))
        out[r, :] = value.astype(bf16)

    loop(out.shape[0], 16, body)


def choose(info, pieces, use):
    step = pl.program_id(0)
    first = (step // 2) != info[1]
    second = lax.rem(step, 2) != info[2]
    for index, piece in enumerate(pieces):
        at_first, at_second = index >= 2, index % 2 == 1

        @pl.when((first == at_first) & (second == at_second))
        def _(piece=piece):
            use(piece)


def place_whole(info, *refs):
    pieces, out = refs[:4], refs[4]

    def put(piece):
        out[...] = piece[...].astype(f32)

    choose(info, pieces, put)


def place_turned(info, *refs):
    pieces, out = refs[:4], refs[4]

    def put(piece):
        out[...] = piece[...].astype(f32).T

    choose(info, pieces, put)


def place_heads(info, *refs):
    qkv, others, out = refs[:4], refs[4:8], refs[8]
    width = out.shape[2]
    last = qkv[0].shape[1] - 2 * width

    def put_qkv(piece):
        for j in range(2):
            out[:, j, :] = piece[:, pl.ds(j * width, width)].astype(f32)
        out[:, 2, :last] = piece[:, 2 * width :].astype(f32)

    def put_others(piece):
        out[:, 3, :] = piece[:, :width].astype(f32)
        out[:, 2, last:] = piece[:, 2 * width :].astype(f32)

    choose(info, qkv, put_qkv)
    choose(info, others, put_others)


def place_rows(info, *refs):
    pieces, out = refs[:4], refs[4]
    rows, width = out.shape[0], out.shape[1] // 2

    def put(piece):
        out[:, :width] = piece[:rows, width : 2 * width].astype(f32)
        out[:, width:] = piece[rows:, width : 2 * width].astype(f32)

    choose(info, pieces, put)


def swap(value, axis, bit):
    return lax.ppermute(value, axis, [(i, i ^ bit) for i in range(lax.axis_size(axis))])


def shift(value, axis, distance):
    count = lax.axis_size(axis)
    return lax.ppermute(
        value, axis, [(i, i + distance) for i in range(count) if 0 <= i + distance < count]
    )


def cross(value, turn):
    pairs = []
    for place in range(lax.axis_size("dp")):
        for core in range(2):
            pairs.append((2 * place + core, 2 * (place ^ (1 << (core ^ turn))) + core))
    return lax.ppermute(value, ("dp", "heads"), pairs)


def part(value, index, rows, axis=0):
    return lax.dynamic_slice_in_dim(value, index * rows, rows, axis)


def add(*terms):
    total = terms[0].astype(f32)
    for term in terms[1:]:
        total = total + term.astype(f32)
    return total.astype(bf16)


class States:
    def __init__(self, spine, local, rate, rows, backward):
        self.spine, self.local, self.rate = spine, local, rate
        self.rows, self.backward = rows, backward
        self.count = lax.axis_size("seq")
        if self.count == 4:
            self.near = swap(local, "seq", 1)

    def second(self):
        if self.count == 4:
            (self.near,) = self.spine.wait(self.near)
            here = View(lambda ref, i, s: ref)
            heads, dim = self.local.shape[:2]
            body = functools.partial(pair_states, heads=heads, dim=dim, rows=self.rows, backward=self.backward, count=4)

            def kernel(info, own, near, rate, out):
                body(info, own=own, near=near, rate=rate, out=out)

            ins = [(self.local, here), (self.near, here), (self.rate, SMEM)]
            outs = [(self.local.shape, bf16, here)]
            self.far = swap(self.spine.call(kernel, 1, ins, outs, name="pair_states")[0], "seq", 2)

    def all(self):
        if self.count == 4:
            (far,) = self.spine.wait(self.far)
            return self.near, far
        sign = -1 if self.backward else 1
        total = shift(self.local.astype(f32), "seq", sign)
        distance = 1
        while distance < self.count - 1:
            power = jnp.exp(-self.rate * self.rows * distance)[:, None, None]
            total = total + power * shift(total, "seq", sign * distance)
            distance *= 2
        return total, total


class Sum:
    last = None

    def __init__(self, spine, send, keep=None, there=None):
        self.spine, self.keep, self.cut = spine, keep, there is not None
        self.first = cross(send, 0)
        self.second_part = cross(there, 0) if self.cut else None
        self.shape = send.shape[0] if self.cut else send.shape[0] // 2, send.shape[1]
        self.four = lax.axis_size("seq") == 4

    def combine(self, body, *terms):
        rows = self.shape[0]

        def view(turn):
            if turn is None:
                return View(lambda ref, i, s: ref)
            return View(lambda ref, i, s: ref.at[span(1 - s[2] if turn else s[2], rows), :])

        ins = [(value, view(turn)) for value, turn in terms]
        outs = [(self.shape, bf16, view(None))]
        return self.spine.call(body, 1, ins, outs, name="combine")[0]

    def second(self):
        (self.first,) = self.spine.wait(self.first)
        turn = None if self.cut else True
        self.across = cross(self.combine(add_kernel, (self.keep, True), (self.first, turn)), 1)

    def last_second(self):
        self.last.second()

    def last_wait(self):
        (self.last.across,) = self.spine.wait(self.last.across)

    def line(self):
        if self.cut:
            across, first = self.spine.wait(self.across, self.second_part)
            first = first, None
        else:
            (across,) = self.spine.wait(self.across)
            first = self.first, False
        terms = [(self.keep, False), first, (across, None)]
        if self.last is None:
            self.value = self.combine(add_kernel, *terms)
        else:
            last = self.last
            terms += [(last.keep, False), (last.first, False), (last.across, None)]
            self.shape = self.shape[0], self.shape[1] + self.last.shape[1]
            self.value = self.combine(join_kernel, *terms)
        if self.four:
            self.inward = lax.ppermute(self.value, "seq", [(0, 1), (3, 2)])

    def line_across(self):
        if self.four:
            (inward,) = self.spine.wait(self.inward)
            self.value = self.combine(add_kernel, (self.value, None), (inward, None))
            self.middle = lax.ppermute(self.value, "seq", [(1, 2), (2, 1)])

    def line_back(self):
        if self.four:
            (middle,) = self.spine.wait(self.middle)
            self.value = self.combine(add_kernel, (self.value, None), (middle, None))
            self.outer = lax.ppermute(self.value, "seq", [(1, 0), (2, 3)])

    def spread(self):
        if self.four:
            (outer,) = self.spine.wait(self.outer)
            total = self.combine(choose_kernel, (self.value, None), (outer, None))
        else:
            total = lax.psum(self.value.astype(f32), "seq").astype(bf16)
            self.spine.after(total)
        self.value, self.second_half, self.own_first = total, cross(total, 1), cross(total, 0)

    def spread_on(self):
        (second,) = self.spine.wait(self.second_half)
        self.pieces = [self.value, second, self.own_first, cross(second, 0)]

    def arrive(self):
        self.pieces[2:] = self.spine.wait(*self.pieces[2:])
        return self.pieces


def shards(
    tokens,
    cotangent,
    qkvu_weight,
    out_weight,
    up_weight,
    gate_weight,
    down_weight,
    decay_rate,
    item_length,
    item_slot,
):
    core = lax.axis_index("heads")
    seq_place = lax.axis_index("seq")
    data_place = lax.axis_index("dp")
    block, width = tokens.shape[1:]
    heads = decay_rate.shape[0]
    half = qkvu_weight.shape[2]
    dim = half // heads
    ff = up_weight.shape[1] // 2
    rows = 2 * block
    tile = block // 2
    rate = (decay_rate, SMEM)

    own, own_cot = tokens[0], cotangent[0]
    other = swap(own, "heads", 1)
    other_cot = swap(own_cot, "heads", 1)
    other_out = swap(out_weight, "heads", 1)
    weights = jnp.transpose(qkvu_weight, (1, 0, 2))
    fine = 32
    lanes = jnp.arange(dim)
    frequency = 10000.0 ** (-(lanes % (dim // 2)).astype(f32) / (dim // 2))
    coarse_steps = seq_place * rows + fine * jnp.arange(rows // fine)
    steps = jnp.concatenate([coarse_steps, jnp.arange(fine)]).astype(f32)
    angles = steps[:, None] * frequency[None, :]
    cosine, sine = lax.optimization_barrier((jnp.cos(angles), jnp.sin(angles)))
    c_far, s_far = cosine[:-fine, None, :], sine[:-fine, None, :]
    c_near, s_near = cosine[None, -fine:, :], sine[None, -fine:, :]
    sign = jnp.where(lanes < dim // 2, -1.0, 1.0)
    cs = (c_far * c_near - s_far * s_near).reshape(rows, dim)
    sn = (sign * (s_far * c_near + c_far * s_near)).reshape(rows, dim)

    def weight(j):
        return weights, View(lambda ref, i, s: ref.at[pl.ds(j, 1)])

    def by(value, size):
        return value, View(lambda ref, i, s: ref.at[span(i, size), :])

    def all_of(value):
        return value, View(lambda ref, i, s: ref)

    def out(columns, kind, size):
        return (rows, columns), kind, View(lambda ref, i, s: ref.at[span(i, size), :])

    def fixed(shape, kind):
        return shape, kind, View(lambda ref, i, s: ref)

    def fn(body, *sizes):
        return functools.partial(body, *sizes)

    down_half = down_weight, View(lambda ref, i, s: ref.at[span(s[0], ff), :])
    columns = View(lambda ref, i, s: ref.at[:, span(s[0], ff)])
    up_half, gate_half = (up_weight, columns), (gate_weight, columns)
    spine = Spine()
    call = spine.call
    square = (heads, dim, dim)
    big, low = pltpu.VMEM((block, half), f32), pltpu.VMEM((block, half), bf16)

    def turned(columns):
        return (columns, rows), bf16, View(lambda ref, i, s: ref.at[:, span(i, block)])

    normed, k, v, pk, pv, contrib, local = call(
        fn(project_kv, block, heads, dim),
        2,
        [all_of(own), all_of(other), weight(1), weight(2), by(cs, block), by(sn, block)]
        + [rate],
        [out(width, bf16, block)]
        + [out(half, bf16, block)] * 4
        + [fixed((2,) + square, f32), fixed(square, bf16)],
        [big, big, low],
        name="project_kv",
    )
    line = States(spine, local, decay_rate, rows, False)
    g, g_t, grad_inner, valid = call(
        fn(begin_back, block),
        2,
        [all_of(own_cot), all_of(other_cot), down_half]
        + [(item_slot, SMEM), (item_length, SMEM)],
        [out(width, bf16, block), turned(width), out(ff, bf16, block), out(dim, f32, block)],
        name="begin_back",
    )
    line.second()
    q, pq, u_own, intra = call(
        fn(project_qu, block, heads, dim),
        2,
        [by(normed, block), weight(0), weight(3), by(cs, block), by(sn, block), rate]
        + [by(k, block), by(v, block)],
        [out(half, bf16, block)] * 3 + [out(half, f32, block)],
        [big],
        name="project_qu",
    )
    u_other = swap(u_own, "heads", 1)
    near, far = line.all()
    att_own, states = call(
        fn(attend, block, heads, dim, line.count),
        1,
        [all_of(q), all_of(intra), all_of(contrib), rate, all_of(near), all_of(far)],
        [fixed((rows, half), bf16), fixed((2,) + square, bf16)],
        name="attend",
    )
    att_other = swap(att_own, "heads", 1)
    att_u = [by(att_own, block), by(att_other, block), by(u_own, block), by(u_other, block)]
    out_both = [all_of(out_weight), all_of(other_out)]
    hidden, n2, mixed = call(
        fn(mix_out, block),
        2,
        att_u + out_both + [all_of(own), all_of(other)],
        [out(width, f32, block), out(width, bf16, block), out(half, bf16, block)],
        [pltpu.VMEM((block, width), bf16)],
        name="mix_out",
    )
    inner, grad_left, grad_right = call(
        fn(feed, block),
        2,
        [by(n2, block), up_half, gate_half, by(grad_inner, block)],
        [out(ff, bf16, block)] * 3,
        [pltpu.VMEM((block, ff), f32)] * 2,
        name="feed",
    )

    def halves(value):
        size = value.shape[0] // 2

        def at(ref, i, s):
            return ref.at[span(jnp.where(i == 0, 1 - s[1], s[1]), size), :]

        return value, View(at)

    def grad(name, lhs, rhs):
        shape = lhs.shape[0] // 2, rhs.shape[1]
        return call(
            weight_grad, 2, [halves(lhs), all_of(rhs)], [fixed(shape, bf16)] * 2, name=name
        )

    def sides(value):
        def at(ref, i, s):
            return ref.at[span(jnp.where(i == 0, 1 - s[0], s[0]), block), :]

        return value, View(at)

    two_sides = [fixed((block, width), bf16)] * 2

    def half_grad(name, lhs, rhs, send):
        size = lhs.shape[0] // 2

        def at(ref, i, s):
            return ref.at[span(1 - s[1] if send else s[1], size), :]

        shape = size, rhs.shape[1]
        ins = [(lhs, View(at)), all_of(rhs)]
        return call(weight_half, 1, ins, [fixed(shape, bf16)], name=name)[0]

    down = Sum(spine, half_grad("down_send", g_t, inner, True))
    *partial, n2_t = call(
        back_two,
        2,
        [by(grad_left, block), by(grad_right, block), up_half, gate_half]
        + [by(n2, block)],
        two_sides + [turned(width)],
        name="back_two",
    )
    partial_other = [swap(value, "heads", 1) for value in partial]
    up = Sum(spine, *grad("up_grad", n2_t, grad_left))
    gate = Sum(spine, *grad("gate_grad", n2_t, grad_right))
    down.keep = half_grad("down_keep", g_t, inner, False)
    mixed_t, normed_t = call(
        turn_kernel,
        2,
        [by(mixed, block), by(normed, block)],
        [turned(half), turned(width)],
        name="turn",
    )
    partial_other = spine.wait(*partial_other)
    down.second()
    dh, branch, dgates, datt, direct, local = call(
        fn(back_mix, block, block, heads, dim),
        2,
        [all_of(x) for x in (*partial, *partial_other)]
        + [sides(x) for x in (hidden, g, att_own, att_other, u_own, u_other)]
        + out_both
        + [sides(q), rate],
        [fixed((block, width), f32)]
        + [((rows, size), bf16, sides(None)[1]) for size in (width, half, half)]
        + [fixed((2,) + square, f32), fixed(square, bf16)],
        [pltpu.VMEM((block, half), f32)] * 2 + [pltpu.VMEM((block, half), bf16)],
        name="back_mix",
    )
    flat = pl.BlockSpec((width // 4, ff), lambda i: (i, 0))

    def place(body, pieces, shape, spec, name):
        return call(
            body, 4, [(p, whole(p)) for p in pieces], [(shape, f32, spec)], name=name
        )[0]
    line = States(spine, local, decay_rate, rows, True)
    out_u = call(
        out_u_grad,
        2,
        [halves(mixed_t), all_of(branch), halves(normed_t), all_of(dgates)],
        [fixed((block, width), bf16)] * 2,
        name="out_u_grad",
    )
    out_u = Sum(spine, *out_u)
    line.second()
    up.second()
    down.line()
    gq, dk, dv = call(
        fn(attend_back, block, heads, dim),
        2,
        [by(q, block), by(k, block), by(v, block), by(datt, block)]
        + [(states, View(lambda ref, i, s: ref.at[pl.ds(i, 1)])), by(pq, block)]
        + [by(cs, block), by(sn, block), rate],
        [out(half, bf16, block), out(half, f32, block), out(half, f32, block)],
        name="attend_back",
    )
    near, far = line.all()
    down.line_across()
    up.line()
    grads = call(
        fn(finish_back, block, heads, dim, line.count),
        2,
        [by(k, block), by(v, block), by(dk, block), by(dv, block), all_of(direct)]
        + [by(pk, block), by(pv, block), by(cs, block), by(sn, block), rate]
        + [by(gq, block), all_of(near), all_of(far)],
        [out(3 * half, bf16, block)],
        [pltpu.VMEM((dim, dim), bf16)],
        name="finish_back",
    )[0]
    flat = pl.BlockSpec((width // 4, ff), lambda i: (i, 0))

    def place(body, pieces, shape, spec, name):
        return call(
            body, 4, [(p, whole(p)) for p in pieces], [(shape, f32, spec)], name=name
        )[0]

    quarter = rows // 4
    on, there, keep, last_send, last_keep = call(
        weight_grad_cut,
        2,
        [halves(normed_t), all_of(grads)],
        [fixed((quarter, ff), bf16)] * 2
        + [fixed((block, ff), bf16)]
        + [fixed((block, 3 * half - ff), bf16)] * 2,
        name="qkv_grad",
    )
    qkv = Sum(spine, on, keep, there)
    out_u.last = Sum(spine, last_send, last_keep)
    gate.second()
    send_in, keep_in = call(
        back_in,
        2,
        [sides(dgates), sides(grads), all_of(weights)],
        two_sides,
        name="back_in",
    )
    out_u.second()
    down.line_back()
    up.line_across()
    sends, keep_out = call(
        split_product,
        2,
        [sides(inner), down_half, sides(hidden), all_of(send_in)],
        [fixed((2, block, width), bf16), fixed((block, width), f32)],
        name="split_product",
    )
    gate.line()
    qkv.second()
    down.spread()
    up.line_back()
    qkv.line()
    gate.line_across()
    out_u.last_second()
    down.spread_on()
    up.spread()
    qkv.line_across()
    gate.line_back()
    out_u.last_wait()
    out_u.line()
    down_grad = place(
        place_turned,
        down.arrive(),
        (ff, width),
        pl.BlockSpec((ff, width // 4), lambda i: (0, i)),
        "place_down",
    )
    (sends,) = spine.wait(sends)
    arrived_both = [swap(sends[n], "heads", 1) for n in range(2)]
    up.spread_on()
    qkv.line_back()
    gate.spread()
    out_u.line_across()
    up_grad = place(place_whole, up.arrive(), (width, ff), flat, "place_up")
    gate.spread_on()
    qkv.spread()
    out_u.line_back()
    qkv.spread_on()
    out_u.spread()
    gate_grad = place(place_whole, gate.arrive(), (width, ff), flat, "place_gate")
    out_u.spread_on()
    arrived_in, arrived_out = spine.wait(*arrived_both)
    def own_rows(value):
        return part(value, core, block)

    def add_wide(a, b):
        return a.astype(f32) + b.astype(f32)

    output = add_wide(keep_out, arrived_out)
    output = (output * own_rows(valid)[:, :1]).astype(bf16)
    x = own.astype(f32)
    scale = lax.rsqrt(jnp.mean(x * x, axis=-1, keepdims=True) + epsilon)
    dn = add_wide(keep_in, arrived_in)
    grad_inputs = (
        dh
        + scale * dn
        - x * (scale * scale * scale) * jnp.mean(x * dn, axis=-1, keepdims=True)
    )
    spine.after(output, grad_inputs)
    out_u_pieces = out_u.arrive()
    out_grad = place(
        place_rows,
        out_u_pieces,
        (half, width),
        pl.BlockSpec((half // 4, width), lambda i: (i, 0)),
        "place_out",
    )
    qkvu_grad = place(
        place_heads,
        qkv.arrive() + out_u_pieces,
        (width, 4, half),
        pl.BlockSpec((width // 4, 4, half), lambda i: (i, 0, 0)),
        "place_qkvu",
    )
    return output[None], grad_inputs[None], qkvu_grad, out_grad, up_grad, gate_grad, down_grad


def solution(mesh):
    placed = (
        P("dp", ("seq", "heads"), None),
        P("dp", ("seq", "heads"), None),
        P(None, None, "heads"),
        P("heads", None),
        P(),
        P(),
        P(),
        P("heads"),
        P(),
        P(),
    )
    return jax.shard_map(
        shards,
        mesh=mesh,
        in_specs=placed,
        out_specs=(
            P("dp", ("seq", "heads"), None),
            P("dp", ("seq", "heads"), None),
            P(None, None, "heads"),
            P("heads", None),
            P(None, "heads"),
            P(None, "heads"),
            P("heads", None),
        ),
        check_vma=False,
    )
```
